32 devices in a mesh: dp: 8 (over y, x, core), tensor: 4 (over z).
Axes of the slice: x: 2, y: 2, z: 4, core: 2. Of those that a mesh axis runs over, the one named last changes fastest.
Arguments:
- tokens: bfloat16 [8, 2048, 768], P('dp', 'tensor'), may hold values from -6 to 6
- segments: int32 [8, 2048], P('dp'), may hold values from 0 to 7, never falling along the last dimension, each value on 1 to 1024 neighbouring positions
- w_qkv: bfloat16 [768, 3, 768], P(None, None, 'tensor'), may hold values from -0.21875 to 0.21875
- w_out: bfloat16 [768, 768], P('tensor'), may hold values from -0.875 to 0.875
- w_gate_up: bfloat16 [768, 2, 3072], P(None, None, 'tensor'), may hold values from -0.21875 to 0.21875
- w_down: bfloat16 [3072, 768], P('tensor'), may hold values from -0.109375 to 0.109375
- norm_gain: float32 [2, 768], replicated, may hold values from 0.25 to 1.75
- norm_bias: float32 [2, 768], replicated, may hold values from -4 to 4
- cotangent: bfloat16 [8, 2048, 768], P('dp', 'tensor'), may hold values from -6 to 6
Outputs:
- output: bfloat16 [8, 2048, 768], P('dp', 'tensor')
- grad_tokens: float32 [8, 2048, 768], P('dp', 'tensor')
- grad_w_qkv: float32 [768, 3, 768], P(None, None, 'tensor')
- grad_w_out: float32 [768, 768], P('tensor')
- grad_w_gate_up: float32 [768, 2, 3072], P(None, None, 'tensor')
- grad_w_down: float32 [3072, 768], P('tensor')
- grad_norm_gain: float32 [2, 768], replicated
- grad_norm_bias: float32 [2, 768], replicated
The draws below stay inside these ranges and needn't reach their ends.
Inputs may be any that keep to these rules, and one draw needn't show every extreme that they name: `segments`: along each row of 2048 positions the segment numbers never fall.
All inputs are finite; a program needn't handle non-finite values.
Results may differ from the reference program's by a relative error of at most 0.017.
Values may be sent and summed in bfloat16 or wider, within the bound.
A program may use at most 128 MiB of HBM per device.

```python
import math
import jax
import jax.numpy as jnp
import numpy as np
from jax import lax

D = 768
HEADS = 12
HEAD_DIM = 64
FF = 3072
SEQ = 2048
QBLK = 512
SEGS = 8
MOST = 1024
ROWS = 8


def block_levels(rng, dims, pieces, smallest, high):
    factor_of = 1.0
    for dim, shards_of in pieces:
        draws = jax.random.uniform(jax.random.fold_in(jax.random.fold_in(rng, 6), dim), (shards_of,), jnp.float32, smallest / len(pieces), high / len(pieces))
        factor_of = factor_of * jnp.repeat(jnp.exp(draws), dims[dim] // shards_of).reshape((-1,) + (1,) * (len(dims) - 1 - dim))
    return factor_of


def split_up(amount, total, bound, skew):
    portions = [(1 << 20) // math.isqrt(rank ** skew) + 1 for rank in range(2, amount + 1)]
    rest, given = total - bound - (amount - 1), [1] * (amount - 1)
    while rest > 0:
        movable = [i for i in range(amount - 1) if given[i] < bound]
        pool, left = sum([portions[i] for i in movable]), rest
        for i in movable:
            addition = min(bound - given[i], max(1, left * portions[i] // pool), rest)
            given[i] = given[i] + addition
            rest = rest - addition
    return np.array([bound] + given)


def ragged_sizes(rng, count, total, bound, skew):
    if count == 2:
        one = jax.random.randint(rng, (), max(1, total - bound), min(bound, total - 1) + 1)
        return jnp.stack([one, total - one])
    lengths = jnp.asarray(split_up(count, total, bound, skew), jnp.int32)
    pairs = (count - 1) // 2
    giver, taker = lengths[1:1 + 2 * pairs:2], lengths[2:2 + 2 * pairs:2]
    margin = jnp.minimum(giver - 1, bound - taker)
    passed = jax.random.randint(jax.random.fold_in(rng, 1), (pairs,), 0, 1 << 20) % (margin + 1)
    lengths = lengths.at[1:1 + 2 * pairs:2].set(giver - passed).at[2:2 + 2 * pairs:2].set(taker + passed)
    return lengths[jax.random.permutation(jax.random.fold_in(rng, 2), count)]


def gaussian(key, shape, deviation, most, split=(), kind=jnp.bfloat16):
    drawn = jax.random.normal(key, shape, jnp.float32) * deviation
    if len(split) > 0:
        drawn = block_levels(key, shape, split, -0.22, 0.18) * drawn
    return jnp.clip(drawn, min=-most, max=most).astype(kind)


def setup_inputs(seed: int = 0) -> dict:
    key_of = jax.random.split(jax.random.key(seed), 10)
    tokens = gaussian(key_of[0], (ROWS, SEQ, D), 1.0, 6.0, ((0, 8), (1, 4)))
    segments = jax.vmap(lambda own: jnp.searchsorted(jnp.cumsum(ragged_sizes(own, SEGS, SEQ, MOST, 2)), jnp.arange(SEQ), side="right"))(jax.random.split(key_of[1], ROWS)).reshape((ROWS, SEQ)).astype(jnp.int32)
    w_qkv = gaussian(key_of[2], (D, 3, D), D ** -0.5, 0.21875, ((2, 4),))
    w_out = gaussian(key_of[3], (D, D), (D // 16) ** -0.5, 0.875, ((0, 4),))
    w_gate_up = gaussian(key_of[4], (D, 2, FF), D ** -0.5, 0.21875, ((2, 4),))
    w_down = gaussian(key_of[5], (FF, D), FF ** -0.5, 0.109375, ((0, 4),))
    norm_gain = jnp.clip(1.0 + 0.15 * jax.random.normal(key_of[6], (2, D), jnp.float32), 0.25, 1.75)
    norm_bias = gaussian(key_of[7], (2, D), 0.3, 4.0, (), jnp.float32)
    cotangent = gaussian(key_of[8], (ROWS, SEQ, D), 1.0, 6.0, ((0, 8), (1, 4)))
    return {"tokens": tokens, "segments": segments, "w_qkv": w_qkv, "w_out": w_out, "w_gate_up": w_gate_up, "w_down": w_down, "norm_gain": norm_gain, "norm_bias": norm_bias, "cotangent": cotangent}


precise = lax.Precision.HIGHEST
epsilon = 1e-05
far_below = -1e+30
log_base = math.log(1000.0)

@jax.custom_vjp
def low(v):
    return lax.optimization_barrier(v.astype(jnp.bfloat16)).astype(jnp.float32)

@jax.custom_vjp
def low_back(v):
    return v

def low_keep(v):
    return (low(v), None)

def low_pass(kept, grad):
    return (grad,)

def back_keep(v):
    return (v, None)

def back_low(kept, grad):
    return (low(grad),)
low.defvjp(low_keep, low_pass)
low_back.defvjp(back_keep, back_low)

def rotary_tables(segments_row):
    length = segments_row.shape[0]
    onehot = (segments_row[:, None] == jnp.arange(SEGS, dtype=jnp.int32)[None, :]).astype(jnp.int32)
    counts = lax.optimization_barrier(jnp.sum(onehot, axis=0)).astype(jnp.int32)
    starts = (jnp.cumsum(counts) - counts).astype(jnp.int32)
    first_place = lax.optimization_barrier(jnp.sum(onehot * starts[None, :], axis=1)).astype(jnp.int32)
    places = (jnp.arange(length, dtype=jnp.int32) - first_place).astype(jnp.float32)
    inverse = jnp.exp(-2.0 * jnp.arange(HEAD_DIM // 2, dtype=jnp.float32) / HEAD_DIM * log_base)
    angles = places[:, None] * inverse[None, :]
    return (jnp.cos(angles), jnp.sin(angles))

def rotate(values, cosine_table, sine_table):
    half_width = values.shape[-1] // 2
    first_half = values[..., :half_width]
    second_half = values[..., half_width:]
    cosine_wide = cosine_table[:, None, :]
    sine_wide = sine_table[:, None, :]
    return jnp.concatenate([first_half * cosine_wide - second_half * sine_wide, second_half * cosine_wide + first_half * sine_wide], axis=-1)

def layer_norm(summed, gain_row, bias_row):
    centred = summed - lax.optimization_barrier(jnp.mean(summed, axis=-1, keepdims=True))
    variance = lax.optimization_barrier(jnp.mean(centred * centred, axis=-1, keepdims=True))
    return centred * lax.rsqrt(variance + epsilon) * gain_row + bias_row

def row_forward(tokens_row, segments_row, qkv_weight, out_weight, gate_up_weight, down_weight, gains, biases):
    length = tokens_row.shape[0]
    cosine_table, sine_table = rotary_tables(segments_row)
    projected = low_back(jnp.einsum('sd,dcf->scf', tokens_row, qkv_weight, precision=precise))
    queries = low(rotate(projected[:, 0].reshape(length, HEADS, HEAD_DIM), cosine_table, sine_table))
    keys_all = low(rotate(projected[:, 1].reshape(length, HEADS, HEAD_DIM), cosine_table, sine_table))
    values_all = low(projected[:, 2].reshape(length, HEADS, HEAD_DIM))
    score_scale = 1.0 / math.sqrt(HEAD_DIM)
    blocks = length // QBLK

    def attend(inputs):
        query_block, segment_block = inputs
        scores = low_back(jnp.einsum('qhe,khe->hqk', query_block, keys_all, precision=precise) * score_scale)
        allowed = segment_block[:, None] == segments_row[None, :]
        scores = jnp.where(allowed[None], scores, far_below)
        largest = lax.optimization_barrier(jnp.max(scores, axis=-1, keepdims=True))
        weights = jnp.exp(scores - largest)
        probability = weights / lax.optimization_barrier(jnp.sum(weights, axis=-1, keepdims=True))
        mixed_heads = jnp.einsum('hqk,khe->qhe', low(probability), values_all, precision=precise)
        return low_back(low(mixed_heads))
    heads_out = lax.map(jax.checkpoint(attend), (queries.reshape(blocks, QBLK, HEADS, HEAD_DIM), segments_row.reshape(blocks, QBLK)))
    heads_out = heads_out.reshape(length, D)
    branch = low_back(jnp.dot(heads_out, out_weight, precision=precise))
    normed = layer_norm(tokens_row + branch, gains[0], biases[0])
    gate_up = low_back(jnp.einsum('sd,dcf->scf', low(normed), gate_up_weight, precision=precise))
    gate_value = gate_up[:, 0]
    hidden = low(gate_value * jax.nn.sigmoid(gate_value) * gate_up[:, 1])
    mlp_out = low_back(jnp.dot(hidden, down_weight, precision=precise))
    return layer_norm(normed + mlp_out, gains[1], biases[1])

def reference(tokens, segments, w_qkv, w_out, w_gate_up, w_down, norm_gain, norm_bias, cotangent):

    def forward(tokens_all, qkv_weight, out_weight, gate_up_weight, down_weight, gains, biases):

        def one_row(inputs):
            return row_forward(inputs[0], inputs[1], qkv_weight, out_weight, gate_up_weight, down_weight, gains, biases)
        return lax.map(jax.checkpoint(one_row), (tokens_all, segments))
    result, pullback = jax.vjp(forward, tokens.astype(jnp.float32), w_qkv.astype(jnp.float32), w_out.astype(jnp.float32), w_gate_up.astype(jnp.float32), w_down.astype(jnp.float32), norm_gain.astype(jnp.float32), norm_bias.astype(jnp.float32))
    gradients = pullback(cotangent.astype(jnp.float32))
    return (result.astype(jnp.bfloat16), gradients[0], gradients[1], gradients[2], gradients[3], gradients[4], gradients[5], gradients[6])
```

```python
import math

import jax
import jax.numpy as jnp
from jax import lax
from jax.sharding import PartitionSpec as P

HEAD_DIM = 64
QBLK = 512
SEGS = 8


epsilon = 1e-05
far_below = -1e30
log_base = math.log(1000.0)


def rotary_tables(segments_row):
    length = segments_row.shape[0]
    onehot = (segments_row[:, None] == jnp.arange(SEGS, dtype=jnp.int32)[None, :]).astype(jnp.int32)
    counts = jnp.sum(onehot, axis=0)
    order = jnp.arange(SEGS, dtype=jnp.int32)
    starts = jnp.sum(jnp.where(order[None, :] < order[:, None], counts[None, :], 0), axis=1)
    first_place = jnp.sum(onehot * starts[None, :], axis=1)
    places = (jnp.arange(length, dtype=jnp.int32) - first_place).astype(jnp.float32)
    inverse = jnp.exp(-2.0 * jnp.arange(HEAD_DIM // 2, dtype=jnp.float32) / HEAD_DIM * log_base)
    angles = places[:, None] * inverse[None, :]
    return (jnp.cos(angles), jnp.sin(angles))


def rotate(values, cosine_table, sine_table):
    half_width = values.shape[-1] // 2
    first_half = values[..., :half_width]
    second_half = values[..., half_width:]
    cosine_wide = cosine_table[:, None, :]
    sine_wide = sine_table[:, None, :]
    return jnp.concatenate(
        [
            first_half * cosine_wide - second_half * sine_wide,
            second_half * cosine_wide + first_half * sine_wide,
        ],
        axis=-1,
    )


def rotate_back(grads, cosine_table, sine_table):
    half_width = grads.shape[-1] // 2
    first_half = grads[..., :half_width]
    second_half = grads[..., half_width:]
    cosine_wide = cosine_table[:, None, :]
    sine_wide = sine_table[:, None, :]
    return jnp.concatenate(
        [
            first_half * cosine_wide + second_half * sine_wide,
            second_half * cosine_wide - first_half * sine_wide,
        ],
        axis=-1,
    )


def norm_forward(summed, gain_row, bias_row):
    centred = summed - jnp.mean(summed, axis=-1, keepdims=True)
    variance = jnp.mean(centred * centred, axis=-1, keepdims=True)
    inverse = lax.rsqrt(variance + epsilon)
    normalized = centred * inverse
    return (normalized * gain_row + bias_row, normalized, inverse)


def norm_backward(grad_out, normalized, inverse, gain_row):
    grad_gain = jnp.sum(grad_out * normalized, axis=0)
    grad_bias = jnp.sum(grad_out, axis=0)
    scaled_grad = grad_out * gain_row
    grad_in = inverse * (
        scaled_grad
        - jnp.mean(scaled_grad, axis=-1, keepdims=True)
        - normalized * jnp.mean(scaled_grad * normalized, axis=-1, keepdims=True)
    )
    return (grad_in, grad_gain, grad_bias)


def block_scores(query_block, segment_block, keys_all, segments_row):
    score_scale = 1.0 / math.sqrt(HEAD_DIM)
    scores = (
        jnp.einsum("qhe,khe->hqk", query_block, keys_all, preferred_element_type=jnp.float32)
        * score_scale
    )
    allowed = segment_block[:, None] == segments_row[None, :]
    return jnp.where(allowed[None], scores, far_below)


def attend_forward(queries, keys_all, values_all, segments_row):
    length, heads_here, _ = queries.shape
    blocks = length // QBLK

    def one_block(inputs):
        query_block, segment_block = inputs
        scores = block_scores(query_block, segment_block, keys_all, segments_row)
        largest = jnp.max(scores, axis=-1, keepdims=True)
        weights = jnp.exp(scores - largest)
        row_total = jnp.sum(weights, axis=-1, keepdims=True)
        mixed_heads = jnp.einsum(
            "hqk,khe->qhe",
            (weights / row_total).astype(jnp.bfloat16),
            values_all,
            preferred_element_type=jnp.float32,
        )
        return (mixed_heads.astype(jnp.bfloat16), largest[..., 0] + jnp.log(row_total[..., 0]))

    mixed_heads, logsum = lax.map(
        one_block,
        (queries.reshape(blocks, QBLK, heads_here, HEAD_DIM), segments_row.reshape(blocks, QBLK)),
    )
    return (mixed_heads.reshape(length, heads_here * HEAD_DIM), logsum)


def attend_backward(queries, keys_all, values_all, segments_row, grad_heads, logsum):
    length, heads_here, _ = queries.shape
    blocks = length // QBLK
    score_scale = 1.0 / math.sqrt(HEAD_DIM)

    def one_block(carried, inputs):
        grad_keys, grad_values = carried
        query_block, segment_block, grad_block, logsum_block = inputs
        scores = block_scores(query_block, segment_block, keys_all, segments_row)
        probability = jnp.exp(scores - logsum_block[..., None])
        grad_probability = jnp.einsum(
            "qhe,khe->hqk", grad_block, values_all, preferred_element_type=jnp.float32
        )
        inner_sum = jnp.sum(probability * grad_probability, axis=-1, keepdims=True)
        grad_scores = (probability * (grad_probability - inner_sum)).astype(jnp.bfloat16)
        grad_query = (
            jnp.einsum("hqk,khe->qhe", grad_scores, keys_all, preferred_element_type=jnp.float32)
            * score_scale
        )
        grad_keys = (
            grad_keys
            + jnp.einsum(
                "hqk,qhe->khe", grad_scores, query_block, preferred_element_type=jnp.float32
            )
            * score_scale
        )
        grad_values = grad_values + jnp.einsum(
            "hqk,qhe->khe",
            probability.astype(jnp.bfloat16),
            grad_block,
            preferred_element_type=jnp.float32,
        )
        return ((grad_keys, grad_values), grad_query)

    zeros_block = jnp.zeros((length, heads_here, HEAD_DIM), jnp.float32)
    (grad_keys, grad_values), grad_queries = lax.scan(
        one_block,
        (zeros_block, zeros_block),
        (
            queries.reshape(blocks, QBLK, heads_here, HEAD_DIM),
            segments_row.reshape(blocks, QBLK),
            grad_heads.reshape(blocks, QBLK, heads_here, HEAD_DIM),
            logsum,
        ),
    )
    return (grad_queries.reshape(length, heads_here, HEAD_DIM), grad_keys, grad_values)


def on_device(tokens, segments, w_qkv, w_out, w_gate_up, w_down, norm_gain, norm_bias, cotangent):
    local_tokens = tokens[0]
    segments_row = segments[0]
    width_here = w_qkv.shape[2]
    heads_here = width_here // HEAD_DIM
    cosine_table, sine_table = rotary_tables(segments_row)
    gathered = lax.all_gather(local_tokens, "tensor", axis=0, tiled=True)
    length = gathered.shape[0]
    projected = jnp.einsum("sd,dcf->scf", gathered, w_qkv, preferred_element_type=jnp.float32)
    queries = rotate(
        projected[:, 0].reshape(length, heads_here, HEAD_DIM), cosine_table, sine_table
    ).astype(jnp.bfloat16)
    keys_all = rotate(
        projected[:, 1].reshape(length, heads_here, HEAD_DIM), cosine_table, sine_table
    ).astype(jnp.bfloat16)
    values_all = projected[:, 2].reshape(length, heads_here, HEAD_DIM).astype(jnp.bfloat16)
    heads_out, logsum = attend_forward(queries, keys_all, values_all, segments_row)
    branch = lax.psum_scatter(
        jnp.dot(heads_out, w_out, preferred_element_type=jnp.float32),
        "tensor",
        scatter_dimension=0,
        tiled=True,
    )
    normed, normal_one, inverse_one = norm_forward(
        local_tokens.astype(jnp.float32) + branch, norm_gain[0], norm_bias[0]
    )
    normed_low = normed.astype(jnp.bfloat16)
    normed_all = lax.all_gather(normed_low, "tensor", axis=0, tiled=True)
    gate_up = jnp.einsum("sd,dcf->scf", normed_all, w_gate_up, preferred_element_type=jnp.float32)
    gate_value = gate_up[:, 0]
    up_value = gate_up[:, 1]
    sigmoid_gate = jax.nn.sigmoid(gate_value)
    active = gate_value * sigmoid_gate
    hidden = (active * up_value).astype(jnp.bfloat16)
    mlp_out = lax.psum_scatter(
        jnp.dot(hidden, w_down, preferred_element_type=jnp.float32),
        "tensor",
        scatter_dimension=0,
        tiled=True,
    )
    result, normal_two, inverse_two = norm_forward(normed + mlp_out, norm_gain[1], norm_bias[1])
    output = result.astype(jnp.bfloat16)[None]
    grad_z2, gain_two, bias_two = norm_backward(
        cotangent[0].astype(jnp.float32), normal_two, inverse_two, norm_gain[1]
    )
    grad_mlp_all = lax.all_gather(grad_z2.astype(jnp.bfloat16), "tensor", axis=0, tiled=True)
    grad_hidden = jnp.einsum("sd,fd->sf", grad_mlp_all, w_down, preferred_element_type=jnp.float32)
    grad_w_down = jnp.einsum("sf,sd->fd", hidden, grad_mlp_all, preferred_element_type=jnp.float32)
    grad_gate = grad_hidden * up_value * sigmoid_gate * (1.0 + gate_value * (1.0 - sigmoid_gate))
    grad_up = grad_hidden * active
    grad_gate_up = jnp.stack([grad_gate, grad_up], axis=1).astype(jnp.bfloat16)
    normed_used = lax.all_gather(normed_low, "tensor", axis=0, tiled=True)
    grad_w_gate_up = jnp.einsum(
        "sd,scf->dcf", normed_used, grad_gate_up, preferred_element_type=jnp.float32
    )
    normed_part = jnp.einsum(
        "scf,dcf->sd", grad_gate_up, w_gate_up, preferred_element_type=jnp.float32
    )
    grad_normed = grad_z2 + lax.psum_scatter(normed_part, "tensor", scatter_dimension=0, tiled=True)
    grad_z1, gain_one, bias_one = norm_backward(grad_normed, normal_one, inverse_one, norm_gain[0])
    grad_branch_all = lax.all_gather(grad_z1.astype(jnp.bfloat16), "tensor", axis=0, tiled=True)
    grad_heads = jnp.einsum(
        "sd,fd->sf", grad_branch_all, w_out, preferred_element_type=jnp.float32
    ).astype(jnp.bfloat16)
    grad_w_out = jnp.einsum(
        "sf,sd->fd", heads_out, grad_branch_all, preferred_element_type=jnp.float32
    )
    grad_queries, grad_keys, grad_values = attend_backward(
        queries, keys_all, values_all, segments_row, grad_heads, logsum
    )
    grad_projected = jnp.stack(
        [
            rotate_back(grad_queries, cosine_table, sine_table).reshape(length, width_here),
            rotate_back(grad_keys, cosine_table, sine_table).reshape(length, width_here),
            grad_values.reshape(length, width_here),
        ],
        axis=1,
    ).astype(jnp.bfloat16)
    tokens_used = lax.all_gather(local_tokens, "tensor", axis=0, tiled=True)
    grad_w_qkv = jnp.einsum(
        "sd,scf->dcf", tokens_used, grad_projected, preferred_element_type=jnp.float32
    )
    input_part = jnp.einsum(
        "scf,dcf->sd", grad_projected, w_qkv, preferred_element_type=jnp.float32
    )
    grad_tokens = grad_z1 + lax.psum_scatter(
        input_part.astype(jnp.bfloat16), "tensor", scatter_dimension=0, tiled=True
    ).astype(jnp.float32)
    gains_part = jnp.stack([gain_one, gain_two], axis=0)
    biases_part = jnp.stack([bias_one, bias_two], axis=0)
    gains_sum, biases_sum = lax.psum((gains_part, biases_part), "tensor")
    grad_w_qkv, grad_w_out, grad_w_gate_up, grad_w_down, gains_sum, biases_sum = lax.psum(
        (grad_w_qkv, grad_w_out, grad_w_gate_up, grad_w_down, gains_sum, biases_sum), "dp"
    )
    return (
        output,
        grad_tokens[None],
        grad_w_qkv,
        grad_w_out,
        grad_w_gate_up,
        grad_w_down,
        gains_sum,
        biases_sum,
    )


def solution(mesh):
    placed = (
        P("dp", "tensor", None),
        P("dp", None),
        P(None, None, "tensor"),
        P("tensor", None),
        P(None, None, "tensor"),
        P("tensor", None),
        P(),
        P(),
        P("dp", "tensor", None),
    )
    return jax.shard_map(
        on_device,
        mesh=mesh,
        in_specs=placed,
        out_specs=(
            P("dp", "tensor", None),
            P("dp", "tensor", None),
            P(None, None, "tensor"),
            P("tensor", None),
            P(None, None, "tensor"),
            P("tensor", None),
            P(),
            P(),
        ),
        check_vma=False,
    )
```

```python
import math

import jax
import jax.numpy as jnp
from jax import lax
from jax.experimental import pallas as pl
from jax.experimental.pallas import tpu as pltpu
from jax.sharding import PartitionSpec as P

HEAD_DIM = 64
SEGS = 8
BLK = 256
F32 = jnp.float32
BF16 = jnp.bfloat16

epsilon = 1e-05
far_below = -1e30
log_base = math.log(1000.0)


def nn(a, b):
    return lax.dot_general(a, b, (((1,), (0,)), ((), ())), preferred_element_type=F32)


def nt(a, b):
    return lax.dot_general(a, b, (((1,), (1,)), ((), ())), preferred_element_type=F32)


def tn(a, b):
    return lax.dot_general(a, b, (((0,), (0,)), ((), ())), preferred_element_type=F32)


def owner_bits(core, h, k):
    low, high = k & 1, k >> 1
    return (core | (low << 1) | (high << 2)) if h == 0 else (core | (high << 1) | (low << 2))


def attend_forward_kernel(
    sc, tok, cos, sin, seg, own, half, other, w, qa, ka, kt, vn, ot, logsum, keep, send, va, mx, acc, sem
):
    heads = 3
    width = heads * HEAD_DIM
    cross = sc[0]
    place = sc[1]

    @pl.when(sc[2] == 0)
    def _():
        copy = pltpu.make_async_copy(own, w, sem.at[0])
        copy.start()
        copy.wait()

    @pl.when(sc[2] == 1)
    def _():
        copies = []
        for core, source in enumerate((half, other)):
            for h in range(2):
                for k in range(4):
                    row = pl.multiple_of((place ^ owner_bits(core, h, k)) * 96 + h * 48, 16)
                    copies.append(
                        pltpu.make_async_copy(
                            source.at[h * 4 + k], w.at[pl.ds(row, 48)], sem.at[len(copies)]
                        )
                    )
                    copies[-1].start()
        for copy in copies:
            copy.wait()

    def project(e, _):
        at = pl.ds(pl.multiple_of(e * 512, 512), 512)
        made = nt(w[: 3 * width], tok[e])
        c, s = cos[:, at], sin[:, at]
        hot = (seg[:, at] == lax.broadcasted_iota(jnp.int32, (SEGS, 512), 0)).astype(F32)
        rest = jnp.zeros((64 - SEGS, 512), F32)
        one_row = (lax.broadcasted_iota(jnp.int32, (16, 512), 0) == 0).astype(F32)
        for h in range(heads):
            r = h * HEAD_DIM
            a1, a2 = made[r : r + 32], made[r + 32 : r + 64]
            q = jnp.concatenate([a1 * c - a2 * s, a2 * c + a1 * s], axis=0).astype(BF16).astype(F32)
            qa[h, :, at] = jnp.concatenate([q * 0.125, hot, rest], axis=0).astype(BF16)
            r += width
            a1, a2 = made[r : r + 32], made[r + 32 : r + 64]
            k = jnp.concatenate([a1 * c - a2 * s, a2 * c + a1 * s], axis=0)
            kt[h * HEAD_DIM : (h + 1) * HEAD_DIM, at] = k.astype(BF16)
            ka[h, at, :] = jnp.concatenate([k, (1.0 - hot) * far_below, rest], axis=0).T.astype(BF16)
            r += width
            v = made[r : r + 64]
            va[h, :, at] = jnp.concatenate([v, one_row], axis=0).astype(BF16)
            vn[h, at, :] = jnp.concatenate([v, jnp.zeros_like(v)], axis=0).T[:, :HEAD_DIM].astype(BF16)
        return 0

    lax.fori_loop(0, 4, project, 0)

    def query_block(i, _):
        at = pl.ds(pl.multiple_of(i * BLK, BLK), BLK)
        for h in range(heads):
            mx[h] = jnp.full((1, BLK), -3e38, F32)
            acc[h] = jnp.zeros((80, BLK), F32)

        def key_block(j, _):
            here = pl.ds(pl.multiple_of((j ^ cross) * BLK, BLK), BLK)
            for h in range(heads):
                scores = nn(ka[h, here, :], qa[h, :, at])
                before = mx[h]
                largest = jnp.maximum(before, jnp.max(scores, axis=0, keepdims=True))
                weights = jnp.exp(scores - largest).astype(BF16)
                acc[h] = acc[h] * jnp.exp(before - largest) + nn(va[h, :, here], weights)
                mx[h] = largest
            return 0

        lax.fori_loop(sc[8 + (i ^ cross)], sc[16 + (i ^ cross)], key_block, 0)
        for h in range(heads):
            total = acc[h, 64:65, :]
            ot[h * HEAD_DIM : (h + 1) * HEAD_DIM, at] = (acc[h, :64, :] / total).astype(BF16)
            logsum[pl.ds(h, 1), at] = mx[h] + jnp.log(total)
        return 0

    lax.fori_loop(0, 2048 // BLK, query_block, 0)
    for e in range(4):
        part = tn(ot[:, e * 512 : (e + 1) * 512], w[3 * width :])
        if e < 2:
            keep[e] = part
        else:
            send[e - 2] = part.astype(BF16)


def attend_backward_kernel(
    sc, gb, tok, w, qa, ka, kt, vn, ot, logsum, cos, sin, grads, keep, send, dot_, inner, dq, dk, dv, gp
):
    heads = 3
    width = heads * HEAD_DIM
    cross = sc[0]
    quarter = sc[3]

    def begin(e, _):
        at = pl.ds(pl.multiple_of(e * 512, 512), 512)
        made = nt(w[3 * width :], gb[e]).astype(BF16)
        dot_[:, at] = made
        product = made.astype(F32) * ot[:, at].astype(F32)
        for h in range(heads):
            inner[pl.ds(h, 1), at] = jnp.sum(product[h * HEAD_DIM : (h + 1) * HEAD_DIM], axis=0, keepdims=True)
        return 0

    lax.fori_loop(0, 4, begin, 0)
    dq[...] = jnp.zeros_like(dq)

    def key_block(j, _):
        here = pl.ds(pl.multiple_of(j * BLK, BLK), BLK)
        for h in range(heads):
            dk[h] = jnp.zeros((HEAD_DIM, BLK), F32)
            dv[h] = jnp.zeros((HEAD_DIM, BLK), F32)

        def query_block(i, _):
            at = pl.ds(pl.multiple_of((i ^ cross) * BLK, BLK), BLK)
            for h in range(heads):
                rows = slice(h * HEAD_DIM, (h + 1) * HEAD_DIM)
                scores = nn(ka[h, here, :], qa[h, :, at])
                probability = jnp.exp(scores - logsum[pl.ds(h, 1), at])
                rise = nn(vn[h, here, :], dot_[rows, at])
                slope = (probability * (rise - inner[pl.ds(h, 1), at])).astype(BF16)
                dv[h] += nt(dot_[rows, at], probability.astype(BF16))
                dk[h] += nt(qa[h, :HEAD_DIM, at], slope)
                dq[rows, at] += nn(kt[rows, here], slope)
            return 0

        lax.fori_loop(sc[8 + (j ^ cross)], sc[16 + (j ^ cross)], query_block, 0)
        c, s = cos[:, here], sin[:, here]
        for h in range(heads):
            d1, d2 = dk[h, :32, :], dk[h, 32:, :]
            r = width + h * HEAD_DIM
            gp[r : r + 64, here] = jnp.concatenate([d1 * c + d2 * s, d2 * c - d1 * s], axis=0).astype(BF16)
            r += width
            gp[r : r + 64, here] = dv[h].astype(BF16)
        return 0

    lax.fori_loop(0, 2048 // BLK, key_block, 0)

    def turn(e, _):
        at = pl.ds(pl.multiple_of(e * 512, 512), 512)
        c, s = cos[:, at] * 0.125, sin[:, at] * 0.125
        for h in range(heads):
            r = h * HEAD_DIM
            d1, d2 = dq[r : r + 32, at], dq[r + 32 : r + 64, at]
            gp[r : r + 64, at] = jnp.concatenate([d1 * c + d2 * s, d2 * c - d1 * s], axis=0).astype(BF16)
        return 0

    lax.fori_loop(0, 4, turn, 0)
    for e in range(4):
        part = tn(gp[:, e * 512 : (e + 1) * 512], w[: 3 * width])
        if e < 2:
            keep[e] = part
        else:
            send[e - 2] = part.astype(BF16)
    for block in range(4):
        if block < 3:
            rows = slice(block * width, (block + 1) * width)
            made = sum(nn(gp[rows, e * 512 : (e + 1) * 512], tok[e]) for e in range(4))
        else:
            made = sum(nn(ot[:, e * 512 : (e + 1) * 512], gb[e]) for e in range(4))
        away = block ^ quarter
        grads[0, away] = made[:96].astype(BF16)
        grads[1, ((away & 1) << 1) | (away >> 1)] = made[96:].astype(BF16)


def row_mean(v):
    return jnp.mean(v, axis=-1, keepdims=True)


def norm_forward(summed):
    centred = summed - row_mean(summed)
    inverse = lax.rsqrt(row_mean(centred * centred) + epsilon)
    return centred * inverse, inverse


def norm_backward(scaled, normalized, inverse):
    return inverse * (scaled - row_mean(scaled) - normalized * row_mean(scaled * normalized))


def feed_forward_kernel(sc, x, b_own, b_far, cot, gain, bias, *refs):
    pieces = refs[:8]
    out, gz1, gz1_low, sums, keep_hi, send_hi, keep_lo, send_lo = refs[8:16]
    w, slope_g, slope_u, hid, nb, nbt, gm, gmt, total, norm1, inv1, dw, in_sem, out_sem = refs[16:]
    place = sc[1]

    def loads(ez):
        copies = []
        for core in range(2):
            for h in range(2):
                for k in range(4):
                    row = pl.multiple_of((place ^ owner_bits(core, h, k)) * 96 + h * 48, 16)
                    copies.append(
                        pltpu.make_async_copy(
                            pieces[ez * 2 + core].at[h * 4 + k],
                            w.at[ez, :, pl.ds(row, 48), :],
                            in_sem.at[ez, len(copies)],
                        )
                    )
        return copies

    for ez in range(4):
        for copy in loads(ez):
            copy.start()

    n1, i1 = norm_forward(x[...].astype(F32) + (b_own[...] + b_far[...].astype(F32)))
    norm1[...] = n1
    inv1[...] = jnp.broadcast_to(i1, inv1.shape)
    low = (n1 * gain[0:1, :] + bias[0:1, :]).astype(BF16)
    nb[...] = low
    nbt[...] = low.astype(F32).T.astype(BF16)
    total[...] = n1 * gain[0:1, :] + bias[0:1, :]
    for ez in range(4):
        for copy in loads(ez):
            copy.wait()

    def forward(ez, _):
        gate = nn(nb[...], w[ez, 0])
        up = nn(nb[...], w[ez, 1])
        sig = 1.0 / (1.0 + jnp.exp(-gate))
        active = gate * sig
        low = (active * up).astype(BF16)
        hid[ez] = low
        slope_u[ez] = active
        slope_g[ez] = up * sig * (1.0 + gate * (1.0 - sig))
        total[...] += nn(low, w[ez, 2])
        return 0

    lax.fori_loop(0, 4, forward, 0)
    n2, i2 = norm_forward(total[...])
    out[...] = (n2 * gain[1:2, :] + bias[1:2, :]).astype(BF16)
    g = cot[...].astype(F32)
    sums[1:2, :] = jnp.sum(g * n2, axis=0, keepdims=True)
    sums[3:4, :] = jnp.sum(g, axis=0, keepdims=True)
    gz2 = norm_backward(g * gain[1:2, :], n2, i2)
    total[...] = gz2
    gm[...] = gz2.astype(BF16)
    gmt[...] = gz2.T.astype(BF16)

    def stores(keep, send, i):
        copies = []
        for core, target in enumerate((keep, send)):
            for h in range(2):
                for k in range(4):
                    row = pl.multiple_of((place ^ owner_bits(core, h, k)) * 96 + h * 48, 16)
                    copies.append(
                        pltpu.make_async_copy(
                            dw.at[i, :, pl.ds(row, 48), :],
                            target.at[i, h * 4 + k],
                            out_sem.at[i, len(copies)],
                        )
                    )
        return copies

    groups = ((2, keep_hi, send_hi), (0, keep_lo, send_lo))
    for number, (first, keep, send) in enumerate(groups):

        def backward(i, _, first=first, keep=keep, send=send, number=number):
            ez = first + i
            if number:
                for copy in stores(*groups[0][1:], i):
                    copy.wait()
            grad_hidden = nt(gm[...], w[ez, 2])
            dw[i, 2] = nn(gmt[...], hid[ez]).astype(BF16)
            gate = (grad_hidden * slope_g[ez]).astype(BF16)
            dw[i, 0] = nn(nbt[...], gate).astype(BF16)
            up = (grad_hidden * slope_u[ez]).astype(BF16)
            dw[i, 1] = nn(nbt[...], up).astype(BF16)
            total[...] += nt(gate, w[ez, 0]) + nt(up, w[ez, 1])
            for copy in stores(keep, send, i):
                copy.start()
            return 0

        lax.fori_loop(0, 2, backward, 0)

    g = total[...]
    sums[0:1, :] = jnp.sum(g * norm1[...], axis=0, keepdims=True)
    sums[2:3, :] = jnp.sum(g, axis=0, keepdims=True)
    sums[4:8, :] = jnp.zeros((4, 768), F32)
    made = norm_backward(g * gain[0:1, :], norm1[...], inv1[:, 0:1])
    gz1[...] = made
    gz1_low[...] = made.astype(BF16)
    for i in range(2):
        for copy in stores(*groups[1][1:], i):
            copy.wait()


def solution(mesh):
    dp, tensor = mesh.shape["dp"], mesh.shape["tensor"]
    assert tensor == 4 and dp >= 8 and dp & (dp - 1) == 0
    extra = [1 << b for b in range(3, dp.bit_length() - 1)]
    both = ("dp", "tensor")

    def cell(i, k):
        return i * tensor + k

    def over(x, bit):
        return lax.ppermute(x, "dp", [(i, i ^ bit) for i in range(dp)])

    def along(x, bit):
        return lax.ppermute(x, "tensor", [(i, i ^ bit) for i in range(tensor)])

    away = [(i, k) for i in range(dp) for k in range(tensor) if (i & 1) != (k >> 1)]

    def trade(x):
        return lax.ppermute(x, both, [(cell(i, k), cell(i ^ 1, k ^ 2)) for i, k in away])

    def core(x):
        return over(x, 1)

    def across(x):
        return over(x, 2)

    def down(x):
        return over(x, 4)

    def plane_gather(a, b):
        a2 = jnp.stack([a, across(a)])
        b2 = jnp.stack([b, down(b)])
        half = jnp.concatenate([a2, down(a2), b2, across(b2)])
        return half, core(half)

    def on_device(tokens, segments, w_qkv, w_out, w_gate_up, w_down, norm_gain, norm_bias, cotangent):
        p, z = lax.axis_index("dp"), lax.axis_index("tensor")
        rho = z >> 1
        swapped = (p & 1) != rho
        slot = jnp.where(swapped, z ^ 2, z)
        place = p & 7

        x = tokens[0]
        traded = trade(jnp.stack([x, cotangent[0]]))
        x = jnp.where(swapped, traded[0], x)
        cot = jnp.where(swapped, traded[1], cotangent[0])
        pair = jnp.stack([x, along(x, 1)])
        tok = jnp.concatenate([pair, core(pair)])

        own = jnp.concatenate([w_qkv.transpose(1, 2, 0).reshape(576, 768), w_out])
        block = along(lax.dynamic_slice(own, (place * 96, 0), (96, 768)), 2)
        far_half, far_other = plane_gather(block[:48], block[48:])

        rows = lax.dynamic_slice(w_gate_up, (place * 96, 0, 0), (96, 2, 768))
        block = jnp.stack(
            [rows[:, 0], rows[:, 1], lax.dynamic_slice(w_down, (place * 96, 0), (96, 768))]
        ).reshape(3, 2, 48, 768)
        blocks = [block, along(block, 1)]
        blocks += [along(blocks[0], 2), along(blocks[1], 2)]
        pieces = []
        for b in blocks:
            pieces += plane_gather(b[:, 0], b[:, 1])

        row = jnp.where(swapped, core(segments), segments)[0]
        length = row.shape[0]
        onehot = (row[None, :] == jnp.arange(SEGS, dtype=jnp.int32)[:, None]).astype(jnp.int32)
        counts = jnp.sum(onehot, axis=1)
        order = jnp.arange(SEGS, dtype=jnp.int32)
        starts = jnp.sum(jnp.where(order[None, :] < order[:, None], counts[None, :], 0), axis=1)
        first_place = jnp.sum(onehot * starts[:, None], axis=0)
        end_place = first_place + jnp.sum(onehot * counts[:, None], axis=0)
        lo = first_place.reshape(-1, BLK)[:, 0] // BLK
        hi = (end_place.reshape(-1, BLK)[:, -1] + (BLK - 1)) // BLK

        def shards(v):
            v = v.reshape(4, 512)
            v = jnp.where((slot & 1) == 1, jnp.concatenate([v[1:2], v[0:1], v[3:4], v[2:3]]), v)
            v = jnp.where((slot & 2) == 2, jnp.concatenate([v[2:4], v[0:2]]), v)
            return v.reshape(1, length)

        seg = shards(row)
        places = shards(jnp.arange(length, dtype=jnp.int32) - first_place).astype(F32)
        inverse = jnp.exp(-2.0 * jnp.arange(HEAD_DIM // 2, dtype=F32) / HEAD_DIM * log_base)
        angles = inverse[:, None] * places
        cos, sin = jnp.cos(angles), jnp.sin(angles)
        head = jnp.stack([slot * 2, place, swapped.astype(jnp.int32), place >> 1] + [slot * 0] * 4)
        sc = jnp.concatenate([head.astype(jnp.int32), lo, hi]).astype(jnp.int32)

        smem = pl.BlockSpec(memory_space=pltpu.SMEM)
        vmem = pl.BlockSpec(memory_space=pltpu.VMEM)
        hbm = pl.BlockSpec(memory_space=pl.ANY)

        def shape(*dims, dtype=BF16):
            return jax.ShapeDtypeStruct(dims, dtype)

        w, qa, ka, kt, vn, ot, logsum, keep, send = pl.pallas_call(
            attend_forward_kernel,
            name="attend_forward",
            out_shape=(
                shape(768, 768), shape(3, 128, length), shape(3, length, 128), shape(192, length),
                shape(3, length, 64), shape(192, length), shape(8, length, dtype=F32),
                shape(2, 512, 768, dtype=F32), shape(2, 512, 768),
            ),
            in_specs=[smem, vmem, vmem, vmem, vmem, hbm, hbm, hbm],
            out_specs=(vmem,) * 9,
            scratch_shapes=[
                pltpu.VMEM((3, 80, length), BF16),
                pltpu.VMEM((3, 1, BLK), F32),
                pltpu.VMEM((3, 80, BLK), F32),
                pltpu.SemaphoreType.DMA((16,)),
            ],
            compiler_params=pltpu.CompilerParams(vmem_limit_bytes=48 << 20),
            cost_estimate=pl.CostEstimate(flops=20_000_000_000, bytes_accessed=24_000_000, transcendentals=6_000_000),
        )(sc, tok, cos, sin, seg, own, far_half, far_other)

        mine = keep + core(send)
        far = along(mine[1].astype(BF16), 1)

        scratch = [
            pltpu.VMEM((4, 3, 768, 768), BF16),
            pltpu.VMEM((4, 512, 768), F32),
            pltpu.VMEM((4, 512, 768), F32),
            pltpu.VMEM((4, 512, 768), BF16),
            pltpu.VMEM((512, 768), BF16),
            pltpu.VMEM((768, 512), BF16),
            pltpu.VMEM((512, 768), BF16),
            pltpu.VMEM((768, 512), BF16),
            pltpu.VMEM((512, 768), F32),
            pltpu.VMEM((512, 768), F32),
            pltpu.VMEM((512, 128), F32),
            pltpu.VMEM((2, 3, 768, 768), BF16),
            pltpu.SemaphoreType.DMA((4, 16)),
            pltpu.SemaphoreType.DMA((2, 16)),
        ]
        out, gz1, gz1_low, sums, keep_hi, send_hi, keep_lo, send_lo = pl.pallas_call(
            feed_forward_kernel,
            name="feed_forward",
            out_shape=(
                shape(512, 768), shape(512, 768, dtype=F32), shape(512, 768), shape(8, 768, dtype=F32),
                shape(2, 8, 3, 48, 768), shape(2, 8, 3, 48, 768), shape(2, 8, 3, 48, 768), shape(2, 8, 3, 48, 768),
            ),
            in_specs=[smem] + [vmem] * 6 + [hbm] * 8,
            out_specs=(vmem,) * 4 + (hbm,) * 4,
            scratch_shapes=scratch,
            compiler_params=pltpu.CompilerParams(vmem_limit_bytes=60 << 20),
            cost_estimate=pl.CostEstimate(flops=22_000_000_000, bytes_accessed=36_000_000, transcendentals=3_000_000),
        )(sc, x, mine[0], far, cot, norm_gain, norm_bias, *pieces)

        pair = jnp.stack([gz1_low, along(gz1_low, 1)])
        gb = jnp.concatenate([pair, core(pair)])
        back = trade(out)
        output = jnp.where(swapped, back, out)[None]

        def add(a, b):
            return (a.astype(F32) + b.astype(F32)).astype(BF16)

        parts = []
        for keep_w, send_w in ((keep_hi, send_hi), (keep_lo, send_lo)):
            v = add(keep_w, core(send_w))
            a, b = v[:, 0:4], v[:, 4:8]
            a, b = add(a[:, 0:2], down(a[:, 2:4])), add(b[:, 0:2], across(b[:, 2:4]))
            a, b = add(a[:, 0], across(a[:, 1])), add(b[:, 0], down(b[:, 1]))
            parts.append(jnp.stack([a, b], axis=1))
        v = add(parts[1], along(parts[0], 2))
        v = add(v[0], along(v[1], 1))
        for bit in extra:
            v = add(v, over(v, bit))
        ff_half, ff_other = plane_gather(v[0], v[1])

        for bit in [1 << b for b in range(dp.bit_length() - 1)]:
            sums = sums + over(sums, bit)
        for bit in (1, 2):
            sums = sums + along(sums, bit)

        grads, keep, send = pl.pallas_call(
            attend_backward_kernel,
            name="attend_backward",
            out_shape=(shape(2, 4, 96, 768), shape(2, 512, 768, dtype=F32), shape(2, 512, 768)),
            in_specs=[smem] + [vmem] * 11,
            out_specs=(vmem,) * 3,
            scratch_shapes=[
                pltpu.VMEM((192, length), BF16),
                pltpu.VMEM((8, length), F32),
                pltpu.VMEM((192, length), F32),
                pltpu.VMEM((3, 64, BLK), F32),
                pltpu.VMEM((3, 64, BLK), F32),
                pltpu.VMEM((576, length), BF16),
            ],
            compiler_params=pltpu.CompilerParams(vmem_limit_bytes=48 << 20),
            cost_estimate=pl.CostEstimate(flops=40_000_000_000, bytes_accessed=24_000_000, transcendentals=6_000_000),
        )(sc, gb, tok, w, qa, ka, kt, vn, ot, logsum, cos, sin)

        mine = keep + core(send)
        got = gz1 + (mine[0] + along(mine[1].astype(BF16), 1).astype(F32))
        back = trade(got.astype(BF16))
        grad_tokens = jnp.where(swapped, back.astype(F32), got)[None]

        a, b = grads[0], grads[1]
        a, b = add(a[0:2], down(a[2:4])), add(b[0:2], across(b[2:4]))
        a, b = add(a[0], across(a[1])), add(b[0], down(b[1]))
        v = jnp.stack([a, b])
        v = add(v, lax.ppermute(v, both, [(cell(i, k), cell(i, k ^ 2)) for i, k in away]))
        for bit in extra:
            v = add(v, over(v, bit))
        sibling = lax.ppermute(
            v, both, [(cell(i, k), cell(i ^ 1, k)) for i in range(dp) for k in range(tensor) if (i, k) not in away]
        )
        v = jnp.where(swapped, sibling, v)
        a = jnp.stack([v[0], across(v[0])])
        a = jnp.concatenate([a, down(a)])
        b = jnp.stack([v[1], down(v[1])])
        b = jnp.concatenate([b, across(b)])
        b = b.reshape(2, 2, 96, 768).transpose(1, 0, 2, 3).reshape(4, 96, 768)
        full = jnp.stack([a, b], axis=1)

        def unturn(v, bit, axis_index):
            n = v.shape[0]
            turned = v.reshape(n // (2 << axis_index), 2, 1 << axis_index, *v.shape[1:])[:, ::-1].reshape(v.shape)
            return jnp.where(((place >> bit) & 1) == 1, turned, v)

        full = unturn(unturn(full, 1, 0), 2, 1).reshape(768, 768).astype(F32)
        grad_w_qkv = full[:576].reshape(3, 192, 768).transpose(2, 0, 1)
        grad_w_out = full[576:]

        ff = jnp.stack([ff_half, ff_other]).reshape(2, 2, 2, 2, 3, 48, 768)
        ff = jnp.stack([ff[:, 0], ff[:, 1].transpose(0, 2, 1, 3, 4, 5)], axis=3)
        ff = ff.transpose(1, 2, 0, 3, 4, 5, 6).reshape(8, 2, 3, 48, 768)
        ff = unturn(unturn(unturn(ff, 0, 0), 1, 1), 2, 2)
        ff = ff.transpose(2, 0, 1, 3, 4).reshape(3, 768, 768)
        grad_w_gate_up = ff[:2].transpose(1, 0, 2).astype(F32)
        grad_w_down = ff[2].T.astype(F32)
        return (
            output, grad_tokens, grad_w_qkv, grad_w_out, grad_w_gate_up, grad_w_down, sums[0:2], sums[2:4],
        )

    placed = (
        P("dp", "tensor", None),
        P("dp", None),
        P(None, None, "tensor"),
        P("tensor", None),
        P(None, None, "tensor"),
        P("tensor", None),
        P(),
        P(),
        P("dp", "tensor", None),
    )
    return jax.shard_map(
        on_device,
        mesh=mesh,
        in_specs=placed,
        out_specs=(
            P("dp", "tensor", None),
            P("dp", "tensor", None),
            P(None, None, "tensor"),
            P("tensor", None),
            P(None, None, "tensor"),
            P("tensor", None),
            P(),
            P(),
        ),
        check_vma=False,
    )
```

```python
import functools
import math

import jax
import jax.numpy as jnp
from jax import lax
from jax.experimental import pallas as pl
from jax.experimental.pallas import tpu as pltpu
from jax.sharding import PartitionSpec as P

HEAD_DIM = 64
SEGS = 8
BLK = 256
F32 = jnp.float32
BF16 = jnp.bfloat16
MESH = pl.DeviceIdType.MESH
CHUNKS = 4
CHUNK = 128

epsilon = 1e-05
far_below = -1e30
log_base = math.log(1000.0)


def nn(a, b):
    return lax.dot_general(a, b, (((1,), (0,)), ((), ())), preferred_element_type=F32)


def nt(a, b):
    return lax.dot_general(a, b, (((1,), (1,)), ((), ())), preferred_element_type=F32)


def tn(a, b):
    return lax.dot_general(a, b, (((0,), (0,)), ((), ())), preferred_element_type=F32)


class Place:
    def __init__(self):
        p, z = lax.axis_index("dp"), lax.axis_index("tensor")
        self.p, self.z = p, z
        c, x, y = p % 2, (p // 2) % 2, (p // 4) % 2
        self.c, self.x, self.y = c, x, y
        self.place = p % 8
        self.x_place = self.place + 2 - 4 * x
        self.y_place = self.place + 4 - 8 * y
        self.d_place = self.x_place + 4 - 8 * y
        self.z1_at, self.z2_at = z + 1 - 2 * (z % 2), (z + 2) % 4
        self.sib = {"dp": p + 1 - 2 * c}
        self.xn = {"dp": p + 2 - 4 * x}
        self.yn = {"dp": p + 4 - 8 * y}
        self.z1 = {"tensor": self.z1_at}
        self.z2 = {"tensor": self.z2_at}
        self.pair = {"dp": p + 1 - 2 * c, "tensor": self.z2_at}
        self.cross = c + z // 2 - 2 * c * (z // 2)
        self.slot = (z + 2 * self.cross) % 4
        self.slot1 = self.slot + 1 - 2 * (self.slot % 2)
        self.slot2 = (self.slot + 2) % 4
        self.slot3 = (self.slot1 + 2) % 4


def greet(partners):
    barrier = pltpu.get_barrier_semaphore()
    for partner in partners:
        pl.semaphore_signal(barrier, inc=1, device_id=partner, device_id_type=MESH)
    pl.semaphore_wait(barrier, len(partners))


class Links:
    def __init__(self, send, recv):
        self.send, self.recv, self.count, self.started = send, recv, 0, []

    def make(self, src, dst, to):
        i = self.count
        self.count += 1
        return pltpu.make_async_remote_copy(
            src_ref=src, dst_ref=dst, send_sem=self.send.at[i], recv_sem=self.recv.at[i], device_id=to, device_id_type=MESH
        )

    def start(self, src, dst, to):
        copy = self.make(src, dst, to)
        copy.start()
        self.started.append(copy)
        return copy

    def wait_sends(self):
        for copy in self.started:
            copy.wait_send()


def rows_of(place, size=96, first=0):
    return pl.ds(pl.multiple_of(place * size + first, 16), size - first if first == 0 else size // 2)


class Spread:
    def __init__(self, me, links, view, src=None):
        self.me, self.links, self.view = me, links, view
        own = view(me.place, 0, 96)
        src = own if src is None else src
        self.from_x = links.start(src, own, me.xn)
        self.from_y = links.start(src, own, me.yn)
        self.from_sib = [links.start(src, own, me.sib)]

    def second(self):
        me, links, view = self.me, self.links, self.view
        self.from_x.wait_recv()
        part = view(me.x_place, 0, 48)
        self.low = links.start(part, part, me.yn)
        block = view(me.x_place, 0, 96)
        self.from_sib.append(links.start(block, block, me.sib))
        self.from_y.wait_recv()
        part = view(me.y_place, 48, 48)
        self.high = links.start(part, part, me.xn)
        block = view(me.y_place, 0, 96)
        self.from_sib.append(links.start(block, block, me.sib))

    def third(self):
        me, links, view = self.me, self.links, self.view
        self.low.wait_recv()
        self.high.wait_recv()
        block = view(me.d_place, 0, 96)
        self.from_sib.append(links.start(block, block, me.sib))

    def last(self):
        for copy in self.from_sib:
            copy.wait_recv()


def view_2d(ref):
    return lambda place, first, size: ref.at[pl.ds(pl.multiple_of(place * 96 + first, 16), size)]


def view_3d(ref):
    return lambda place, first, size: ref.at[:, pl.ds(pl.multiple_of(place * 96 + first, 16), size)]


def start_kernel(x, wo, fb, tok, wx, wf0, wf2, zb, token_send, token_recv, send, recv, local):
    me = Place()
    c, z = me.c, me.z
    away = z + c * (3 - 2 * z)

    barrier = pltpu.get_barrier_semaphore()
    partners = (me.sib, me.xn, me.yn, me.z1, me.z2)
    for partner in partners:
        pl.semaphore_signal(barrier, inc=1, device_id=partner, device_id_type=MESH)
    @pl.when(z % 3 != 0)
    def _():
        pl.semaphore_signal(barrier, inc=1, device_id={"tensor": 3 - z}, device_id_type=MESH)

    pl.semaphore_wait(barrier, len(partners) + z * (3 - z) // 2)

    def line(k):
        return k + c * (3 - 2 * k)

    def line_sib(k):
        return k + (1 - c) * (3 - 2 * k)

    far, near = {"tensor": line(0)}, {"tensor": line(1)}

    def part(ch):
        return pl.ds(ch * CHUNK, CHUNK)

    def copy(kind, k, ch, src, to):
        return pltpu.make_async_remote_copy(
            src_ref=src, dst_ref=tok.at[line(k), part(ch)], send_sem=token_send.at[kind, k, ch],
            recv_sem=token_recv.at[k, ch], device_id=to, device_id_type=MESH,
        )

    def own(ch):
        return x.at[part(ch)]

    def held(k, ch):
        return tok.at[line(k), part(ch)]

    for k, to in ((0, near), (1, far), (2, near), (3, near)):

        @pl.when(away == k)
        def _(k=k, to=to):
            for ch in range(CHUNKS):
                copy(0, k, ch, own(ch), to).start()
                if k < 2:
                    copy(1, k, ch, own(ch), me.sib).start()

    links = Links(send, recv)
    attn_z = links.start(view_2d(wo)(me.place, 0, 96), view_2d(wx)(me.place, 0, 96), me.z2)
    ff_z = links.start(fb, view_3d(wf2)(me.place, 0, 96), me.z2)
    ff0 = Spread(me, links, view_3d(wf0), fb)
    here = [
        pltpu.make_async_copy(fb, view_3d(wf0)(me.place, 0, 96), local.at[0]),
        pltpu.make_async_copy(fb, zb.at[0], local.at[1]),
    ]
    for h in here:
        h.start()

    @pl.when(away < 2)
    def _():
        mine = pltpu.make_async_copy(x, tok.at[z], local.at[2])
        mine.start()
        mine.wait()

    def forward(ch):
        @pl.when(away == 0)
        def _():
            for k in (1, 2, 3):
                copy(1, k, ch, held(k, ch), me.sib).wait_recv()
                copy(1, k, ch, held(k, ch), me.sib).start()

        @pl.when(away == 1)
        def _():
            for k in (2, 3, 0):
                copy(1, k, ch, held(k, ch), me.sib).wait_recv()
                if k:
                    copy(0, k, ch, held(k, ch), far).start()
                copy(1, k, ch, held(k, ch), me.sib).start()

    attn_z.wait_recv()
    attn = Spread(me, links, view_2d(wx))
    forward(0)
    attn.second()
    ff0.second()
    attn.third()
    forward(1)
    ff_z.wait_recv()
    ff2 = Spread(me, links, view_3d(wf2))
    keep = pltpu.make_async_copy(view_3d(wf2)(me.place, 0, 96), zb.at[1], local.at[3])
    keep.start()
    ff0.third()
    forward(2)
    ff2.second()
    forward(3)
    ff2.third()

    @pl.when(away >= 2)
    def _():
        for ch in range(CHUNKS):
            for k in range(4):
                pltpu.make_async_remote_copy(
                    src_ref=own(ch), dst_ref=tok.at[line_sib(k), part(ch)], send_sem=token_send.at[0, k, ch],
                    recv_sem=token_recv.at[k, ch], device_id=me.sib, device_id_type=MESH,
                ).wait_recv()

    for spread in (attn, ff0, ff2):
        spread.last()
    for h in here:
        h.wait()
    keep.wait()
    links.wait_sends()
    for k, to in ((0, near), (1, far), (2, near), (3, near)):

        @pl.when(away == k)
        def _(k=k, to=to):
            for ch in range(CHUNKS):
                copy(0, k, ch, own(ch), to).wait_send()
                if k == 1:
                    for j in (2, 3):
                        copy(0, j, ch, held(j, ch), to).wait_send()
                if k < 2:
                    for j in range(4):
                        copy(1, j, ch, own(ch) if j == k else held(j, ch), me.sib).wait_send()


def attend_forward_kernel(
    sc, tok, cos, sin, seg, own, other, w, qa, ka, kt, vn, ot, logsum, part, va, mx, acc, sem
):
    heads = 3
    width = heads * HEAD_DIM

    @pl.when(sc[0] == 0)
    def _():
        copy = pltpu.make_async_copy(own, w, sem.at[0])
        copy.start()
        copy.wait()

    @pl.when(sc[0] == 1)
    def _():
        copy = pltpu.make_async_copy(other, w, sem.at[0])
        copy.start()
        copy.wait()

    def project(e, _):
        at = pl.ds(pl.multiple_of(e * 512, 512), 512)
        made = nt(w[: 3 * width], tok[e])
        c, s = cos[:, at], sin[:, at]
        hot = (seg[:, at] == lax.broadcasted_iota(jnp.int32, (SEGS, 512), 0)).astype(F32)
        rest = jnp.zeros((64 - SEGS, 512), F32)
        one_row = (lax.broadcasted_iota(jnp.int32, (16, 512), 0) == 0).astype(F32)
        for h in range(heads):
            r = h * HEAD_DIM
            a1, a2 = made[r : r + 32], made[r + 32 : r + 64]
            q = jnp.concatenate([a1 * c - a2 * s, a2 * c + a1 * s], axis=0).astype(BF16).astype(F32)
            qa[h, :, at] = jnp.concatenate([q * 0.125, hot, rest], axis=0).astype(BF16)
            r += width
            a1, a2 = made[r : r + 32], made[r + 32 : r + 64]
            k = jnp.concatenate([a1 * c - a2 * s, a2 * c + a1 * s], axis=0)
            kt[h * HEAD_DIM : (h + 1) * HEAD_DIM, at] = k.astype(BF16)
            ka[h, at, :] = jnp.concatenate([k, (1.0 - hot) * far_below, rest], axis=0).T.astype(BF16)
            r += width
            v = made[r : r + 64]
            va[h, :, at] = jnp.concatenate([v, one_row], axis=0).astype(BF16)
            vn[h, at, :] = jnp.concatenate([v, jnp.zeros_like(v)], axis=0).T[:, :HEAD_DIM].astype(BF16)
        return 0

    lax.fori_loop(0, 4, project, 0)

    def query_block(i, _):
        at = pl.ds(pl.multiple_of(i * BLK, BLK), BLK)
        for h in range(heads):
            mx[h] = jnp.full((1, BLK), -3e38, F32)
            acc[h] = jnp.zeros((80, BLK), F32)

        def key_block(j, _):
            here = pl.ds(pl.multiple_of(j * BLK, BLK), BLK)
            for h in range(heads):
                scores = nn(ka[h, here, :], qa[h, :, at])
                before = mx[h]
                largest = jnp.maximum(before, jnp.max(scores, axis=0, keepdims=True))
                weights = jnp.exp(scores - largest).astype(BF16)
                acc[h] = acc[h] * jnp.exp(before - largest) + nn(va[h, :, here], weights)
                mx[h] = largest
            return 0

        lax.fori_loop(sc[8 + i], sc[16 + i], key_block, 0)
        for h in range(heads):
            total = acc[h, 64:65, :]
            ot[h * HEAD_DIM : (h + 1) * HEAD_DIM, at] = (acc[h, :64, :] / total).astype(BF16)
            logsum[pl.ds(h, 1), at] = mx[h] + jnp.log(total)
        return 0

    lax.fori_loop(0, 2048 // BLK, query_block, 0)
    for e in range(4):
        part[e] = tn(ot[:, e * 512 : (e + 1) * 512], w[3 * width :]).astype(BF16)


def attend_backward_kernel(
    sc, gb, tok, w, qa, ka, kt, vn, ot, logsum, cos, sin, grads, part, dot_, inner, dq, dk, dv, gp
):
    heads = 3
    width = heads * HEAD_DIM

    def begin(e, _):
        at = pl.ds(pl.multiple_of(e * 512, 512), 512)
        made = nt(w[3 * width :], gb[e]).astype(BF16)
        dot_[:, at] = made
        product = made.astype(F32) * ot[:, at].astype(F32)
        for h in range(heads):
            inner[pl.ds(h, 1), at] = jnp.sum(product[h * HEAD_DIM : (h + 1) * HEAD_DIM], axis=0, keepdims=True)
        return 0

    lax.fori_loop(0, 4, begin, 0)
    dq[...] = jnp.zeros_like(dq)

    def key_block(j, _):
        here = pl.ds(pl.multiple_of(j * BLK, BLK), BLK)
        for h in range(heads):
            dk[h] = jnp.zeros((HEAD_DIM, BLK), F32)
            dv[h] = jnp.zeros((HEAD_DIM, BLK), F32)

        def query_block(i, _):
            at = pl.ds(pl.multiple_of(i * BLK, BLK), BLK)
            for h in range(heads):
                rows = slice(h * HEAD_DIM, (h + 1) * HEAD_DIM)
                scores = nn(ka[h, here, :], qa[h, :, at])
                probability = jnp.exp(scores - logsum[pl.ds(h, 1), at])
                rise = nn(vn[h, here, :], dot_[rows, at])
                slope = (probability * (rise - inner[pl.ds(h, 1), at])).astype(BF16)
                dv[h] += nt(dot_[rows, at], probability.astype(BF16))
                dk[h] += nt(qa[h, :HEAD_DIM, at], slope)
                dq[rows, at] += nn(kt[rows, here], slope)
            return 0

        lax.fori_loop(sc[8 + j], sc[16 + j], query_block, 0)
        c, s = cos[:, here], sin[:, here]
        for h in range(heads):
            d1, d2 = dk[h, :32, :], dk[h, 32:, :]
            r = width + h * HEAD_DIM
            gp[r : r + 64, here] = jnp.concatenate([d1 * c + d2 * s, d2 * c - d1 * s], axis=0).astype(BF16)
            r += width
            gp[r : r + 64, here] = dv[h].astype(BF16)
        return 0

    lax.fori_loop(0, 2048 // BLK, key_block, 0)

    def turn(e, _):
        at = pl.ds(pl.multiple_of(e * 512, 512), 512)
        c, s = cos[:, at] * 0.125, sin[:, at] * 0.125
        for h in range(heads):
            r = h * HEAD_DIM
            d1, d2 = dq[r : r + 32, at], dq[r + 32 : r + 64, at]
            gp[r : r + 64, at] = jnp.concatenate([d1 * c + d2 * s, d2 * c - d1 * s], axis=0).astype(BF16)
        return 0

    lax.fori_loop(0, 4, turn, 0)
    for e in range(4):
        part[e] = tn(gp[:, e * 512 : (e + 1) * 512], w[: 3 * width]).astype(BF16)
    for block in range(4):
        if block < 3:
            rows = slice(block * width, (block + 1) * width)
            made = sum(nn(gp[rows, e * 512 : (e + 1) * 512], tok[e]) for e in range(4))
        else:
            made = sum(nn(ot[:, e * 512 : (e + 1) * 512], gb[e]) for e in range(4))
        grads[block * width : (block + 1) * width] = made.astype(BF16)


def row_mean(v):
    return jnp.mean(v, axis=-1, keepdims=True)


def norm_forward(summed):
    centred = summed - row_mean(summed)
    inverse = lax.rsqrt(row_mean(centred * centred) + epsilon)
    return centred * inverse, inverse


def norm_backward(scaled, normalized, inverse):
    return inverse * (scaled - row_mean(scaled) - normalized * row_mean(scaled * normalized))


def feed_forward_kernel(
    tok, part, cot, gain, bias, wf0, wf2, zc,
    out, gz1, gb, sums, keep_a, keep_b, send_a, send_b,
    w, slope_g, slope_u, hid, nb, nbt, gm, gmt, total, norm1, inv1, dw, lw, xs, from_core, from_z, to_z,
    send, recv, local, out_sem,
):
    me = Place()
    greet((me.sib, me.xn, me.yn, me.z1))
    links = Links(send, recv)
    loads = [
        pltpu.make_async_copy(tok.at[me.slot], xs, local.at[0]),
        pltpu.make_async_copy(wf0, w.at[0], local.at[1]),
        pltpu.make_async_copy(wf2, w.at[2], local.at[2]),
        pltpu.make_async_copy(zc.at[0], view_3d(w.at[1])(me.place, 0, 96), local.at[3]),
        pltpu.make_async_copy(zc.at[1], view_3d(w.at[3])(me.place, 0, 96), local.at[4]),
    ]

    def rows(ch):
        return pl.ds(ch * CHUNK, CHUNK)

    cores = [
        [links.start(part.at[shard, rows(ch)], from_core.at[i, rows(ch)], me.sib) for ch in range(CHUNKS)]
        for i, shard in ((1, me.slot3), (0, me.slot2))
    ]
    ff1 = Spread(me, links, view_3d(w.at[1]), zc.at[0])
    ff3 = Spread(me, links, view_3d(w.at[3]), zc.at[1])
    for load in loads:
        load.start()
    zs = []
    for ch in range(CHUNKS):
        cores[0][ch].wait_recv()
        at = rows(ch)
        to_z[at] = (part[me.slot1, at].astype(F32) + from_core[1, at].astype(F32)).astype(BF16)
        zs.append(links.start(to_z.at[at], from_z.at[at], me.z1))
    ff1.second()
    loads[0].wait()
    for ch in range(CHUNKS):
        if ch == CHUNKS - 1:
            ff3.second()
        cores[1][ch].wait_recv()
        zs[ch].wait_recv()
        at = rows(ch)
        branch = part[me.slot, at].astype(F32) + from_core[0, at].astype(F32) + from_z[at].astype(F32)
        n1, i1 = norm_forward(xs[at].astype(F32) + branch)
        norm1[at] = n1
        inv1[at] = jnp.broadcast_to(i1, (CHUNK, 128))
        normed = n1 * gain[0:1, :] + bias[0:1, :]
        total[at] = normed
        nb[at] = normed.astype(BF16)
        nbt[:, ch * CHUNK : (ch + 1) * CHUNK] = normed.T.astype(BF16)
    ff1.third()

    def forward(ez):
        gate = nn(nb[...], w[ez, 0])
        up = nn(nb[...], w[ez, 1])
        sig = 1.0 / (1.0 + jnp.exp(-gate))
        active = gate * sig
        low = (active * up).astype(BF16)
        hid[ez] = low
        slope_u[ez] = active.astype(BF16)
        slope_g[ez] = (up * sig * (1.0 + gate * (1.0 - sig))).astype(BF16)
        total[...] += nn(low, w[ez, 2])

    loads[1].wait()
    forward(0)
    ff3.third()
    loads[2].wait()
    forward(2)
    loads[3].wait()
    ff1.last()
    forward(1)
    loads[4].wait()
    ff3.last()
    forward(3)
    n2, i2 = norm_forward(total[...])
    out[...] = (n2 * gain[1:2, :] + bias[1:2, :]).astype(BF16)
    g = cot[...].astype(F32)
    sums[1:2, :] = jnp.sum(g * n2, axis=0, keepdims=True)
    sums[3:4, :] = jnp.sum(g, axis=0, keepdims=True)
    gz2 = norm_backward(g * gain[1:2, :], n2, i2)
    total[...] = gz2
    gm[...] = gz2.astype(BF16)
    gmt[...] = gz2.T.astype(BF16)

    def block(quad, core):
        return pl.ds(pl.multiple_of((quad * 2 + core) * 96, 32), 96)

    def stores(ez, i):
        made = []
        for oy in range(2):
            for ox in range(2):
                row = pl.multiple_of(((oy * 2 + ox) * 2 + me.c) * 96, 32)
                made.append((me.y == oy, dw.at[i, :, pl.ds(row, 48)], keep_a.at[ez, ox], send_a.at[ez, ox]))
                row = pl.multiple_of(row + 48, 16)
                made.append((me.x == ox, dw.at[i, :, pl.ds(row, 48)], keep_b.at[ez, oy], send_b.at[ez, oy]))
        return made

    def store(ez, i):
        for n, (here, src, kept, sent) in enumerate(stores(ez, i)):

            @pl.when(here)
            def _(n=n, src=src, kept=kept):
                pltpu.make_async_copy(src, kept, out_sem.at[i, n]).start()

            @pl.when(jnp.logical_not(here))
            def _(n=n, src=src, sent=sent):
                pltpu.make_async_copy(src, sent, out_sem.at[i, n]).start()

    def stored(ez, i):
        for n, (_, src, kept, _) in enumerate(stores(ez, i)):
            pltpu.make_async_copy(src, kept, out_sem.at[i, n]).wait()

    order = (1, 3, 0, 2)
    halves = []

    def settle(n):
        i = n % 2
        for quad in range(4):
            halves[n][quad].wait_recv()
            at = block(quad, me.c)
            for m in range(3):
                dw[i, m, at] = (dw[i, m, at].astype(F32) + lw[n, quad, m].astype(F32)).astype(BF16)
        store(order[n], i)

    for n, ez in enumerate(order):
        i = n % 2
        if n >= 2:
            stored(order[n - 2], i)
            for copy in halves[n - 2]:
                copy.wait_send()
        grad_hidden = nt(gm[...], w[ez, 2])
        dw[i, 2] = nn(gmt[...], hid[ez]).astype(BF16)
        gate = (grad_hidden * slope_g[ez].astype(F32)).astype(BF16)
        dw[i, 0] = nn(nbt[...], gate).astype(BF16)
        up = (grad_hidden * slope_u[ez].astype(F32)).astype(BF16)
        dw[i, 1] = nn(nbt[...], up).astype(BF16)
        halves.append(
            [links.make(dw.at[i, :, block(quad, 1 - me.c)], lw.at[n, quad], me.sib) for quad in range(4)]
        )
        for copy in halves[n]:
            copy.start()
        total[...] += nt(gate, w[ez, 0]) + nt(up, w[ez, 1])
        if n:
            settle(n - 1)

    g = total[...]
    sums[0:1, :] = jnp.sum(g * norm1[...], axis=0, keepdims=True)
    sums[2:3, :] = jnp.sum(g, axis=0, keepdims=True)
    sums[4:8, :] = jnp.zeros((4, 768), F32)
    first, second, third = [], [], []
    for ch in range(CHUNKS):
        at = rows(ch)
        made = norm_backward(total[at] * gain[0:1, :], norm1[at], inv1[at, 0:1])
        gz1[at] = made
        gb[me.slot, at] = made.astype(BF16)
        mine = gb.at[me.slot, at]
        first.append(links.start(mine, mine, me.z1))
        second.append(links.start(mine, mine, me.sib))
    settle(len(order) - 1)
    for ch in range(CHUNKS):
        at = rows(ch)
        first[ch].wait_recv()
        other = gb.at[me.slot1, at]
        third.append(links.start(other, other, me.sib))
    for copy in second + third:
        copy.wait_recv()
    for n in (2, 3):
        stored(order[n], n % 2)
        for copy in halves[n]:
            copy.wait_send()
    links.wait_sends()


def finish_kernel(
    extra, keep_a, keep_b, recv_a, recv_b, ga, part, gz1, sums_in,
    g_ff, g_attn, g_tok, sums,
    sa, sb, f2a, f2b, va, f3, f4, fe, a_in, a_mid, a_out, a_fin, a_two, ae, from_core, from_z, to_z, trade_out, trade_in, sum_in,
    send, recv, a_send, a_recv,
):
    me = Place()
    bits = [{"dp": me.p + bit - 2 * bit * ((me.p // bit) % 2)} for bit in extra]
    greet([me.sib, me.xn, me.yn, me.z1, me.z2, me.pair] + bits)
    links = Links(send, recv)

    def rows(ch):
        return pl.ds(ch * CHUNK, CHUNK)

    def add(*terms):
        return sum(t.astype(F32) for t in terms).astype(BF16)

    cores = [
        [links.start(part.at[shard, rows(ch)], from_core.at[i, rows(ch)], me.sib) for ch in range(CHUNKS)]
        for i, shard in ((1, me.slot3), (0, me.slot2))
    ]

    def half(oy, ox, h):
        return pl.ds(pl.multiple_of((oy * 2 + ox) * 192 + h * 96, 32), 96)

    attn_1 = []
    for o in range(2):
        attn_1.append(links.start(ga.at[half(1 - me.y, o, 0)], a_in.at[0, o], me.yn))
        attn_1.append(links.start(ga.at[half(o, 1 - me.x, 1)], a_in.at[1, o], me.xn))

    sums[...] = sums_in[...]
    around = [me.sib, me.xn, me.yn, me.z1, me.z2] + bits
    small = [links.start(sums, sum_in.at[0], around[0])]

    def small_step():
        n = len(small)
        small[-1].wait_recv()
        small[-1].wait_send()
        links.started = [copy for copy in links.started if copy is not small[n - 1]]
        sums[...] += sum_in[n - 1]
        if n < len(around):
            small.append(links.start(sums, sum_in.at[n], around[n]))

    order = (1, 3, 0, 2)
    ff_2 = {}

    def plane(ez):
        sa[ez] = add(keep_a[ez, 1 - me.x], recv_a[ez, 1 - me.x])
        sb[ez] = add(keep_b[ez, 1 - me.y], recv_b[ez, 1 - me.y])
        ff_2[ez] = (links.start(sa.at[ez], f2a.at[ez], me.xn), links.start(sb.at[ez], f2b.at[ez], me.yn))

    def planed(ez):
        ff_2[ez][0].wait_recv()
        va[ez, 0] = add(keep_a[ez, me.x], recv_a[ez, me.x], f2a[ez])
        ff_2[ez][1].wait_recv()
        va[ez, 1] = add(keep_b[ez, me.y], recv_b[ez, me.y], f2b[ez])

    plane(1)
    plane(3)
    zs = []
    for ch in range(CHUNKS):
        cores[0][ch].wait_recv()
        at = rows(ch)
        to_z[at] = add(part[me.slot1, at], from_core[1, at])
        zs.append(links.start(to_z.at[at], from_z.at[at], me.z1))
    plane(0)
    plane(2)
    small_step()
    for copy in attn_1:
        copy.wait_recv()
    a_mid[0] = add(ga[half(me.y, 1 - me.x, 0)], a_in[0, 1 - me.x])
    a_mid[1] = add(ga[half(1 - me.y, me.x, 1)], a_in[1, 1 - me.y])
    attn_2 = [links.start(a_mid.at[0], a_out.at[0], me.xn), links.start(a_mid.at[1], a_out.at[1], me.yn)]
    small_step()
    ff_3 = []
    for ez in (1, 3):
        planed(ez)
        ff_3.append(links.start(va.at[ez], f3.at[(ez - 1) // 2], me.z1))
    small_step()
    for copy in attn_2:
        copy.wait_recv()
    a_fin[:96] = add(ga[half(me.y, me.x, 0)], a_in[0, me.x], a_out[0])
    a_fin[96:] = add(ga[half(me.y, me.x, 1)], a_in[1, me.y], a_out[1])

    def attn_copy(n, src, dst, to):
        return pltpu.make_async_remote_copy(
            src_ref=src, dst_ref=dst, send_sem=a_send.at[n], recv_sem=a_recv.at[n], device_id=to, device_id_type=MESH
        )

    def quarter(oy, ox, first=0, size=192):
        return g_attn.at[pl.ds(pl.multiple_of((oy * 2 + ox) * 192 + first, 32), size)]

    def attn_over():
        return attn_copy(0, a_fin, a_two, me.z2)

    @pl.when(me.cross == 1)
    def _():
        attn_over().start()

    small_step()

    trades = [
        pltpu.make_async_remote_copy(
            src_ref=trade_out.at[rows(ch)], dst_ref=trade_in.at[rows(ch)], send_sem=a_send.at[8 + ch],
            recv_sem=a_recv.at[8 + ch], device_id=me.pair, device_id_type=MESH,
        )
        for ch in range(CHUNKS)
    ]
    for ch in range(CHUNKS):
        cores[1][ch].wait_recv()
        zs[ch].wait_recv()
        at = rows(ch)
        got = gz1[at] + (part[me.slot, at].astype(F32) + from_core[0, at].astype(F32) + from_z[at].astype(F32))

        @pl.when(me.cross == 0)
        def _(at=at, got=got):
            g_tok[at] = got

        @pl.when(me.cross == 1)
        def _(at=at, got=got, ch=ch):
            trade_out[at] = got.astype(BF16)
            trades[ch].start()

    planed(0)
    planed(2)
    ff_3[1].wait_recv()
    va[2] = add(va[2], f3[1])
    ff_4 = links.start(va.at[2], f4, me.z2)
    while len(small) < len(around):
        small_step()
    small_step()

    mine = quarter(me.y, me.x)

    def attn_send(n, src, to):
        return attn_copy(n, src, src, to)

    block_x, block_y = quarter(me.y, 1 - me.x), quarter(1 - me.y, me.x)
    low_x, high_y = quarter(me.y, 1 - me.x, 0, 96), quarter(1 - me.y, me.x, 96, 96)
    corner = quarter(1 - me.y, 1 - me.x)

    @pl.when(me.cross == 0)
    def _():
        attn_over().wait_recv()
        total = add(a_fin[...], a_two[...])
        for n, bit in enumerate(bits):
            ae[n, 0] = total
            step = attn_copy(16 + n, ae.at[n, 0], ae.at[n, 1], bit)
            step.start()
            step.wait()
            total = add(total, ae[n, 1])
        g_attn[pl.ds(pl.multiple_of((me.y * 2 + me.x) * 192, 32), 192)] = total
        attn_send(1, mine, me.xn).start()
        attn_send(2, mine, me.yn).start()
        attn_send(3, mine, me.sib).start()

    ff_3[0].wait_recv()
    va[0] = add(va[0], f3[0])
    ff_4.wait_recv()
    total = add(va[0], f4[...])
    for n, bit in enumerate(bits):
        fe[n, 0] = total
        step = links.start(fe.at[n, 0], fe.at[n, 1], bit)
        step.wait_recv()
        total = add(total, fe[n, 1])
    for h in range(2):
        g_ff[:, pl.ds(pl.multiple_of(me.place * 96 + h * 48, 16), 48)] = total[h]
    spread = Spread(me, links, view_3d(g_ff))

    @pl.when(me.cross == 0)
    def _():
        attn_send(1, block_x, me.xn).wait_recv()
        attn_send(4, low_x, me.yn).start()
        attn_send(5, block_x, me.sib).start()
        attn_send(2, block_y, me.yn).wait_recv()
        attn_send(6, high_y, me.xn).start()
        attn_send(7, block_y, me.sib).start()

    spread.second()

    @pl.when(me.cross == 0)
    def _():
        attn_send(4, low_x, me.yn).wait_recv()
        attn_send(6, high_y, me.xn).wait_recv()
        attn_send(12, corner, me.sib).start()
        for n, src, to in (
            (1, mine, me.xn), (2, mine, me.yn), (3, mine, me.sib), (4, low_x, me.yn), (5, block_x, me.sib),
            (6, high_y, me.xn), (7, block_y, me.sib), (12, corner, me.sib),
        ):
            attn_send(n, src, to).wait_send()

    @pl.when(me.cross == 1)
    def _():
        for ch in range(CHUNKS):
            trades[ch].wait_recv()
            g_tok[rows(ch)] = trade_in[rows(ch)].astype(F32)
        attn_over().wait_send()
        for n, src in ((3, mine), (5, block_x), (7, block_y), (12, corner)):
            attn_send(n, src, me.sib).wait_recv()
        for ch in range(CHUNKS):
            trades[ch].wait_send()

    spread.third()
    spread.last()
    links.wait_sends()


def solution(mesh):
    dp, tensor = mesh.shape["dp"], mesh.shape["tensor"]
    assert tensor == 4 and dp >= 8 and dp & (dp - 1) == 0
    extra = [1 << b for b in range(3, dp.bit_length() - 1)]
    both = ("dp", "tensor")

    def cell(i, k):
        return i * tensor + k

    def over(x, bit):
        return lax.ppermute(x, "dp", [(i, i ^ bit) for i in range(dp)])

    away = [(i, k) for i in range(dp) for k in range(tensor) if (i & 1) != (k >> 1)]

    def trade(x):
        return lax.ppermute(x, both, [(cell(i, k), cell(i ^ 1, k ^ 2)) for i, k in away])

    smem = pl.BlockSpec(memory_space=pltpu.SMEM)
    vmem = pl.BlockSpec(memory_space=pltpu.VMEM)
    hbm = pl.BlockSpec(memory_space=pl.ANY)

    def shape(*dims, dtype=BF16):
        return jax.ShapeDtypeStruct(dims, dtype)

    def dma(*dims):
        return pltpu.SemaphoreType.DMA(dims)

    def params(mib, number=None):
        if number is None:
            return pltpu.CompilerParams(vmem_limit_bytes=mib << 20)
        return pltpu.CompilerParams(vmem_limit_bytes=mib << 20, collective_id=number, has_side_effects=True)

    def on_device(tokens, segments, w_qkv, w_out, w_gate_up, w_down, norm_gain, norm_bias, cotangent):
        p, z = lax.axis_index("dp"), lax.axis_index("tensor")
        swapped = (p & 1) != (z >> 1)
        place = p & 7

        own = jnp.concatenate([w_qkv.transpose(1, 2, 0).reshape(576, 768), w_out])
        rows = lax.dynamic_slice(w_gate_up, (place * 96, 0, 0), (96, 2, 768))
        block = jnp.stack([rows[:, 0], rows[:, 1], lax.dynamic_slice(w_down, (place * 96, 0), (96, 768))])

        tok, wx, wf0, wf2, zb = pl.pallas_call(
            start_kernel,
            name="start",
            out_shape=(
                shape(4, 512, 768), shape(768, 768), shape(3, 768, 768), shape(3, 768, 768), shape(2, 3, 96, 768),
            ),
            in_specs=[hbm] * 3,
            out_specs=(hbm,) * 5,
            scratch_shapes=[dma(2, 4, CHUNKS), dma(4, CHUNKS), dma(40), dma(40), dma(4)],
            compiler_params=params(16, 0),
        )(tokens[0], own, block)

        row = jnp.where(swapped, over(segments, 1), segments)[0]
        length = row.shape[0]
        onehot = (row[None, :] == jnp.arange(SEGS, dtype=jnp.int32)[:, None]).astype(jnp.int32)
        counts = jnp.sum(onehot, axis=1)
        order = jnp.arange(SEGS, dtype=jnp.int32)
        starts = jnp.sum(jnp.where(order[None, :] < order[:, None], counts[None, :], 0), axis=1)
        first_place = jnp.sum(onehot * starts[:, None], axis=0)
        end_place = first_place + jnp.sum(onehot * counts[:, None], axis=0)
        lo = first_place.reshape(-1, BLK)[:, 0] // BLK
        hi = (end_place.reshape(-1, BLK)[:, -1] + (BLK - 1)) // BLK
        seg = row[None, :]
        places = (jnp.arange(length, dtype=jnp.int32) - first_place)[None, :].astype(F32)
        inverse = jnp.exp(-2.0 * jnp.arange(HEAD_DIM // 2, dtype=F32) / HEAD_DIM * log_base)
        angles = inverse[:, None] * places
        cos, sin = jnp.cos(angles), jnp.sin(angles)
        sc = jnp.concatenate([jnp.full((8,), swapped.astype(jnp.int32)), lo, hi]).astype(jnp.int32)

        zc = lax.ppermute(zb, "tensor", [(i, i ^ 1) for i in range(tensor)])
        cot, _ = lax.optimization_barrier((cotangent[0], zb))
        cot = jnp.where(swapped, trade(cot), cot)

        w, qa, ka, kt, vn, ot, logsum, part = pl.pallas_call(
            attend_forward_kernel,
            name="attend_forward",
            out_shape=(
                shape(768, 768), shape(3, 128, length), shape(3, length, 128), shape(192, length),
                shape(3, length, 64), shape(192, length), shape(8, length, dtype=F32), shape(4, 512, 768),
            ),
            in_specs=[smem, vmem, vmem, vmem, vmem, hbm, hbm],
            out_specs=(vmem,) * 8,
            scratch_shapes=[
                pltpu.VMEM((3, 80, length), BF16),
                pltpu.VMEM((3, 1, BLK), F32),
                pltpu.VMEM((3, 80, BLK), F32),
                dma(1),
            ],
            compiler_params=params(48),
            cost_estimate=pl.CostEstimate(flops=20_000_000_000, bytes_accessed=24_000_000, transcendentals=6_000_000),
        )(sc, tok, cos, sin, seg, own, wx)

        out, gz1, gb, sums, keep_a, keep_b, send_a, send_b = pl.pallas_call(
            feed_forward_kernel,
            name="feed_forward",
            out_shape=(
                shape(512, 768), shape(512, 768, dtype=F32), shape(4, 512, 768), shape(8, 768, dtype=F32),
                *(shape(4, 2, 3, 48, 768),) * 4,
            ),
            in_specs=[hbm] + [vmem] * 4 + [hbm] * 3,
            out_specs=(vmem,) * 4 + (hbm,) * 4,
            scratch_shapes=[
                pltpu.VMEM((4, 3, 768, 768), BF16),
                pltpu.VMEM((4, 512, 768), BF16),
                pltpu.VMEM((4, 512, 768), BF16),
                pltpu.VMEM((4, 512, 768), BF16),
                pltpu.VMEM((512, 768), BF16),
                pltpu.VMEM((768, 512), BF16),
                pltpu.VMEM((512, 768), BF16),
                pltpu.VMEM((768, 512), BF16),
                pltpu.VMEM((512, 768), F32),
                pltpu.VMEM((512, 768), F32),
                pltpu.VMEM((512, 128), F32),
                pltpu.VMEM((2, 3, 768, 768), BF16),
                pltpu.VMEM((4, 4, 3, 96, 768), BF16),
                pltpu.VMEM((512, 768), BF16),
                pltpu.VMEM((2, 512, 768), BF16),
                pltpu.VMEM((512, 768), BF16),
                pltpu.VMEM((512, 768), BF16),
                dma(64), dma(64), dma(5), dma(2, 8),
            ],
            compiler_params=params(62, 1),
            cost_estimate=pl.CostEstimate(flops=22_000_000_000, bytes_accessed=36_000_000, transcendentals=3_000_000),
        )(tok, part, cot, norm_gain, norm_bias, wf0, wf2, zc)

        recv_a, recv_b = over(send_a, 4), over(send_b, 2)
        output = jnp.where(swapped, trade(out), out)[None]

        grads, part = pl.pallas_call(
            attend_backward_kernel,
            name="attend_backward",
            out_shape=(shape(768, 768), shape(4, 512, 768)),
            in_specs=[smem] + [vmem] * 11,
            out_specs=(vmem,) * 2,
            scratch_shapes=[
                pltpu.VMEM((192, length), BF16),
                pltpu.VMEM((8, length), F32),
                pltpu.VMEM((192, length), F32),
                pltpu.VMEM((3, 64, BLK), F32),
                pltpu.VMEM((3, 64, BLK), F32),
                pltpu.VMEM((576, length), BF16),
            ],
            compiler_params=params(48),
            cost_estimate=pl.CostEstimate(flops=40_000_000_000, bytes_accessed=24_000_000, transcendentals=6_000_000),
        )(sc, gb, tok, w, qa, ka, kt, vn, ot, logsum, cos, sin)

        spare = max(len(extra), 1)
        half = (48, 768)
        g_ff, g_attn, g_tok, sums = pl.pallas_call(
            functools.partial(finish_kernel, extra),
            name="finish",
            out_shape=(shape(3, 768, 768), shape(768, 768), shape(512, 768, dtype=F32), shape(8, 768, dtype=F32)),
            in_specs=[vmem] * 8,
            out_specs=(vmem,) * 4,
            scratch_shapes=[
                pltpu.VMEM((4, 3, *half), BF16),
                pltpu.VMEM((4, 3, *half), BF16),
                pltpu.VMEM((4, 3, *half), BF16),
                pltpu.VMEM((4, 3, *half), BF16),
                pltpu.VMEM((4, 2, 3, *half), BF16),
                pltpu.VMEM((2, 2, 3, *half), BF16),
                pltpu.VMEM((2, 3, *half), BF16),
                pltpu.VMEM((spare, 2, 2, 3, *half), BF16),
                pltpu.VMEM((2, 2, 96, 768), BF16),
                pltpu.VMEM((2, 96, 768), BF16),
                pltpu.VMEM((2, 96, 768), BF16),
                pltpu.VMEM((192, 768), BF16),
                pltpu.VMEM((192, 768), BF16),
                pltpu.VMEM((spare, 2, 192, 768), BF16),
                pltpu.VMEM((2, 512, 768), BF16),
                pltpu.VMEM((512, 768), BF16),
                pltpu.VMEM((512, 768), BF16),
                pltpu.VMEM((512, 768), BF16),
                pltpu.VMEM((512, 768), BF16),
                pltpu.VMEM((5 + spare, 8, 768), F32),
                dma(64), dma(64), dma(16 + spare), dma(16 + spare),
            ],
            compiler_params=params(48, 2),
        )(keep_a, keep_b, recv_a, recv_b, grads, part, gz1, sums)

        full = g_attn.astype(F32)
        return (
            output,
            g_tok[None],
            full[:576].reshape(3, 192, 768).transpose(2, 0, 1),
            full[576:],
            g_ff[:2].transpose(1, 0, 2).astype(F32),
            g_ff[2].T.astype(F32),
            sums[0:2],
            sums[2:4],
        )

    placed = (
        P("dp", "tensor", None),
        P("dp", None),
        P(None, None, "tensor"),
        P("tensor", None),
        P(None, None, "tensor"),
        P("tensor", None),
        P(),
        P(),
        P("dp", "tensor", None),
    )
    return jax.shard_map(
        on_device,
        mesh=mesh,
        in_specs=placed,
        out_specs=(
            P("dp", "tensor", None),
            P("dp", "tensor", None),
            P(None, None, "tensor"),
            P("tensor", None),
            P(None, None, "tensor"),
            P("tensor", None),
            P(),
            P(),
        ),
        check_vma=False,
    )
```

```python
import functools
import math

import jax
import jax.numpy as jnp
from jax import lax
from jax.experimental import pallas as pl
from jax.experimental.pallas import tpu as pltpu
from jax.sharding import PartitionSpec as P

HEAD_DIM = 64
SEGS = 8
BLK = 256
F32 = jnp.float32
BF16 = jnp.bfloat16
MESH = pl.DeviceIdType.MESH
CHUNKS = 4
CHUNK = 128

epsilon = 1e-05
far_below = -1e30
log_base = math.log(1000.0)


def nn(a, b):
    return lax.dot_general(a, b, (((1,), (0,)), ((), ())), preferred_element_type=F32)


def nt(a, b):
    return lax.dot_general(a, b, (((1,), (1,)), ((), ())), preferred_element_type=F32)


def tn(a, b):
    return lax.dot_general(a, b, (((0,), (0,)), ((), ())), preferred_element_type=F32)


class Place:
    def __init__(self):
        p, z = lax.axis_index("dp"), lax.axis_index("tensor")
        self.p, self.z = p, z
        c, x, y = p % 2, (p // 2) % 2, (p // 4) % 2
        self.c, self.x, self.y = c, x, y
        self.place = p % 8
        self.x_place = self.place + 2 - 4 * x
        self.y_place = self.place + 4 - 8 * y
        self.d_place = self.x_place + 4 - 8 * y
        self.z1_at, self.z2_at = z + 1 - 2 * (z % 2), (z + 2) % 4
        self.sib = {"dp": p + 1 - 2 * c}
        self.xn = {"dp": p + 2 - 4 * x}
        self.yn = {"dp": p + 4 - 8 * y}
        self.z1 = {"tensor": self.z1_at}
        self.z2 = {"tensor": self.z2_at}
        self.pair = {"dp": p + 1 - 2 * c, "tensor": self.z2_at}
        self.cross = c + z // 2 - 2 * c * (z // 2)
        self.slot = (z + 2 * self.cross) % 4
        self.slot1 = self.slot + 1 - 2 * (self.slot % 2)
        self.slot2 = (self.slot + 2) % 4
        self.slot3 = (self.slot1 + 2) % 4


def greet(partners):
    barrier = pltpu.get_barrier_semaphore()
    for partner in partners:
        pl.semaphore_signal(barrier, inc=1, device_id=partner, device_id_type=MESH)
    pl.semaphore_wait(barrier, len(partners))


class Links:
    def __init__(self, send, recv):
        self.send, self.recv, self.count, self.started = send, recv, 0, []

    def make(self, src, dst, to):
        i = self.count
        self.count += 1
        return pltpu.make_async_remote_copy(
            src_ref=src, dst_ref=dst, send_sem=self.send.at[i], recv_sem=self.recv.at[i], device_id=to, device_id_type=MESH
        )

    def start(self, src, dst, to):
        copy = self.make(src, dst, to)
        copy.start()
        self.started.append(copy)
        return copy

    def wait_sends(self):
        for copy in self.started:
            copy.wait_send()


class Spread:
    def __init__(self, me, links, view, src=None):
        self.me, self.links, self.view = me, links, view
        own = view(me.place, 0, 96)
        src = own if src is None else src
        self.from_x = links.start(src, own, me.xn)
        self.from_y = links.start(src, own, me.yn)
        self.from_sib = [links.start(src, own, me.sib)]

    def second(self):
        me, links, view = self.me, self.links, self.view
        self.from_x.wait_recv()
        part = view(me.x_place, 0, 48)
        self.low = links.start(part, part, me.yn)
        block = view(me.x_place, 0, 96)
        self.from_sib.append(links.start(block, block, me.sib))
        self.from_y.wait_recv()
        part = view(me.y_place, 48, 48)
        self.high = links.start(part, part, me.xn)
        block = view(me.y_place, 0, 96)
        self.from_sib.append(links.start(block, block, me.sib))

    def third(self):
        me, links, view = self.me, self.links, self.view
        self.low.wait_recv()
        self.high.wait_recv()
        block = view(me.d_place, 0, 96)
        self.from_sib.append(links.start(block, block, me.sib))

    def last(self):
        for copy in self.from_sib:
            copy.wait_recv()


class Corner(Spread):
    def __init__(self, me, links, view, own, from_x, from_y):
        self.me, self.links, self.view = me, links, view
        first, last = pl.ds(0, 48), pl.ds(48, 48)
        self.low = links.start(from_x.at[:, first], view(me.x_place, 0, 48), me.yn)
        self.high = links.start(from_y.at[:, last], view(me.y_place, 48, 48), me.xn)
        self.from_sib = [
            links.start(src, view(place, 0, 96), me.sib)
            for src, place in ((own, me.place), (from_x, me.x_place), (from_y, me.y_place))
        ]


def view_2d(ref):
    return lambda place, first, size: ref.at[pl.ds(pl.multiple_of(place * 96 + first, 16), size)]


def view_3d(ref):
    return lambda place, first, size: ref.at[:, pl.ds(pl.multiple_of(place * 96 + first, 16), size)]


def start_kernel(x, wo, fb, tok, wx, wf0, zb, token_send, token_recv, send, recv, local):
    me = Place()
    c, z = me.c, me.z
    away = z + c * (3 - 2 * z)

    barrier = pltpu.get_barrier_semaphore()
    partners = (me.sib, me.xn, me.yn, me.z1, me.z2)
    for partner in partners:
        pl.semaphore_signal(barrier, inc=1, device_id=partner, device_id_type=MESH)
    @pl.when(z % 3 != 0)
    def _():
        pl.semaphore_signal(barrier, inc=1, device_id={"tensor": 3 - z}, device_id_type=MESH)

    pl.semaphore_wait(barrier, len(partners) + z * (3 - z) // 2)

    def line(k):
        return k + c * (3 - 2 * k)

    def line_sib(k):
        return k + (1 - c) * (3 - 2 * k)

    far, near = {"tensor": line(0)}, {"tensor": line(1)}

    def part(ch):
        return pl.ds(ch * CHUNK, CHUNK)

    def copy(kind, k, ch, src, to):
        return pltpu.make_async_remote_copy(
            src_ref=src, dst_ref=tok.at[line(k), part(ch)], send_sem=token_send.at[kind, k, ch],
            recv_sem=token_recv.at[k, ch], device_id=to, device_id_type=MESH,
        )

    def own(ch):
        return x.at[part(ch)]

    def held(k, ch):
        return tok.at[line(k), part(ch)]

    for k, to in ((0, near), (1, far), (2, near), (3, near)):

        @pl.when(away == k)
        def _(k=k, to=to):
            for ch in range(CHUNKS):
                copy(0, k, ch, own(ch), to).start()
                if k < 2:
                    copy(1, k, ch, own(ch), me.sib).start()

    links = Links(send, recv)
    attn_z = links.start(view_2d(wo)(me.place, 0, 96), view_2d(wx)(me.place, 0, 96), me.z2)
    ff_z = links.start(fb, zb.at[1], me.z2)
    ff0 = Spread(me, links, view_3d(wf0), fb)
    here = [
        pltpu.make_async_copy(fb, view_3d(wf0)(me.place, 0, 96), local.at[0]),
        pltpu.make_async_copy(fb, zb.at[0], local.at[1]),
    ]
    for h in here:
        h.start()

    @pl.when(away < 2)
    def _():
        mine = pltpu.make_async_copy(x, tok.at[z], local.at[2])
        mine.start()
        mine.wait()

    def forward(ch):
        @pl.when(away == 0)
        def _():
            for k in (1, 2, 3):
                copy(1, k, ch, held(k, ch), me.sib).wait_recv()
                copy(1, k, ch, held(k, ch), me.sib).start()

        @pl.when(away == 1)
        def _():
            for k in (2, 3, 0):
                copy(1, k, ch, held(k, ch), me.sib).wait_recv()
                if k:
                    copy(0, k, ch, held(k, ch), far).start()
                copy(1, k, ch, held(k, ch), me.sib).start()

    attn_z.wait_recv()
    attn = Spread(me, links, view_2d(wx))
    forward(0)
    ff0.second()
    forward(1)
    attn.second()
    ff0.third()
    forward(2)
    attn.third()
    forward(3)

    @pl.when(away >= 2)
    def _():
        for ch in range(CHUNKS):
            for k in range(4):
                pltpu.make_async_remote_copy(
                    src_ref=own(ch), dst_ref=tok.at[line_sib(k), part(ch)], send_sem=token_send.at[0, k, ch],
                    recv_sem=token_recv.at[k, ch], device_id=me.sib, device_id_type=MESH,
                ).wait_recv()

    for spread in (attn, ff0):
        spread.last()
    ff_z.wait_recv()
    for h in here:
        h.wait()
    links.wait_sends()
    for k, to in ((0, near), (1, far), (2, near), (3, near)):

        @pl.when(away == k)
        def _(k=k, to=to):
            for ch in range(CHUNKS):
                copy(0, k, ch, own(ch), to).wait_send()
                if k == 1:
                    for j in (2, 3):
                        copy(0, j, ch, held(j, ch), to).wait_send()
                if k < 2:
                    for j in range(4):
                        copy(1, j, ch, own(ch) if j == k else held(j, ch), me.sib).wait_send()


def attend_forward_kernel(
    sc, tok, cos, sin, seg, own, other, w, qa, ka, kt, vn, ot, logsum, part, va, mx, acc, sem
):
    heads = 3
    width = heads * HEAD_DIM

    @pl.when(sc[0] == 0)
    def _():
        copy = pltpu.make_async_copy(own, w, sem.at[0])
        copy.start()
        copy.wait()

    @pl.when(sc[0] == 1)
    def _():
        copy = pltpu.make_async_copy(other, w, sem.at[0])
        copy.start()
        copy.wait()

    def project(e, _):
        at = pl.ds(pl.multiple_of(e * 512, 512), 512)
        made = nt(w[: 3 * width], tok[e])
        c, s = cos[:, at], sin[:, at]
        hot = (seg[:, at] == lax.broadcasted_iota(jnp.int32, (SEGS, 512), 0)).astype(F32)
        rest = jnp.zeros((64 - SEGS, 512), F32)
        one_row = (lax.broadcasted_iota(jnp.int32, (16, 512), 0) == 0).astype(F32)
        for h in range(heads):
            r = h * HEAD_DIM
            a1, a2 = made[r : r + 32], made[r + 32 : r + 64]
            q = jnp.concatenate([a1 * c - a2 * s, a2 * c + a1 * s], axis=0).astype(BF16).astype(F32)
            qa[h, :, at] = jnp.concatenate([q * 0.125, hot, rest], axis=0).astype(BF16)
            r += width
            a1, a2 = made[r : r + 32], made[r + 32 : r + 64]
            k = jnp.concatenate([a1 * c - a2 * s, a2 * c + a1 * s], axis=0)
            kt[h * HEAD_DIM : (h + 1) * HEAD_DIM, at] = k.astype(BF16)
            ka[h, at, :] = jnp.concatenate([k, (1.0 - hot) * far_below, rest], axis=0).T.astype(BF16)
            r += width
            v = made[r : r + 64]
            va[h, :, at] = jnp.concatenate([v, one_row], axis=0).astype(BF16)
            vn[h, at, :] = jnp.concatenate([v, jnp.zeros_like(v)], axis=0).T[:, :HEAD_DIM].astype(BF16)
        return 0

    lax.fori_loop(0, 4, project, 0)

    def query_block(i, _):
        at = pl.ds(pl.multiple_of(i * BLK, BLK), BLK)
        for h in range(heads):
            mx[h] = jnp.full((1, BLK), -3e38, F32)
            acc[h] = jnp.zeros((80, BLK), F32)

        def key_block(j, _):
            here = pl.ds(pl.multiple_of(j * BLK, BLK), BLK)
            for h in range(heads):
                scores = nn(ka[h, here, :], qa[h, :, at])
                before = mx[h]
                largest = jnp.maximum(before, jnp.max(scores, axis=0, keepdims=True))
                weights = jnp.exp(scores - largest).astype(BF16)
                acc[h] = acc[h] * jnp.exp(before - largest) + nn(va[h, :, here], weights)
                mx[h] = largest
            return 0

        lax.fori_loop(sc[8 + i], sc[16 + i], key_block, 0)
        for h in range(heads):
            total = acc[h, 64:65, :]
            ot[h * HEAD_DIM : (h + 1) * HEAD_DIM, at] = (acc[h, :64, :] / total).astype(BF16)
            logsum[pl.ds(h, 1), at] = mx[h] + jnp.log(total)
        return 0

    lax.fori_loop(0, 2048 // BLK, query_block, 0)
    for e in range(4):
        part[e] = tn(ot[:, e * 512 : (e + 1) * 512], w[3 * width :]).astype(BF16)


def attend_backward_kernel(
    sc, gb, tok, w, qa, ka, kt, vn, ot, logsum, cos, sin, grads, part, dot_, inner, dq, dk, dv, gp
):
    heads = 3
    width = heads * HEAD_DIM

    def begin(e, _):
        at = pl.ds(pl.multiple_of(e * 512, 512), 512)
        made = nt(w[3 * width :], gb[e]).astype(BF16)
        dot_[:, at] = made
        product = made.astype(F32) * ot[:, at].astype(F32)
        for h in range(heads):
            inner[pl.ds(h, 1), at] = jnp.sum(product[h * HEAD_DIM : (h + 1) * HEAD_DIM], axis=0, keepdims=True)
        return 0

    lax.fori_loop(0, 4, begin, 0)
    dq[...] = jnp.zeros_like(dq)

    def key_block(j, _):
        here = pl.ds(pl.multiple_of(j * BLK, BLK), BLK)
        for h in range(heads):
            dk[h] = jnp.zeros((HEAD_DIM, BLK), F32)
            dv[h] = jnp.zeros((HEAD_DIM, BLK), F32)

        def query_block(i, _):
            at = pl.ds(pl.multiple_of(i * BLK, BLK), BLK)
            for h in range(heads):
                rows = slice(h * HEAD_DIM, (h + 1) * HEAD_DIM)
                scores = nn(ka[h, here, :], qa[h, :, at])
                probability = jnp.exp(scores - logsum[pl.ds(h, 1), at])
                rise = nn(vn[h, here, :], dot_[rows, at])
                slope = (probability * (rise - inner[pl.ds(h, 1), at])).astype(BF16)
                dv[h] += nt(dot_[rows, at], probability.astype(BF16))
                dk[h] += nt(qa[h, :HEAD_DIM, at], slope)
                dq[rows, at] += nn(kt[rows, here], slope)
            return 0

        lax.fori_loop(sc[8 + j], sc[16 + j], query_block, 0)
        c, s = cos[:, here], sin[:, here]
        for h in range(heads):
            d1, d2 = dk[h, :32, :], dk[h, 32:, :]
            r = width + h * HEAD_DIM
            gp[r : r + 64, here] = jnp.concatenate([d1 * c + d2 * s, d2 * c - d1 * s], axis=0).astype(BF16)
            r += width
            gp[r : r + 64, here] = dv[h].astype(BF16)
        return 0

    lax.fori_loop(0, 2048 // BLK, key_block, 0)

    def turn(e, _):
        at = pl.ds(pl.multiple_of(e * 512, 512), 512)
        c, s = cos[:, at] * 0.125, sin[:, at] * 0.125
        for h in range(heads):
            r = h * HEAD_DIM
            d1, d2 = dq[r : r + 32, at], dq[r + 32 : r + 64, at]
            gp[r : r + 64, at] = jnp.concatenate([d1 * c + d2 * s, d2 * c - d1 * s], axis=0).astype(BF16)
        return 0

    lax.fori_loop(0, 4, turn, 0)
    for e in range(4):
        part[e] = tn(gp[:, e * 512 : (e + 1) * 512], w[: 3 * width]).astype(BF16)
    for block in range(4):
        if block < 3:
            rows = slice(block * width, (block + 1) * width)
            made = sum(nn(gp[rows, e * 512 : (e + 1) * 512], tok[e]) for e in range(4))
        else:
            made = sum(nn(ot[:, e * 512 : (e + 1) * 512], gb[e]) for e in range(4))
        grads[block * width : (block + 1) * width] = made.astype(BF16)


def row_mean(v):
    return jnp.mean(v, axis=-1, keepdims=True)


def norm_forward(summed):
    centred = summed - row_mean(summed)
    inverse = lax.rsqrt(row_mean(centred * centred) + epsilon)
    return centred * inverse, inverse


def norm_backward(scaled, normalized, inverse):
    return inverse * (scaled - row_mean(scaled) - normalized * row_mean(scaled * normalized))


def feed_forward_kernel(
    tok, part, cot_in, gain, bias, wf0, zb, zx, zy, zc,
    out, gz1, gb, sums, keep_a, keep_b, send_a, send_b, zs_out,
    w, slope_g, slope_u, hid, nb, nbt, gm, gmt, total, norm1, inv1, dw, lw, xs, cot, from_core, from_z, to_z,
    f1a, f1b, f2a, f2b, send, recv, local, out_sem, trade_sem,
):
    me = Place()
    greet((me.sib, me.xn, me.yn, me.z1, me.pair))
    links = Links(send, recv)
    loads = [
        pltpu.make_async_copy(tok.at[me.slot], xs, local.at[0]),
        pltpu.make_async_copy(wf0, w.at[0], local.at[1]),
        pltpu.make_async_copy(zb.at[1], view_3d(w.at[2])(me.place, 0, 96), local.at[2]),
        pltpu.make_async_copy(zc.at[0], view_3d(w.at[1])(me.place, 0, 96), local.at[3]),
        pltpu.make_async_copy(zc.at[1], view_3d(w.at[3])(me.place, 0, 96), local.at[4]),
        pltpu.make_async_copy(zx, view_3d(w.at[2])(me.x_place, 0, 96), local.at[5]),
        pltpu.make_async_copy(zy, view_3d(w.at[2])(me.y_place, 0, 96), local.at[6]),
    ]

    def cot_here():
        return pltpu.make_async_copy(cot_in, cot, local.at[7])

    def cot_there():
        return pltpu.make_async_remote_copy(
            src_ref=cot_in, dst_ref=cot, send_sem=trade_sem.at[0], recv_sem=trade_sem.at[1], device_id=me.pair,
            device_id_type=MESH,
        )

    def rows(ch):
        return pl.ds(ch * CHUNK, CHUNK)

    cores = [
        [links.start(part.at[shard, rows(ch)], from_core.at[i, rows(ch)], me.sib) for ch in range(CHUNKS)]
        for i, shard in ((1, me.slot3), (0, me.slot2))
    ]
    ff2 = Corner(me, links, view_3d(w.at[2]), zb.at[1], zx, zy)
    ff1 = Spread(me, links, view_3d(w.at[1]), zc.at[0])
    ff3 = Spread(me, links, view_3d(w.at[3]), zc.at[1])
    for load in loads:
        load.start()
    zs = []
    for ch in range(CHUNKS):
        cores[0][ch].wait_recv()
        at = rows(ch)
        to_z[at] = (part[me.slot1, at].astype(F32) + from_core[1, at].astype(F32)).astype(BF16)
        zs.append(links.start(to_z.at[at], from_z.at[at], me.z1))

    @pl.when(me.cross == 0)
    def _():
        cot_here().start()

    @pl.when(me.cross == 1)
    def _():
        cot_there().start()

    ff2.third()
    ff1.second()
    loads[0].wait()
    for ch in range(CHUNKS):
        if ch == CHUNKS - 1:
            ff3.second()
        cores[1][ch].wait_recv()
        zs[ch].wait_recv()
        at = rows(ch)
        branch = part[me.slot, at].astype(F32) + from_core[0, at].astype(F32) + from_z[at].astype(F32)
        n1, i1 = norm_forward(xs[at].astype(F32) + branch)
        norm1[at] = n1
        inv1[at] = jnp.broadcast_to(i1, (CHUNK, 128))
        normed = n1 * gain[0:1, :] + bias[0:1, :]
        total[at] = normed
        nb[at] = normed.astype(BF16)
        nbt[:, ch * CHUNK : (ch + 1) * CHUNK] = normed.T.astype(BF16)
    ff1.third()

    def forward(ez):
        gate = nn(nb[...], w[ez, 0])
        up = nn(nb[...], w[ez, 1])
        sig = 1.0 / (1.0 + jnp.exp(-gate))
        active = gate * sig
        low = (active * up).astype(BF16)
        hid[ez] = low
        slope_u[ez] = active.astype(BF16)
        slope_g[ez] = (up * sig * (1.0 + gate * (1.0 - sig))).astype(BF16)
        total[...] += nn(low, w[ez, 2])

    loads[1].wait()
    forward(0)
    ff3.third()
    for load in (loads[2], loads[5], loads[6]):
        load.wait()
    ff2.last()
    forward(2)
    loads[3].wait()
    ff1.last()
    forward(1)
    loads[4].wait()
    ff3.last()
    forward(3)
    n2, i2 = norm_forward(total[...])
    out[...] = (n2 * gain[1:2, :] + bias[1:2, :]).astype(BF16)

    @pl.when(me.cross == 0)
    def _():
        cot_here().wait()

    @pl.when(me.cross == 1)
    def _():
        cot_there().wait()

    g = cot[...].astype(F32)
    sums[1:2, :] = jnp.sum(g * n2, axis=0, keepdims=True)
    sums[3:4, :] = jnp.sum(g, axis=0, keepdims=True)
    gz2 = norm_backward(g * gain[1:2, :], n2, i2)
    total[...] = gz2
    gm[...] = gz2.astype(BF16)
    gmt[...] = gz2.T.astype(BF16)

    def block(quad, core):
        return pl.ds(pl.multiple_of((quad * 2 + core) * 96, 32), 96)

    order = (1, 3, 0, 2)
    halves = []
    first, last = pl.ds(0, 48), pl.ds(48, 48)

    def slopes(ez):
        grad_hidden = nt(gm[...], w[ez, 2])
        gate = (grad_hidden * slope_g[ez].astype(F32)).astype(BF16)
        up = (grad_hidden * slope_u[ez].astype(F32)).astype(BF16)
        slope_g[ez] = gate
        slope_u[ez] = up
        total[...] += nt(gate, w[ez, 0]) + nt(up, w[ez, 1])

    def weights(n):
        i, ez = n % 2, order[n]
        if n >= 2:
            for copy in halves[n - 2]:
                copy.wait_send()
        dw[i, 2] = nn(gmt[...], hid[ez]).astype(BF16)
        dw[i, 0] = nn(nbt[...], slope_g[ez]).astype(BF16)
        dw[i, 1] = nn(nbt[...], slope_u[ez]).astype(BF16)
        halves.append([links.make(dw.at[i, :, block(quad, 1 - me.c)], lw.at[n, quad], me.sib) for quad in range(4)])
        for copy in halves[n]:
            copy.start()

    def settle(n):
        for quad in range(4):
            halves[n][quad].wait_recv()
            for m in range(3):
                lw[n, quad, m] = (lw[n, quad, m].astype(F32) + dw[n % 2, m, block(quad, me.c)].astype(F32)).astype(BF16)

    plane_1, plane_2 = {}, {}

    def plane_first(n):
        plane_1[n] = [
            (
                links.start(lw.at[n, (1 - me.y) * 2 + o, :, first], f1a.at[n, o], me.yn),
                links.start(lw.at[n, o * 2 + 1 - me.x, :, last], f1b.at[n, o], me.xn),
            )
            for o in range(2)
        ]

    def plane_second(n):
        for o in range(2):
            plane_1[n][o][0].wait_recv()
            f1a[n, o] = (f1a[n, o].astype(F32) + lw[n, me.y * 2 + o, :, first].astype(F32)).astype(BF16)
            plane_1[n][o][1].wait_recv()
            f1b[n, o] = (f1b[n, o].astype(F32) + lw[n, o * 2 + me.x, :, last].astype(F32)).astype(BF16)
        plane_2[n] = (
            links.start(f1a.at[n, 1 - me.x], f2a.at[n], me.xn),
            links.start(f1b.at[n, 1 - me.y], f2b.at[n], me.yn),
        )

    def plane_last(n):
        plane_2[n][0].wait_recv()
        zs_out[n, 0] = (f1a[n, me.x].astype(F32) + f2a[n].astype(F32)).astype(BF16)
        plane_2[n][1].wait_recv()
        zs_out[n, 1] = (f1b[n, me.y].astype(F32) + f2b[n].astype(F32)).astype(BF16)

    def stores(n):
        made = []
        for oy in range(2):
            for ox in range(2):
                src = lw.at[n, oy * 2 + ox]
                made.append((me.y == oy, src.at[:, first], keep_a.at[n - 2, ox], send_a.at[n - 2, ox]))
                made.append((me.x == ox, src.at[:, last], keep_b.at[n - 2, oy], send_b.at[n - 2, oy]))
        return made

    def store(n):
        for number, (here, src, kept, sent) in enumerate(stores(n)):

            @pl.when(here)
            def _(number=number, src=src, kept=kept):
                pltpu.make_async_copy(src, kept, out_sem.at[n - 2, number]).start()

            @pl.when(jnp.logical_not(here))
            def _(number=number, src=src, sent=sent):
                pltpu.make_async_copy(src, sent, out_sem.at[n - 2, number]).start()

    slopes(1)
    weights(0)
    slopes(3)
    settle(0)
    plane_first(0)
    weights(1)
    slopes(0)
    settle(1)
    plane_first(1)
    slopes(2)
    g = total[...]
    sums[0:1, :] = jnp.sum(g * norm1[...], axis=0, keepdims=True)
    sums[2:3, :] = jnp.sum(g, axis=0, keepdims=True)
    sums[4:8, :] = jnp.zeros((4, 768), F32)
    to_pair, to_core, on_core = [], [], []
    for ch in range(CHUNKS):
        at = rows(ch)
        made = norm_backward(total[at] * gain[0:1, :], norm1[at], inv1[at, 0:1])
        gz1[at] = made
        gb[me.slot, at] = made.astype(BF16)
        mine = gb.at[me.slot, at]
        to_pair.append(links.start(mine, mine, me.z1))
        to_core.append(links.start(mine, mine, me.sib))
    weights(2)
    plane_second(0)
    weights(3)
    settle(2)
    store(2)
    plane_second(1)
    settle(3)
    store(3)
    for ch in range(CHUNKS):
        to_pair[ch].wait_recv()
        other = gb.at[me.slot1, rows(ch)]
        on_core.append(links.start(other, other, me.sib))
    plane_last(0)
    plane_last(1)
    for copy in to_core + on_core:
        copy.wait_recv()
    for n in (2, 3):
        for number, (_, src, kept, _) in enumerate(stores(n)):
            pltpu.make_async_copy(src, kept, out_sem.at[n - 2, number]).wait()
        for copy in halves[n]:
            copy.wait_send()
    links.wait_sends()


def finish_kernel(
    extra, keep_a, keep_b, recv_a, recv_b, zr, ga, part, gz1, sums_in,
    g_ff, g_attn, g_tok, sums,
    sa, sb, f2a, f2b, va, f4, fe, a_in, a_mid, a_out, a_fin, a_two, ae, from_core, from_z, to_z, trade_out, trade_in, sum_in,
    send, recv, a_send, a_recv,
):
    me = Place()
    bits = [{"dp": me.p + bit - 2 * bit * ((me.p // bit) % 2)} for bit in extra]
    greet([me.sib, me.xn, me.yn, me.z1, me.z2, me.pair] + bits)
    links = Links(send, recv)

    def rows(ch):
        return pl.ds(ch * CHUNK, CHUNK)

    def add(*terms):
        return sum(t.astype(F32) for t in terms).astype(BF16)

    cores = [
        [links.start(part.at[shard, rows(ch)], from_core.at[i, rows(ch)], me.sib) for ch in range(CHUNKS)]
        for i, shard in ((1, me.slot3), (0, me.slot2))
    ]

    def half(oy, ox, h):
        return pl.ds(pl.multiple_of((oy * 2 + ox) * 192 + h * 96, 32), 96)

    attn_1 = []
    for o in range(2):
        attn_1.append(links.start(ga.at[half(1 - me.y, o, 0)], a_in.at[0, o], me.yn))
        attn_1.append(links.start(ga.at[half(o, 1 - me.x, 1)], a_in.at[1, o], me.xn))

    sums[...] = sums_in[...]
    around = [me.sib, me.xn, me.yn, me.z1, me.z2] + bits
    small = [links.start(sums, sum_in.at[0], around[0])]

    def small_step():
        n = len(small)
        small[-1].wait_recv()
        small[-1].wait_send()
        links.started = [copy for copy in links.started if copy is not small[n - 1]]
        sums[...] += sum_in[n - 1]
        if n < len(around):
            small.append(links.start(sums, sum_in.at[n], around[n]))

    ff_2 = {}

    def plane(ez):
        sa[ez] = add(keep_a[ez, 1 - me.x], recv_a[ez, 1 - me.x])
        sb[ez] = add(keep_b[ez, 1 - me.y], recv_b[ez, 1 - me.y])
        ff_2[ez] = (links.start(sa.at[ez], f2a.at[ez], me.xn), links.start(sb.at[ez], f2b.at[ez], me.yn))

    def planed(ez):
        ff_2[ez][0].wait_recv()
        va[ez, 0] = add(keep_a[ez, me.x], recv_a[ez, me.x], f2a[ez], zr[ez, 0])
        ff_2[ez][1].wait_recv()
        va[ez, 1] = add(keep_b[ez, me.y], recv_b[ez, me.y], f2b[ez], zr[ez, 1])

    plane(1)
    zs = []
    for ch in range(CHUNKS):
        cores[0][ch].wait_recv()
        at = rows(ch)
        to_z[at] = add(part[me.slot1, at], from_core[1, at])
        zs.append(links.start(to_z.at[at], from_z.at[at], me.z1))
    plane(0)
    planed(1)
    ff_4 = links.start(va.at[1], f4, me.z2)
    small_step()
    for copy in attn_1:
        copy.wait_recv()
    a_mid[0] = add(ga[half(me.y, 1 - me.x, 0)], a_in[0, 1 - me.x])
    a_mid[1] = add(ga[half(1 - me.y, me.x, 1)], a_in[1, 1 - me.y])
    attn_2 = [links.start(a_mid.at[0], a_out.at[0], me.xn), links.start(a_mid.at[1], a_out.at[1], me.yn)]
    small_step()
    planed(0)
    small_step()
    for copy in attn_2:
        copy.wait_recv()
    a_fin[:96] = add(ga[half(me.y, me.x, 0)], a_in[0, me.x], a_out[0])
    a_fin[96:] = add(ga[half(me.y, me.x, 1)], a_in[1, me.y], a_out[1])

    def attn_copy(n, src, dst, to):
        return pltpu.make_async_remote_copy(
            src_ref=src, dst_ref=dst, send_sem=a_send.at[n], recv_sem=a_recv.at[n], device_id=to, device_id_type=MESH
        )

    def quarter(oy, ox, first=0, size=192):
        return g_attn.at[pl.ds(pl.multiple_of((oy * 2 + ox) * 192 + first, 32), size)]

    def attn_over():
        return attn_copy(0, a_fin, a_two, me.z2)

    @pl.when(me.cross == 1)
    def _():
        attn_over().start()

    small_step()

    trades = [
        pltpu.make_async_remote_copy(
            src_ref=trade_out.at[rows(ch)], dst_ref=trade_in.at[rows(ch)], send_sem=a_send.at[8 + ch],
            recv_sem=a_recv.at[8 + ch], device_id=me.pair, device_id_type=MESH,
        )
        for ch in range(CHUNKS)
    ]
    for ch in range(CHUNKS):
        cores[1][ch].wait_recv()
        zs[ch].wait_recv()
        at = rows(ch)
        got = gz1[at] + (part[me.slot, at].astype(F32) + from_core[0, at].astype(F32) + from_z[at].astype(F32))

        @pl.when(me.cross == 0)
        def _(at=at, got=got):
            g_tok[at] = got

        @pl.when(me.cross == 1)
        def _(at=at, got=got, ch=ch):
            trade_out[at] = got.astype(BF16)
            trades[ch].start()

    while len(small) < len(around):
        small_step()
    small_step()

    mine = quarter(me.y, me.x)

    def attn_send(n, src, to):
        return attn_copy(n, src, src, to)

    block_x, block_y = quarter(me.y, 1 - me.x), quarter(1 - me.y, me.x)
    low_x, high_y = quarter(me.y, 1 - me.x, 0, 96), quarter(1 - me.y, me.x, 96, 96)
    corner = quarter(1 - me.y, 1 - me.x)

    @pl.when(me.cross == 0)
    def _():
        attn_over().wait_recv()
        total = add(a_fin[...], a_two[...])
        for n, bit in enumerate(bits):
            ae[n, 0] = total
            step = attn_copy(16 + n, ae.at[n, 0], ae.at[n, 1], bit)
            step.start()
            step.wait()
            total = add(total, ae[n, 1])
        g_attn[pl.ds(pl.multiple_of((me.y * 2 + me.x) * 192, 32), 192)] = total
        attn_send(1, mine, me.xn).start()
        attn_send(2, mine, me.yn).start()
        attn_send(3, mine, me.sib).start()

    ff_4.wait_recv()
    total = add(va[0], f4[...])
    for n, bit in enumerate(bits):
        fe[n, 0] = total
        step = links.start(fe.at[n, 0], fe.at[n, 1], bit)
        step.wait_recv()
        total = add(total, fe[n, 1])
    for h in range(2):
        g_ff[:, pl.ds(pl.multiple_of(me.place * 96 + h * 48, 16), 48)] = total[h]
    spread = Spread(me, links, view_3d(g_ff))

    @pl.when(me.cross == 0)
    def _():
        attn_send(1, block_x, me.xn).wait_recv()
        attn_send(4, low_x, me.yn).start()
        attn_send(5, block_x, me.sib).start()
        attn_send(2, block_y, me.yn).wait_recv()
        attn_send(6, high_y, me.xn).start()
        attn_send(7, block_y, me.sib).start()

    spread.second()

    @pl.when(me.cross == 0)
    def _():
        attn_send(4, low_x, me.yn).wait_recv()
        attn_send(6, high_y, me.xn).wait_recv()
        attn_send(12, corner, me.sib).start()
        for n, src, to in (
            (1, mine, me.xn), (2, mine, me.yn), (3, mine, me.sib), (4, low_x, me.yn), (5, block_x, me.sib),
            (6, high_y, me.xn), (7, block_y, me.sib), (12, corner, me.sib),
        ):
            attn_send(n, src, to).wait_send()

    @pl.when(me.cross == 1)
    def _():
        for ch in range(CHUNKS):
            trades[ch].wait_recv()
            g_tok[rows(ch)] = trade_in[rows(ch)].astype(F32)
        attn_over().wait_send()
        for n, src in ((3, mine), (5, block_x), (7, block_y), (12, corner)):
            attn_send(n, src, me.sib).wait_recv()
        for ch in range(CHUNKS):
            trades[ch].wait_send()

    spread.third()
    spread.last()
    links.wait_sends()


def widen_kernel(attn, out_rows, gate_up, down, g_qkv, g_out, g_gate_up, g_down):
    g_qkv[...] = attn[...].astype(F32)
    g_out[...] = out_rows[...].astype(F32)
    g_gate_up[:, 0, :] = gate_up[0].astype(F32)
    g_gate_up[:, 1, :] = gate_up[1].astype(F32)
    g_down[...] = down[0].astype(F32).T


def solution(mesh):
    dp, tensor = mesh.shape["dp"], mesh.shape["tensor"]
    assert tensor == 4 and dp >= 8 and dp & (dp - 1) == 0
    extra = [1 << b for b in range(3, dp.bit_length() - 1)]
    both = ("dp", "tensor")

    def cell(i, k):
        return i * tensor + k

    def over(x, bit):
        return lax.ppermute(x, "dp", [(i, i ^ bit) for i in range(dp)])

    away = [(i, k) for i in range(dp) for k in range(tensor) if (i & 1) != (k >> 1)]

    def trade(x):
        return lax.ppermute(x, both, [(cell(i, k), cell(i ^ 1, k ^ 2)) for i, k in away])

    smem = pl.BlockSpec(memory_space=pltpu.SMEM)
    vmem = pl.BlockSpec(memory_space=pltpu.VMEM)
    hbm = pl.BlockSpec(memory_space=pl.ANY)

    def shape(*dims, dtype=BF16):
        return jax.ShapeDtypeStruct(dims, dtype)

    def dma(*dims):
        return pltpu.SemaphoreType.DMA(dims)

    def params(mib, number=None):
        if number is None:
            return pltpu.CompilerParams(vmem_limit_bytes=mib << 20)
        return pltpu.CompilerParams(vmem_limit_bytes=mib << 20, collective_id=number, has_side_effects=True)

    def on_device(tokens, segments, w_qkv, w_out, w_gate_up, w_down, norm_gain, norm_bias, cotangent):
        p, z = lax.axis_index("dp"), lax.axis_index("tensor")
        swapped = (p & 1) != (z >> 1)
        place = p & 7

        own = jnp.concatenate([w_qkv.transpose(1, 2, 0).reshape(576, 768), w_out])
        rows = lax.dynamic_slice(w_gate_up, (place * 96, 0, 0), (96, 2, 768))
        block = jnp.stack([rows[:, 0], rows[:, 1], lax.dynamic_slice(w_down, (place * 96, 0), (96, 768))])

        tok, wx, wf0, zb = pl.pallas_call(
            start_kernel,
            name="start",
            out_shape=(
                shape(4, 512, 768), shape(768, 768), shape(3, 768, 768), shape(2, 3, 96, 768),
            ),
            in_specs=[hbm] * 3,
            out_specs=(hbm,) * 4,
            scratch_shapes=[dma(2, 4, CHUNKS), dma(4, CHUNKS), dma(40), dma(40), dma(4)],
            compiler_params=params(16, 0),
        )(tokens[0], own, block)

        row = jnp.where(swapped, over(segments, 1), segments)[0]
        length = row.shape[0]
        onehot = (row[None, :] == jnp.arange(SEGS, dtype=jnp.int32)[:, None]).astype(jnp.int32)
        counts = jnp.sum(onehot, axis=1)
        order = jnp.arange(SEGS, dtype=jnp.int32)
        starts = jnp.sum(jnp.where(order[None, :] < order[:, None], counts[None, :], 0), axis=1)
        first_place = jnp.sum(onehot * starts[:, None], axis=0)
        end_place = first_place + jnp.sum(onehot * counts[:, None], axis=0)
        lo = first_place.reshape(-1, BLK)[:, 0] // BLK
        hi = (end_place.reshape(-1, BLK)[:, -1] + (BLK - 1)) // BLK
        seg = row[None, :]
        places = (jnp.arange(length, dtype=jnp.int32) - first_place)[None, :].astype(F32)
        inverse = jnp.exp(-2.0 * jnp.arange(HEAD_DIM // 2, dtype=F32) / HEAD_DIM * log_base)
        angles = inverse[:, None] * places
        cos, sin = jnp.cos(angles), jnp.sin(angles)
        sc = jnp.concatenate([jnp.full((8,), swapped.astype(jnp.int32)), lo, hi]).astype(jnp.int32)

        zc = lax.ppermute(zb, "tensor", [(i, i ^ 1) for i in range(tensor)])
        zx, zy = over(zb[1], 2), over(zb[1], 4)

        w, qa, ka, kt, vn, ot, logsum, part = pl.pallas_call(
            attend_forward_kernel,
            name="attend_forward",
            out_shape=(
                shape(768, 768), shape(3, 128, length), shape(3, length, 128), shape(192, length),
                shape(3, length, 64), shape(192, length), shape(8, length, dtype=F32), shape(4, 512, 768),
            ),
            in_specs=[smem, vmem, vmem, vmem, vmem, hbm, hbm],
            out_specs=(vmem,) * 8,
            scratch_shapes=[
                pltpu.VMEM((3, 80, length), BF16),
                pltpu.VMEM((3, 1, BLK), F32),
                pltpu.VMEM((3, 80, BLK), F32),
                dma(1),
            ],
            compiler_params=params(48),
            cost_estimate=pl.CostEstimate(flops=20_000_000_000, bytes_accessed=24_000_000, transcendentals=6_000_000),
        )(sc, tok, cos, sin, seg, own, wx)

        out, gz1, gb, sums, keep_a, keep_b, send_a, send_b, zs = pl.pallas_call(
            feed_forward_kernel,
            name="feed_forward",
            out_shape=(
                shape(512, 768), shape(512, 768, dtype=F32), shape(4, 512, 768), shape(8, 768, dtype=F32),
                *(shape(2, 2, 3, 48, 768),) * 5,
            ),
            in_specs=[hbm, vmem, hbm, vmem, vmem] + [hbm] * 5,
            out_specs=(vmem,) * 4 + (hbm,) * 4 + (vmem,),
            scratch_shapes=[
                pltpu.VMEM((4, 3, 768, 768), BF16),
                pltpu.VMEM((4, 512, 768), BF16),
                pltpu.VMEM((4, 512, 768), BF16),
                pltpu.VMEM((4, 512, 768), BF16),
                pltpu.VMEM((512, 768), BF16),
                pltpu.VMEM((768, 512), BF16),
                pltpu.VMEM((512, 768), BF16),
                pltpu.VMEM((768, 512), BF16),
                pltpu.VMEM((512, 768), F32),
                pltpu.VMEM((512, 768), F32),
                pltpu.VMEM((512, 128), F32),
                pltpu.VMEM((2, 3, 768, 768), BF16),
                pltpu.VMEM((4, 4, 3, 96, 768), BF16),
                pltpu.VMEM((512, 768), BF16),
                pltpu.VMEM((512, 768), BF16),
                pltpu.VMEM((2, 512, 768), BF16),
                pltpu.VMEM((512, 768), BF16),
                pltpu.VMEM((512, 768), BF16),
                pltpu.VMEM((2, 2, 3, 48, 768), BF16),
                pltpu.VMEM((2, 2, 3, 48, 768), BF16),
                pltpu.VMEM((2, 3, 48, 768), BF16),
                pltpu.VMEM((2, 3, 48, 768), BF16),
                dma(80), dma(80), dma(8), dma(2, 8), dma(2),
            ],
            compiler_params=params(62, 1),
            cost_estimate=pl.CostEstimate(flops=22_000_000_000, bytes_accessed=36_000_000, transcendentals=3_000_000),
        )(tok, part, cotangent[0], norm_gain, norm_bias, wf0, zb, zx, zy, zc)

        recv_a, recv_b = over(send_a, 4), over(send_b, 2)
        zr = lax.ppermute(zs, "tensor", [(i, i ^ 1) for i in range(tensor)])
        output = jnp.where(swapped, trade(out), out)[None]

        grads, part = pl.pallas_call(
            attend_backward_kernel,
            name="attend_backward",
            out_shape=(shape(768, 768), shape(4, 512, 768)),
            in_specs=[smem] + [vmem] * 11,
            out_specs=(vmem,) * 2,
            scratch_shapes=[
                pltpu.VMEM((192, length), BF16),
                pltpu.VMEM((8, length), F32),
                pltpu.VMEM((192, length), F32),
                pltpu.VMEM((3, 64, BLK), F32),
                pltpu.VMEM((3, 64, BLK), F32),
                pltpu.VMEM((576, length), BF16),
            ],
            compiler_params=params(48),
            cost_estimate=pl.CostEstimate(flops=40_000_000_000, bytes_accessed=24_000_000, transcendentals=6_000_000),
        )(sc, gb, tok, w, qa, ka, kt, vn, ot, logsum, cos, sin)

        spare = max(len(extra), 1)
        half = (48, 768)
        g_ff, g_attn, g_tok, sums = pl.pallas_call(
            functools.partial(finish_kernel, extra),
            name="finish",
            out_shape=(shape(3, 768, 768), shape(768, 768), shape(512, 768, dtype=F32), shape(8, 768, dtype=F32)),
            in_specs=[vmem] * 9,
            out_specs=(vmem,) * 4,
            scratch_shapes=[
                *[pltpu.VMEM((2, 3, *half), BF16)] * 4,
                pltpu.VMEM((2, 2, 3, *half), BF16),
                pltpu.VMEM((2, 3, *half), BF16),
                pltpu.VMEM((spare, 2, 2, 3, *half), BF16),
                pltpu.VMEM((2, 2, 96, 768), BF16),
                pltpu.VMEM((2, 96, 768), BF16),
                pltpu.VMEM((2, 96, 768), BF16),
                pltpu.VMEM((192, 768), BF16),
                pltpu.VMEM((192, 768), BF16),
                pltpu.VMEM((spare, 2, 192, 768), BF16),
                pltpu.VMEM((2, 512, 768), BF16),
                pltpu.VMEM((512, 768), BF16),
                pltpu.VMEM((512, 768), BF16),
                pltpu.VMEM((512, 768), BF16),
                pltpu.VMEM((512, 768), BF16),
                pltpu.VMEM((5 + spare, 8, 768), F32),
                dma(64), dma(64), dma(16 + spare), dma(16 + spare),
            ],
            compiler_params=params(48, 2),
        )(keep_a, keep_b, recv_a, recv_b, zr, grads, part, gz1, sums)

        g_qkv, g_out, g_gate_up, g_down = pl.pallas_call(
            widen_kernel,
            name="widen",
            grid=(3,),
            out_shape=(
                shape(576, 768, dtype=F32), shape(192, 768, dtype=F32), shape(768, 2, 768, dtype=F32),
                shape(768, 768, dtype=F32),
            ),
            in_specs=[
                pl.BlockSpec((192, 768), lambda i: (i, 0)),
                pl.BlockSpec((64, 768), lambda i: (9 + i, 0)),
                pl.BlockSpec((2, 256, 768), lambda i: (0, i, 0)),
                pl.BlockSpec((1, 768, 256), lambda i: (2, 0, i)),
            ],
            out_specs=(
                pl.BlockSpec((192, 768), lambda i: (i, 0)),
                pl.BlockSpec((64, 768), lambda i: (i, 0)),
                pl.BlockSpec((256, 2, 768), lambda i: (i, 0, 0)),
                pl.BlockSpec((256, 768), lambda i: (i, 0)),
            ),
            compiler_params=params(32),
            cost_estimate=pl.CostEstimate(flops=0, bytes_accessed=16_000_000, transcendentals=0),
        )(g_attn, g_attn, g_ff, g_ff)
        return (
            output, g_tok[None], g_qkv.reshape(3, 192, 768).transpose(2, 0, 1), g_out, g_gate_up, g_down,
            sums[0:2], sums[2:4],
        )

    placed = (
        P("dp", "tensor", None),
        P("dp", None),
        P(None, None, "tensor"),
        P("tensor", None),
        P(None, None, "tensor"),
        P("tensor", None),
        P(),
        P(),
        P("dp", "tensor", None),
    )
    return jax.shard_map(
        on_device,
        mesh=mesh,
        in_specs=placed,
        out_specs=(
            P("dp", "tensor", None),
            P("dp", "tensor", None),
            P(None, None, "tensor"),
            P("tensor", None),
            P(None, None, "tensor"),
            P("tensor", None),
            P(),
            P(),
        ),
        check_vma=False,
    )
```

```python
import functools
import math

import jax
import jax.numpy as jnp
from jax import lax
from jax.experimental import pallas as pl
from jax.experimental.pallas import tpu as pltpu
from jax.sharding import PartitionSpec as P

HEAD_DIM = 64
SEGS = 8
BLK = 256
F32 = jnp.float32
BF16 = jnp.bfloat16
MESH = pl.DeviceIdType.MESH
CHUNKS = 4
CHUNK = 128

epsilon = 1e-05
far_below = -1e30
log_base = math.log(1000.0)


def nn(a, b):
    return lax.dot_general(a, b, (((1,), (0,)), ((), ())), preferred_element_type=F32)


def nt(a, b):
    return lax.dot_general(a, b, (((1,), (1,)), ((), ())), preferred_element_type=F32)


def tn(a, b):
    return lax.dot_general(a, b, (((0,), (0,)), ((), ())), preferred_element_type=F32)


class Place:
    def __init__(self):
        p, z = lax.axis_index("dp"), lax.axis_index("tensor")
        self.p, self.z = p, z
        c, x, y = p % 2, (p // 2) % 2, (p // 4) % 2
        self.c, self.x, self.y = c, x, y
        self.place = p % 8
        self.x_place = self.place + 2 - 4 * x
        self.y_place = self.place + 4 - 8 * y
        self.d_place = self.x_place + 4 - 8 * y
        self.z1_at, self.z2_at = z + 1 - 2 * (z % 2), (z + 2) % 4
        self.sib = {"dp": p + 1 - 2 * c}
        self.xn = {"dp": p + 2 - 4 * x}
        self.yn = {"dp": p + 4 - 8 * y}
        self.z1 = {"tensor": self.z1_at}
        self.z2 = {"tensor": self.z2_at}
        self.pair = {"dp": p + 1 - 2 * c, "tensor": self.z2_at}
        self.cross = c + z // 2 - 2 * c * (z // 2)
        self.slot = (z + 2 * self.cross) % 4
        self.slot1 = self.slot + 1 - 2 * (self.slot % 2)
        self.slot2 = (self.slot + 2) % 4
        self.slot3 = (self.slot1 + 2) % 4


def greet(partners):
    barrier = pltpu.get_barrier_semaphore()
    for partner in partners:
        pl.semaphore_signal(barrier, inc=1, device_id=partner, device_id_type=MESH)
    pl.semaphore_wait(barrier, len(partners))


class Links:
    def __init__(self, send, recv):
        self.send, self.recv, self.count, self.started = send, recv, 0, []

    def make(self, src, dst, to):
        i = self.count
        self.count += 1
        return pltpu.make_async_remote_copy(
            src_ref=src, dst_ref=dst, send_sem=self.send.at[i], recv_sem=self.recv.at[i], device_id=to, device_id_type=MESH
        )

    def start(self, src, dst, to):
        copy = self.make(src, dst, to)
        copy.start()
        self.started.append(copy)
        return copy

    def wait_sends(self):
        for copy in self.started:
            copy.wait_send()


class Spread:
    def __init__(self, me, links, view, src=None):
        self.me, self.links, self.view = me, links, view
        own = view(me.place, 0, 96)
        src = own if src is None else src
        self.from_x = links.start(src, own, me.xn)
        self.from_y = links.start(src, own, me.yn)
        self.from_sib = [links.start(src, own, me.sib)]

    def second(self):
        me, links, view = self.me, self.links, self.view
        self.from_x.wait_recv()
        part = view(me.x_place, 0, 48)
        self.low = links.start(part, part, me.yn)
        block = view(me.x_place, 0, 96)
        self.from_sib.append(links.start(block, block, me.sib))
        self.from_y.wait_recv()
        part = view(me.y_place, 48, 48)
        self.high = links.start(part, part, me.xn)
        block = view(me.y_place, 0, 96)
        self.from_sib.append(links.start(block, block, me.sib))

    def third(self):
        me, links, view = self.me, self.links, self.view
        self.low.wait_recv()
        self.high.wait_recv()
        block = view(me.d_place, 0, 96)
        self.from_sib.append(links.start(block, block, me.sib))

    def last(self):
        for copy in self.from_sib:
            copy.wait_recv()


class Corner(Spread):
    def __init__(self, me, links, view, own, from_x, from_y):
        self.me, self.links, self.view = me, links, view
        first, last = pl.ds(0, 48), pl.ds(48, 48)
        self.low = links.start(from_x.at[:, first], view(me.x_place, 0, 48), me.yn)
        self.high = links.start(from_y.at[:, last], view(me.y_place, 48, 48), me.xn)
        self.from_sib = [
            links.start(src, view(place, 0, 96), me.sib)
            for src, place in ((own, me.place), (from_x, me.x_place), (from_y, me.y_place))
        ]


def view_2d(ref):
    return lambda place, first, size: ref.at[pl.ds(pl.multiple_of(place * 96 + first, 16), size)]


def view_3d(ref):
    return lambda place, first, size: ref.at[:, pl.ds(pl.multiple_of(place * 96 + first, 16), size)]


def start_kernel(x, wo, fb, tok, wx, wf0, zb, token_send, token_recv, send, recv, local):
    me = Place()
    c, z = me.c, me.z
    away = z + c * (3 - 2 * z)

    barrier = pltpu.get_barrier_semaphore()
    partners = (me.sib, me.xn, me.yn, me.z1, me.z2)
    for partner in partners:
        pl.semaphore_signal(barrier, inc=1, device_id=partner, device_id_type=MESH)
    @pl.when(z % 3 != 0)
    def _():
        pl.semaphore_signal(barrier, inc=1, device_id={"tensor": 3 - z}, device_id_type=MESH)

    pl.semaphore_wait(barrier, len(partners) + z * (3 - z) // 2)

    def line(k):
        return k + c * (3 - 2 * k)

    def line_sib(k):
        return k + (1 - c) * (3 - 2 * k)

    far, near = {"tensor": line(0)}, {"tensor": line(1)}

    def part(ch):
        return pl.ds(ch * CHUNK, CHUNK)

    def copy(kind, k, ch, src, to):
        return pltpu.make_async_remote_copy(
            src_ref=src, dst_ref=tok.at[line(k), part(ch)],
            send_sem=token_send.at[kind, k, ch],
            recv_sem=token_recv.at[k, ch], device_id=to, device_id_type=MESH,
        )

    def own(ch):
        return x.at[part(ch)]

    def held(k, ch):
        return tok.at[line(k), part(ch)]

    for k, to in ((0, near), (1, far), (2, near), (3, near)):

        @pl.when(away == k)
        def _(k=k, to=to):
            for ch in range(CHUNKS):
                copy(0, k, ch, own(ch), to).start()
                if k < 2:
                    copy(1, k, ch, own(ch), me.sib).start()

    links = Links(send, recv)
    attn_z = links.start(view_2d(wo)(me.place, 0, 96), view_2d(wx)(me.place, 0, 96), me.z2)
    ff_z = links.make(fb, zb.at[1], me.z2)
    ff0 = Spread(me, links, view_3d(wf0), fb)
    here = [
        pltpu.make_async_copy(fb, view_3d(wf0)(me.place, 0, 96), local.at[0]),
        pltpu.make_async_copy(fb, zb.at[0], local.at[1]),
    ]
    for h in here:
        h.start()

    @pl.when(away < 2)
    def _():
        mine = pltpu.make_async_copy(x, tok.at[z], local.at[2])
        mine.start()
        mine.wait()

    def forward(ch):
        @pl.when(away == 0)
        def _():
            for k in (1, 2, 3):
                copy(1, k, ch, held(k, ch), me.sib).wait_recv()
                copy(1, k, ch, held(k, ch), me.sib).start()

        @pl.when(away == 1)
        def _():
            for k in (2, 3, 0):
                copy(1, k, ch, held(k, ch), me.sib).wait_recv()
                if k:
                    copy(0, k, ch, held(k, ch), far).start()
                copy(1, k, ch, held(k, ch), me.sib).start()

    attn_z.wait_recv()
    attn = Spread(me, links, view_2d(wx))
    forward(0)
    ff0.second()
    forward(1)
    attn.second()
    ff0.third()
    forward(2)

    for k in (2, 3):

        @pl.when(away == k)
        def _(k=k):
            copy(0, k, 2, own(2), near).wait_send()

    ff_z.start()
    links.started.append(ff_z)
    attn.third()
    forward(3)

    @pl.when(away >= 2)
    def _():
        for ch in range(CHUNKS):
            for k in range(4):
                pltpu.make_async_remote_copy(
                    src_ref=own(ch), dst_ref=tok.at[line_sib(k), part(ch)], send_sem=token_send.at[0, k, ch],
                    recv_sem=token_recv.at[k, ch], device_id=me.sib, device_id_type=MESH,
                ).wait_recv()

    for spread in (attn, ff0):
        spread.last()
    ff_z.wait_recv()
    for h in here:
        h.wait()
    links.wait_sends()
    for k, to in ((0, near), (1, far), (2, near), (3, near)):

        @pl.when(away == k)
        def _(k=k, to=to):
            for ch in range(CHUNKS):
                if k < 2 or ch != 2:
                    copy(0, k, ch, own(ch), to).wait_send()
                if k == 1:
                    for j in (2, 3):
                        copy(0, j, ch, held(j, ch), to).wait_send()
                if k < 2:
                    for j in range(4):
                        copy(1, j, ch, own(ch) if j == k else held(j, ch), me.sib).wait_send()


FIRST, LAST = 256, 512


def list_pairs(sc, pairs):
    idle = 8 * 16 + 8
    pairs[0] = idle

    def of_query(i, n):
        lo, hi = sc[8 + i], sc[16 + i]

        def of_key(j, n):
            first = jnp.where(j == lo, FIRST, 0)
            last = jnp.where(j == hi - 1, LAST, 0)
            pairs[n] = i * 16 + j + first + last
            return n + 1

        return lax.fori_loop(lo, hi, of_key, n)

    n = lax.fori_loop(0, 2048 // BLK, of_query, 1)
    for more in range(3):
        pairs[n + more] = idle
    return n - 1


def split_pair(code):
    return (code // 16) % 16, code % 16


def columns(block):
    return pl.ds(pl.multiple_of(block * BLK, BLK), BLK)


def real(block):
    return jnp.where(block == 8, 0, block)


def attend_forward_kernel(
    sc, tok, cos, sin, seg, own, other, w, qa, ka, kt, vn, ot, logsum, part, va, mx, acc, s0, s1, p0, p1, al0, al1, pairs, sem
):
    heads = 3
    width = heads * HEAD_DIM

    @pl.when(sc[0] == 0)
    def _():
        copy = pltpu.make_async_copy(own, w, sem.at[0])
        copy.start()
        copy.wait()

    @pl.when(sc[0] == 1)
    def _():
        copy = pltpu.make_async_copy(other, w, sem.at[0])
        copy.start()
        copy.wait()

    def project(e, _):
        at = pl.ds(pl.multiple_of(e * 512, 512), 512)
        made = nt(w[: 3 * width], tok[e])
        c, s = cos[:, at], sin[:, at]
        hot = (seg[:, at] == lax.broadcasted_iota(jnp.int32, (SEGS, 512), 0)).astype(F32)
        rest = jnp.zeros((64 - SEGS, 512), F32)
        one_row = (lax.broadcasted_iota(jnp.int32, (16, 512), 0) == 0).astype(F32)
        for h in range(heads):
            r = h * HEAD_DIM
            a1, a2 = made[r : r + 32], made[r + 32 : r + 64]
            q = jnp.concatenate([a1 * c - a2 * s, a2 * c + a1 * s], axis=0).astype(BF16).astype(F32)
            qa[h, :, at] = jnp.concatenate([q * 0.125, hot, rest], axis=0).astype(BF16)
            r += width
            a1, a2 = made[r : r + 32], made[r + 32 : r + 64]
            k = jnp.concatenate([a1 * c - a2 * s, a2 * c + a1 * s], axis=0)
            kt[h * HEAD_DIM : (h + 1) * HEAD_DIM, at] = k.astype(BF16)
            ka[h, at, :] = jnp.concatenate([k, (1.0 - hot) * far_below, rest], axis=0).T.astype(BF16)
            r += width
            v = made[r : r + 64]
            va[h, :, at] = jnp.concatenate([v, one_row], axis=0).astype(BF16)
            vn[h, at, :] = jnp.concatenate([v, jnp.zeros_like(v)], axis=0).T[:, :HEAD_DIM].astype(BF16)
        return 0

    lax.fori_loop(0, 4, project, 0)

    count = list_pairs(sc, pairs)

    def score(t, s):
        i, j = split_pair(pairs[t])
        at, here = columns(real(i)), columns(real(j))
        for h in range(heads):
            s[h] = nn(ka[h, here, :], qa[h, :, at])

    def weigh(t, s, p, al):
        fresh = pairs[t] & FIRST
        for h in range(heads):
            scores = s[h]
            before = jnp.where(fresh > 0, -3e38, mx[h])
            largest = jnp.maximum(before, jnp.max(scores, axis=0, keepdims=True))
            p[h] = jnp.exp(scores - largest).astype(BF16)
            al[h] = jnp.exp(before - largest)
            mx[h] = largest

    def gather(t, p, al):
        code = pairs[t]
        i, j = split_pair(code)
        here = columns(real(j))
        for h in range(heads):
            acc[h] = acc[h] * al[h] + nn(va[h, :, here], p[h])

        @pl.when((code & LAST) > 0)
        def _():
            at = columns(i)
            for h in range(heads):
                total = acc[h, 64:65, :]
                ot[h * HEAD_DIM : (h + 1) * HEAD_DIM, at] = (acc[h, :64, :] / total).astype(BF16)
                logsum[pl.ds(h, 1), at] = mx[h] + jnp.log(total)

    def step(u, _):
        t = 2 * u + 1
        gather(t - 1, p1, al1)
        weigh(t, s0, p0, al0)
        score(t + 1, s1)
        gather(t, p0, al0)
        weigh(t + 1, s1, p1, al1)
        score(t + 2, s0)
        return 0

    acc[...] = jnp.zeros_like(acc)
    p1[...] = jnp.zeros_like(p1)
    al1[...] = jnp.zeros_like(al1)
    score(1, s0)
    lax.fori_loop(0, (count + 2) // 2, step, 0)
    for e in range(4):
        part[e] = tn(ot[:, e * 512 : (e + 1) * 512], w[3 * width :]).astype(BF16)


def attend_backward_kernel(
    sc, gb, tok, w, qa, ka, kt, vn, ot, logsum, cos, sin, grads, part, dot_, inner, dq, dk, dv, gp, s0, s1, r0, r1, p0, p1, d0, d1, pairs
):
    heads = 3
    width = heads * HEAD_DIM

    def begin(e, _):
        at = pl.ds(pl.multiple_of(e * 512, 512), 512)
        made = nt(w[3 * width :], gb[e]).astype(BF16)
        dot_[:, at] = made
        product = made.astype(F32) * ot[:, at].astype(F32)
        for h in range(heads):
            inner[pl.ds(h, 1), at] = jnp.sum(product[h * HEAD_DIM : (h + 1) * HEAD_DIM], axis=0, keepdims=True)
        return 0

    lax.fori_loop(0, 4, begin, 0)
    for total in (dq, dk, dv, p1, d1):
        total[...] = jnp.zeros_like(total)
    count = list_pairs(sc, pairs)

    def score(t, s, r):
        i, j = split_pair(pairs[t])
        at, here = columns(real(i)), columns(real(j))
        for h in range(heads):
            rows = slice(h * HEAD_DIM, (h + 1) * HEAD_DIM)
            s[h] = nn(ka[h, here, :], qa[h, :, at])
            r[h] = nn(vn[h, here, :], dot_[rows, at])

    def weigh(t, s, r, p, d):
        at = columns(real(split_pair(pairs[t])[0]))
        for h in range(heads):
            probability = jnp.exp(s[h] - logsum[pl.ds(h, 1), at])
            p[h] = probability.astype(BF16)
            d[h] = (probability * (r[h] - inner[pl.ds(h, 1), at])).astype(BF16)

    def gather(t, p, d):
        i, j = split_pair(pairs[t])
        at, here = columns(real(i)), columns(real(j))
        to_query, to_key = columns(i), columns(j)
        for h in range(heads):
            rows = slice(h * HEAD_DIM, (h + 1) * HEAD_DIM)
            dv[rows, to_key] += nt(dot_[rows, at], p[h])
            dk[rows, to_key] += nt(qa[h, :HEAD_DIM, at], d[h])
            dq[rows, to_query] += nn(kt[rows, here], d[h])

    def step(u, _):
        t = 2 * u + 1
        gather(t - 1, p1, d1)
        weigh(t, s0, r0, p0, d0)
        score(t + 1, s1, r1)
        gather(t, p0, d0)
        weigh(t + 1, s1, r1, p1, d1)
        score(t + 2, s0, r0)
        return 0

    score(1, s0, r0)
    lax.fori_loop(0, (count + 2) // 2, step, 0)

    def turn(e, _):
        at = pl.ds(pl.multiple_of(e * 512, 512), 512)
        c, s = cos[:, at], sin[:, at]
        for h in range(heads):
            r = h * HEAD_DIM
            for first, total, scale in ((0, dq, 0.125), (width, dk, 1.0)):
                d1_, d2_ = total[r : r + 32, at] * scale, total[r + 32 : r + 64, at] * scale
                gp[first + r : first + r + 64, at] = jnp.concatenate(
                    [d1_ * c + d2_ * s, d2_ * c - d1_ * s], axis=0
                ).astype(BF16)
        gp[2 * width :, at] = dv[:, at].astype(BF16)
        return 0

    lax.fori_loop(0, 4, turn, 0)
    for e in range(4):
        part[e] = tn(gp[:, e * 512 : (e + 1) * 512], w[: 3 * width]).astype(BF16)
    for block in range(4):
        if block < 3:
            rows = slice(block * width, (block + 1) * width)
            made = sum(nn(gp[rows, e * 512 : (e + 1) * 512], tok[e]) for e in range(4))
        else:
            made = sum(nn(ot[:, e * 512 : (e + 1) * 512], gb[e]) for e in range(4))
        grads[block * width : (block + 1) * width] = made.astype(BF16)


def row_mean(v):
    return jnp.mean(v, axis=-1, keepdims=True)


def norm_forward(summed):
    centred = summed - row_mean(summed)
    inverse = lax.rsqrt(row_mean(centred * centred) + epsilon)
    return centred * inverse, inverse


def norm_backward(scaled, normalized, inverse):
    return inverse * (scaled - row_mean(scaled) - normalized * row_mean(scaled * normalized))


def feed_forward_kernel(
    tok, part, cot_in, gain, bias, wf0, zb, zx, zy, zc,
    out, gz1, gb, sums, keep_a, keep_b, send_a, send_b, zs_out,
    w, slope_g, slope_u, hid, nb, nbt, gm, gmt, total, norm1, inv1, dw, lw, xs, cot, from_core, from_z, to_z,
    f1a, f1b, f2a, f2b, send, recv, local, out_sem, trade_sem,
):
    me = Place()
    greet((me.sib, me.xn, me.yn, me.z1, me.pair))
    links = Links(send, recv)
    loads = [
        pltpu.make_async_copy(tok.at[me.slot], xs, local.at[0]),
        pltpu.make_async_copy(wf0, w.at[0], local.at[1]),
        pltpu.make_async_copy(zb.at[1], view_3d(w.at[2])(me.place, 0, 96), local.at[2]),
        pltpu.make_async_copy(zc.at[0], view_3d(w.at[1])(me.place, 0, 96), local.at[3]),
        pltpu.make_async_copy(zc.at[1], view_3d(w.at[3])(me.place, 0, 96), local.at[4]),
        pltpu.make_async_copy(zx, view_3d(w.at[2])(me.x_place, 0, 96), local.at[5]),
        pltpu.make_async_copy(zy, view_3d(w.at[2])(me.y_place, 0, 96), local.at[6]),
    ]

    def cot_here():
        return pltpu.make_async_copy(cot_in, cot, local.at[7])

    def cot_there():
        return pltpu.make_async_remote_copy(
            src_ref=cot_in, dst_ref=cot, send_sem=trade_sem.at[0], recv_sem=trade_sem.at[1], device_id=me.pair,
            device_id_type=MESH,
        )

    def rows(ch):
        return pl.ds(ch * CHUNK, CHUNK)

    cores = [
        [links.start(part.at[shard, rows(ch)], from_core.at[i, rows(ch)], me.sib) for ch in range(CHUNKS)]
        for i, shard in ((1, me.slot3), (0, me.slot2))
    ]
    ff2 = Corner(me, links, view_3d(w.at[2]), zb.at[1], zx, zy)
    ff1 = Spread(me, links, view_3d(w.at[1]), zc.at[0])
    ff3 = Spread(me, links, view_3d(w.at[3]), zc.at[1])
    for load in loads:
        load.start()
    zs = []
    for ch in range(CHUNKS):
        cores[0][ch].wait_recv()
        at = rows(ch)
        to_z[at] = (part[me.slot1, at].astype(F32) + from_core[1, at].astype(F32)).astype(BF16)
        zs.append(links.start(to_z.at[at], from_z.at[at], me.z1))

    @pl.when(me.cross == 0)
    def _():
        cot_here().start()

    @pl.when(me.cross == 1)
    def _():
        cot_there().start()

    ff2.third()
    ff1.second()
    loads[0].wait()
    for ch in range(CHUNKS):
        if ch == CHUNKS - 1:
            ff3.second()
        cores[1][ch].wait_recv()
        zs[ch].wait_recv()
        at = rows(ch)
        branch = part[me.slot, at].astype(F32) + from_core[0, at].astype(F32) + from_z[at].astype(F32)
        n1, i1 = norm_forward(xs[at].astype(F32) + branch)
        norm1[at] = n1
        inv1[at] = jnp.broadcast_to(i1, (CHUNK, 128))
        normed = n1 * gain[0:1, :] + bias[0:1, :]
        total[at] = normed
        nb[at] = normed.astype(BF16)
        nbt[:, ch * CHUNK : (ch + 1) * CHUNK] = normed.T.astype(BF16)
    ff1.third()

    def forward(ez):
        gate = nn(nb[...], w[ez, 0])
        up = nn(nb[...], w[ez, 1])
        sig = 1.0 / (1.0 + jnp.exp(-gate))
        active = gate * sig
        low = (active * up).astype(BF16)
        hid[ez] = low
        slope_u[ez] = active.astype(BF16)
        slope_g[ez] = (up * sig * (1.0 + gate * (1.0 - sig))).astype(BF16)
        total[...] += nn(low, w[ez, 2])

    loads[1].wait()
    forward(0)
    ff3.third()
    for load in (loads[2], loads[5], loads[6]):
        load.wait()
    ff2.last()
    forward(2)
    loads[3].wait()
    ff1.last()
    forward(1)
    loads[4].wait()
    ff3.last()
    forward(3)
    n2, i2 = norm_forward(total[...])
    out[...] = (n2 * gain[1:2, :] + bias[1:2, :]).astype(BF16)

    @pl.when(me.cross == 0)
    def _():
        cot_here().wait()

    @pl.when(me.cross == 1)
    def _():
        cot_there().wait()

    g = cot[...].astype(F32)
    sums[1:2, :] = jnp.sum(g * n2, axis=0, keepdims=True)
    sums[3:4, :] = jnp.sum(g, axis=0, keepdims=True)
    gz2 = norm_backward(g * gain[1:2, :], n2, i2)
    total[...] = gz2
    gm[...] = gz2.astype(BF16)
    gmt[...] = gz2.T.astype(BF16)

    def block(quad, core):
        return pl.ds(pl.multiple_of((quad * 2 + core) * 96, 32), 96)

    order = (1, 3, 0, 2)
    halves = []
    first, last = pl.ds(0, 48), pl.ds(48, 48)

    def slopes(ez):
        grad_hidden = nt(gm[...], w[ez, 2])
        gate = (grad_hidden * slope_g[ez].astype(F32)).astype(BF16)
        up = (grad_hidden * slope_u[ez].astype(F32)).astype(BF16)
        slope_g[ez] = gate
        slope_u[ez] = up
        total[...] += nt(gate, w[ez, 0]) + nt(up, w[ez, 1])

    def weights(n):
        i, ez = n % 2, order[n]
        if n >= 2:
            for copy in halves[n - 2]:
                copy.wait_send()
        dw[i, 2] = nn(gmt[...], hid[ez]).astype(BF16)
        dw[i, 0] = nn(nbt[...], slope_g[ez]).astype(BF16)
        dw[i, 1] = nn(nbt[...], slope_u[ez]).astype(BF16)
        halves.append([links.make(dw.at[i, :, block(quad, 1 - me.c)], lw.at[n, quad], me.sib) for quad in range(4)])
        for copy in halves[n]:
            copy.start()

    def settle(n):
        for quad in range(4):
            halves[n][quad].wait_recv()
            for m in range(3):
                lw[n, quad, m] = (lw[n, quad, m].astype(F32) + dw[n % 2, m, block(quad, me.c)].astype(F32)).astype(BF16)

    plane_1, plane_2 = {}, {}

    def plane_first(n):
        plane_1[n] = [
            (
                links.start(lw.at[n, (1 - me.y) * 2 + o, :, first], f1a.at[n, o], me.yn),
                links.start(lw.at[n, o * 2 + 1 - me.x, :, last], f1b.at[n, o], me.xn),
            )
            for o in range(2)
        ]

    def plane_second(n):
        for o in range(2):
            plane_1[n][o][0].wait_recv()
            f1a[n, o] = (f1a[n, o].astype(F32) + lw[n, me.y * 2 + o, :, first].astype(F32)).astype(BF16)
            plane_1[n][o][1].wait_recv()
            f1b[n, o] = (f1b[n, o].astype(F32) + lw[n, o * 2 + me.x, :, last].astype(F32)).astype(BF16)
        plane_2[n] = (
            links.start(f1a.at[n, 1 - me.x], f2a.at[n], me.xn),
            links.start(f1b.at[n, 1 - me.y], f2b.at[n], me.yn),
        )

    def plane_last(n):
        plane_2[n][0].wait_recv()
        zs_out[n, 0] = (f1a[n, me.x].astype(F32) + f2a[n].astype(F32)).astype(BF16)
        plane_2[n][1].wait_recv()
        zs_out[n, 1] = (f1b[n, me.y].astype(F32) + f2b[n].astype(F32)).astype(BF16)

    def stores(n):
        made = []
        for oy in range(2):
            for ox in range(2):
                src = lw.at[n, oy * 2 + ox]
                made.append((me.y == oy, src.at[:, first], keep_a.at[n - 2, ox], send_a.at[n - 2, ox]))
                made.append((me.x == ox, src.at[:, last], keep_b.at[n - 2, oy], send_b.at[n - 2, oy]))
        return made

    def store(n):
        for number, (here, src, kept, sent) in enumerate(stores(n)):

            @pl.when(here)
            def _(number=number, src=src, kept=kept):
                pltpu.make_async_copy(src, kept, out_sem.at[n - 2, number]).start()

            @pl.when(jnp.logical_not(here))
            def _(number=number, src=src, sent=sent):
                pltpu.make_async_copy(src, sent, out_sem.at[n - 2, number]).start()

    slopes(1)
    weights(0)
    slopes(3)
    settle(0)
    plane_first(0)
    weights(1)
    slopes(0)
    settle(1)
    plane_first(1)
    slopes(2)
    g = total[...]
    sums[0:1, :] = jnp.sum(g * norm1[...], axis=0, keepdims=True)
    sums[2:3, :] = jnp.sum(g, axis=0, keepdims=True)
    sums[4:8, :] = jnp.zeros((4, 768), F32)
    to_pair, to_core, on_core = [], [], []
    for ch in range(CHUNKS):
        at = rows(ch)
        made = norm_backward(total[at] * gain[0:1, :], norm1[at], inv1[at, 0:1])
        gz1[at] = made
        gb[me.slot, at] = made.astype(BF16)
        mine = gb.at[me.slot, at]
        to_pair.append(links.start(mine, mine, me.z1))
        to_core.append(links.start(mine, mine, me.sib))
    weights(2)
    plane_second(0)
    weights(3)
    settle(2)
    store(2)
    plane_second(1)
    settle(3)
    store(3)
    for ch in range(CHUNKS):
        to_pair[ch].wait_recv()
        other = gb.at[me.slot1, rows(ch)]
        on_core.append(links.start(other, other, me.sib))
    plane_last(0)
    plane_last(1)
    for copy in to_core + on_core:
        copy.wait_recv()
    for n in (2, 3):
        for number, (_, src, kept, _) in enumerate(stores(n)):
            pltpu.make_async_copy(src, kept, out_sem.at[n - 2, number]).wait()
        for copy in halves[n]:
            copy.wait_send()
    links.wait_sends()


def finish_kernel(
    extra, keep_a, keep_b, recv_a, recv_b, zr, ga, part, gz1, sums_in,
    g_ff, g_attn, g_tok, sums,
    sa, sb, f2a, f2b, va, f4, fe, a_in, a_mid, a_out, a_fin, a_two, ae, from_core, from_z, to_z, trade_out, trade_in, sum_in,
    send, recv, a_send, a_recv,
):
    me = Place()
    bits = [{"dp": me.p + bit - 2 * bit * ((me.p // bit) % 2)} for bit in extra]
    greet([me.sib, me.xn, me.yn, me.z1, me.z2, me.pair] + bits)
    links = Links(send, recv)

    def rows(ch):
        return pl.ds(ch * CHUNK, CHUNK)

    def add(*terms):
        return sum(t.astype(F32) for t in terms).astype(BF16)

    cores = [
        [links.start(part.at[shard, rows(ch)], from_core.at[i, rows(ch)], me.sib) for ch in range(CHUNKS)]
        for i, shard in ((1, me.slot3), (0, me.slot2))
    ]

    def half(oy, ox, h):
        return pl.ds(pl.multiple_of((oy * 2 + ox) * 192 + h * 96, 32), 96)

    attn_1 = []
    for o in range(2):
        attn_1.append(links.start(ga.at[half(1 - me.y, o, 0)], a_in.at[0, o], me.yn))
        attn_1.append(links.start(ga.at[half(o, 1 - me.x, 1)], a_in.at[1, o], me.xn))

    sums[...] = sums_in[...]
    around = [me.sib, me.xn, me.yn, me.z1, me.z2] + bits
    small = [links.start(sums, sum_in.at[0], around[0])]

    def small_step():
        n = len(small)
        small[-1].wait_recv()
        small[-1].wait_send()
        links.started = [copy for copy in links.started if copy is not small[n - 1]]
        sums[...] += sum_in[n - 1]
        if n < len(around):
            small.append(links.start(sums, sum_in.at[n], around[n]))

    ff_2 = {}

    def plane(ez):
        sa[ez] = add(keep_a[ez, 1 - me.x], recv_a[ez, 1 - me.x])
        sb[ez] = add(keep_b[ez, 1 - me.y], recv_b[ez, 1 - me.y])
        ff_2[ez] = (links.start(sa.at[ez], f2a.at[ez], me.xn), links.start(sb.at[ez], f2b.at[ez], me.yn))

    def planed(ez):
        ff_2[ez][0].wait_recv()
        va[ez, 0] = add(keep_a[ez, me.x], recv_a[ez, me.x], f2a[ez], zr[ez, 0])
        ff_2[ez][1].wait_recv()
        va[ez, 1] = add(keep_b[ez, me.y], recv_b[ez, me.y], f2b[ez], zr[ez, 1])

    plane(1)
    plane(0)
    zs = []
    for ch in range(CHUNKS):
        cores[0][ch].wait_recv()
        at = rows(ch)
        to_z[at] = add(part[me.slot1, at], from_core[1, at])
        zs.append(links.start(to_z.at[at], from_z.at[at], me.z1))
    small_step()
    planed(1)
    ff_4 = links.start(va.at[1], f4, me.z2)
    for copy in attn_1:
        copy.wait_recv()
    a_mid[0] = add(ga[half(me.y, 1 - me.x, 0)], a_in[0, 1 - me.x])
    a_mid[1] = add(ga[half(1 - me.y, me.x, 1)], a_in[1, 1 - me.y])
    attn_2 = [links.start(a_mid.at[0], a_out.at[0], me.xn), links.start(a_mid.at[1], a_out.at[1], me.yn)]
    planed(0)
    for copy in attn_2:
        copy.wait_recv()
    a_fin[:96] = add(ga[half(me.y, me.x, 0)], a_in[0, me.x], a_out[0])
    a_fin[96:] = add(ga[half(me.y, me.x, 1)], a_in[1, me.y], a_out[1])

    def attn_copy(n, src, dst, to):
        return pltpu.make_async_remote_copy(
            src_ref=src, dst_ref=dst, send_sem=a_send.at[n], recv_sem=a_recv.at[n], device_id=to, device_id_type=MESH
        )

    def quarter(oy, ox, first=0, size=192):
        return g_attn.at[pl.ds(pl.multiple_of((oy * 2 + ox) * 192 + first, 32), size)]

    def attn_over():
        return attn_copy(0, a_fin, a_two, me.z2)

    @pl.when(me.cross == 1)
    def _():
        attn_over().start()

    small_step()
    small_step()

    trades = [
        pltpu.make_async_remote_copy(
            src_ref=trade_out.at[rows(ch)], dst_ref=trade_in.at[rows(ch)], send_sem=a_send.at[8 + ch],
            recv_sem=a_recv.at[8 + ch], device_id=me.pair, device_id_type=MESH,
        )
        for ch in range(CHUNKS)
    ]
    for ch in range(CHUNKS):
        cores[1][ch].wait_recv()
        zs[ch].wait_recv()
        at = rows(ch)
        got = gz1[at] + (part[me.slot, at].astype(F32) + from_core[0, at].astype(F32) + from_z[at].astype(F32))

        @pl.when(me.cross == 0)
        def _(at=at, got=got):
            g_tok[at] = got

        @pl.when(me.cross == 1)
        def _(at=at, got=got, ch=ch):
            trade_out[at] = got.astype(BF16)

    mine = quarter(me.y, me.x)

    def attn_send(n, src, to):
        return attn_copy(n, src, src, to)

    block_x, block_y = quarter(me.y, 1 - me.x), quarter(1 - me.y, me.x)
    low_x, high_y = quarter(me.y, 1 - me.x, 0, 96), quarter(1 - me.y, me.x, 96, 96)
    corner = quarter(1 - me.y, 1 - me.x)

    @pl.when(me.cross == 0)
    def _():
        attn_over().wait_recv()
        total = add(a_fin[...], a_two[...])
        for n, bit in enumerate(bits):
            ae[n, 0] = total
            step = attn_copy(16 + n, ae.at[n, 0], ae.at[n, 1], bit)
            step.start()
            step.wait()
            total = add(total, ae[n, 1])
        g_attn[pl.ds(pl.multiple_of((me.y * 2 + me.x) * 192, 32), 192)] = total
        attn_send(1, mine, me.xn).start()
        attn_send(2, mine, me.yn).start()
        attn_send(3, mine, me.sib).start()

    ff_4.wait_recv()

    @pl.when(me.cross == 1)
    def _():
        for ch in range(CHUNKS):
            trades[ch].start()

    total = add(va[0], f4[...])
    for n, bit in enumerate(bits):
        fe[n, 0] = total
        step = links.start(fe.at[n, 0], fe.at[n, 1], bit)
        step.wait_recv()
        total = add(total, fe[n, 1])
    for h in range(2):
        g_ff[:, pl.ds(pl.multiple_of(me.place * 96 + h * 48, 16), 48)] = total[h]
    spread = Spread(me, links, view_3d(g_ff))
    while len(small) < len(around):
        small_step()
    small_step()

    @pl.when(me.cross == 0)
    def _():
        attn_send(1, block_x, me.xn).wait_recv()
        attn_send(4, low_x, me.yn).start()
        attn_send(5, block_x, me.sib).start()
        attn_send(2, block_y, me.yn).wait_recv()
        attn_send(6, high_y, me.xn).start()
        attn_send(7, block_y, me.sib).start()

    spread.second()

    @pl.when(me.cross == 0)
    def _():
        attn_send(4, low_x, me.yn).wait_recv()
        attn_send(6, high_y, me.xn).wait_recv()
        attn_send(12, corner, me.sib).start()
        for n, src, to in (
            (1, mine, me.xn), (2, mine, me.yn), (3, mine, me.sib), (4, low_x, me.yn), (5, block_x, me.sib),
            (6, high_y, me.xn), (7, block_y, me.sib), (12, corner, me.sib),
        ):
            attn_send(n, src, to).wait_send()

    @pl.when(me.cross == 1)
    def _():
        for ch in range(CHUNKS):
            trades[ch].wait_recv()
            g_tok[rows(ch)] = trade_in[rows(ch)].astype(F32)
        attn_over().wait_send()
        for n, src in ((3, mine), (5, block_x), (7, block_y), (12, corner)):
            attn_send(n, src, me.sib).wait_recv()
        for ch in range(CHUNKS):
            trades[ch].wait_send()

    spread.third()
    spread.last()
    links.wait_sends()


def widen_kernel(attn, out_rows, gate_up, down, g_qkv, g_out, g_gate_up, g_down):
    g_qkv[...] = attn[...].astype(F32)
    g_out[...] = out_rows[...].astype(F32)
    g_gate_up[:, 0, :] = gate_up[0].astype(F32)
    g_gate_up[:, 1, :] = gate_up[1].astype(F32)
    g_down[...] = down[0].astype(F32).T


def solution(mesh):
    dp, tensor = mesh.shape["dp"], mesh.shape["tensor"]
    assert tensor == 4 and dp >= 8 and dp & (dp - 1) == 0
    extra = [1 << b for b in range(3, dp.bit_length() - 1)]
    both = ("dp", "tensor")

    def cell(i, k):
        return i * tensor + k

    def over(x, bit):
        return lax.ppermute(x, "dp", [(i, i ^ bit) for i in range(dp)])

    away = [(i, k) for i in range(dp) for k in range(tensor) if (i & 1) != (k >> 1)]

    def trade(x):
        return lax.ppermute(x, both, [(cell(i, k), cell(i ^ 1, k ^ 2)) for i, k in away])

    smem = pl.BlockSpec(memory_space=pltpu.SMEM)
    vmem = pl.BlockSpec(memory_space=pltpu.VMEM)
    hbm = pl.BlockSpec(memory_space=pl.ANY)

    def shape(*dims, dtype=BF16):
        return jax.ShapeDtypeStruct(dims, dtype)

    def dma(*dims):
        return pltpu.SemaphoreType.DMA(dims)

    def params(mib, number=None):
        if number is None:
            return pltpu.CompilerParams(vmem_limit_bytes=mib << 20)
        return pltpu.CompilerParams(vmem_limit_bytes=mib << 20, collective_id=number, has_side_effects=True)

    def on_device(tokens, segments, w_qkv, w_out, w_gate_up, w_down, norm_gain, norm_bias, cotangent):
        p, z = lax.axis_index("dp"), lax.axis_index("tensor")
        swapped = (p & 1) != (z >> 1)
        place = p & 7

        own = jnp.concatenate([w_qkv.transpose(1, 2, 0).reshape(576, 768), w_out])
        rows = lax.dynamic_slice(w_gate_up, (place * 96, 0, 0), (96, 2, 768))
        block = jnp.stack([rows[:, 0], rows[:, 1], lax.dynamic_slice(w_down, (place * 96, 0), (96, 768))])

        tok, wx, wf0, zb = pl.pallas_call(
            start_kernel,
            name="start",
            out_shape=(
                shape(4, 512, 768), shape(768, 768), shape(3, 768, 768), shape(2, 3, 96, 768),
            ),
            in_specs=[hbm] * 3,
            out_specs=(hbm,) * 4,
            scratch_shapes=[dma(2, 4, CHUNKS), dma(4, CHUNKS), dma(40), dma(40), dma(4)],
            compiler_params=params(16, 0),
        )(tokens[0], own, block)

        row = jnp.where(swapped, over(segments, 1), segments)[0]
        length = row.shape[0]
        onehot = (row[None, :] == jnp.arange(SEGS, dtype=jnp.int32)[:, None]).astype(jnp.int32)
        counts = jnp.sum(onehot, axis=1)
        order = jnp.arange(SEGS, dtype=jnp.int32)
        starts = jnp.sum(jnp.where(order[None, :] < order[:, None], counts[None, :], 0), axis=1)
        first_place = jnp.sum(onehot * starts[:, None], axis=0)
        end_place = first_place + jnp.sum(onehot * counts[:, None], axis=0)
        lo = first_place.reshape(-1, BLK)[:, 0] // BLK
        hi = (end_place.reshape(-1, BLK)[:, -1] + (BLK - 1)) // BLK
        seg = row[None, :]
        places = (jnp.arange(length, dtype=jnp.int32) - first_place)[None, :].astype(F32)
        inverse = jnp.exp(-2.0 * jnp.arange(HEAD_DIM // 2, dtype=F32) / HEAD_DIM * log_base)
        angles = inverse[:, None] * places
        cos, sin = jnp.cos(angles), jnp.sin(angles)
        sc = jnp.concatenate([jnp.full((8,), swapped.astype(jnp.int32)), lo, hi]).astype(jnp.int32)

        zc = lax.ppermute(zb, "tensor", [(i, i ^ 1) for i in range(tensor)])
        zx, zy = over(zb[1], 2), over(zb[1], 4)

        w, qa, ka, kt, vn, ot, logsum, part = pl.pallas_call(
            attend_forward_kernel,
            name="attend_forward",
            out_shape=(
                shape(768, 768), shape(3, 128, length), shape(3, length, 128), shape(192, length),
                shape(3, length, 64), shape(192, length), shape(8, length, dtype=F32), shape(4, 512, 768),
            ),
            in_specs=[smem, vmem, vmem, vmem, vmem, hbm, hbm],
            out_specs=(vmem,) * 8,
            scratch_shapes=[
                pltpu.VMEM((3, 80, length), BF16),
                pltpu.VMEM((3, 1, BLK), F32),
                pltpu.VMEM((3, 80, BLK), F32),
                *[pltpu.VMEM((3, BLK, BLK), F32)] * 2,
                *[pltpu.VMEM((3, BLK, BLK), BF16)] * 2,
                *[pltpu.VMEM((3, 1, BLK), F32)] * 2,
                pltpu.SMEM((72,), jnp.int32),
                dma(1),
            ],
            compiler_params=params(48),
            cost_estimate=pl.CostEstimate(flops=20_000_000_000, bytes_accessed=24_000_000, transcendentals=6_000_000),
        )(sc, tok, cos, sin, seg, own, wx)

        out, gz1, gb, sums, keep_a, keep_b, send_a, send_b, zs = pl.pallas_call(
            feed_forward_kernel,
            name="feed_forward",
            out_shape=(
                shape(512, 768), shape(512, 768, dtype=F32), shape(4, 512, 768), shape(8, 768, dtype=F32),
                *(shape(2, 2, 3, 48, 768),) * 5,
            ),
            in_specs=[hbm, vmem, hbm, vmem, vmem] + [hbm] * 5,
            out_specs=(vmem,) * 4 + (hbm,) * 4 + (vmem,),
            scratch_shapes=[
                pltpu.VMEM((4, 3, 768, 768), BF16),
                pltpu.VMEM((4, 512, 768), BF16),
                pltpu.VMEM((4, 512, 768), BF16),
                pltpu.VMEM((4, 512, 768), BF16),
                pltpu.VMEM((512, 768), BF16),
                pltpu.VMEM((768, 512), BF16),
                pltpu.VMEM((512, 768), BF16),
                pltpu.VMEM((768, 512), BF16),
                pltpu.VMEM((512, 768), F32),
                pltpu.VMEM((512, 768), F32),
                pltpu.VMEM((512, 128), F32),
                pltpu.VMEM((2, 3, 768, 768), BF16),
                pltpu.VMEM((4, 4, 3, 96, 768), BF16),
                pltpu.VMEM((512, 768), BF16),
                pltpu.VMEM((512, 768), BF16),
                pltpu.VMEM((2, 512, 768), BF16),
                pltpu.VMEM((512, 768), BF16),
                pltpu.VMEM((512, 768), BF16),
                pltpu.VMEM((2, 2, 3, 48, 768), BF16),
                pltpu.VMEM((2, 2, 3, 48, 768), BF16),
                pltpu.VMEM((2, 3, 48, 768), BF16),
                pltpu.VMEM((2, 3, 48, 768), BF16),
                dma(80), dma(80), dma(8), dma(2, 8), dma(2),
            ],
            compiler_params=params(62, 1),
            cost_estimate=pl.CostEstimate(flops=22_000_000_000, bytes_accessed=36_000_000, transcendentals=3_000_000),
        )(tok, part, cotangent[0], norm_gain, norm_bias, wf0, zb, zx, zy, zc)

        recv_a, recv_b = over(send_a, 4), over(send_b, 2)
        zr = lax.ppermute(zs, "tensor", [(i, i ^ 1) for i in range(tensor)])
        output = jnp.where(swapped, trade(out), out)[None]

        grads, part = pl.pallas_call(
            attend_backward_kernel,
            name="attend_backward",
            out_shape=(shape(768, 768), shape(4, 512, 768)),
            in_specs=[smem] + [vmem] * 11,
            out_specs=(vmem,) * 2,
            scratch_shapes=[
                pltpu.VMEM((192, length), BF16),
                pltpu.VMEM((8, length), F32),
                *[pltpu.VMEM((192, length + BLK), F32)] * 3,
                pltpu.VMEM((576, length), BF16),
                *[pltpu.VMEM((3, BLK, BLK), F32)] * 4,
                *[pltpu.VMEM((3, BLK, BLK), BF16)] * 4,
                pltpu.SMEM((72,), jnp.int32),
            ],
            compiler_params=params(48),
            cost_estimate=pl.CostEstimate(flops=40_000_000_000, bytes_accessed=24_000_000, transcendentals=6_000_000),
        )(sc, gb, tok, w, qa, ka, kt, vn, ot, logsum, cos, sin)

        spare = max(len(extra), 1)
        half = (48, 768)
        g_ff, g_attn, g_tok, sums = pl.pallas_call(
            functools.partial(finish_kernel, extra),
            name="finish",
            out_shape=(shape(3, 768, 768), shape(768, 768), shape(512, 768, dtype=F32), shape(8, 768, dtype=F32)),
            in_specs=[vmem] * 9,
            out_specs=(vmem,) * 4,
            scratch_shapes=[
                *[pltpu.VMEM((2, 3, *half), BF16)] * 4,
                pltpu.VMEM((2, 2, 3, *half), BF16),
                pltpu.VMEM((2, 3, *half), BF16),
                pltpu.VMEM((spare, 2, 2, 3, *half), BF16),
                pltpu.VMEM((2, 2, 96, 768), BF16),
                pltpu.VMEM((2, 96, 768), BF16),
                pltpu.VMEM((2, 96, 768), BF16),
                pltpu.VMEM((192, 768), BF16),
                pltpu.VMEM((192, 768), BF16),
                pltpu.VMEM((spare, 2, 192, 768), BF16),
                pltpu.VMEM((2, 512, 768), BF16),
                pltpu.VMEM((512, 768), BF16),
                pltpu.VMEM((512, 768), BF16),
                pltpu.VMEM((512, 768), BF16),
                pltpu.VMEM((512, 768), BF16),
                pltpu.VMEM((5 + spare, 8, 768), F32),
                dma(64), dma(64), dma(16 + spare), dma(16 + spare),
            ],
            compiler_params=params(48, 2),
        )(keep_a, keep_b, recv_a, recv_b, zr, grads, part, gz1, sums)

        g_qkv, g_out, g_gate_up, g_down = pl.pallas_call(
            widen_kernel,
            name="widen",
            grid=(3,),
            out_shape=(
                shape(576, 768, dtype=F32), shape(192, 768, dtype=F32), shape(768, 2, 768, dtype=F32),
                shape(768, 768, dtype=F32),
            ),
            in_specs=[
                pl.BlockSpec((192, 768), lambda i: (i, 0)),
                pl.BlockSpec((64, 768), lambda i: (9 + i, 0)),
                pl.BlockSpec((2, 256, 768), lambda i: (0, i, 0)),
                pl.BlockSpec((1, 768, 256), lambda i: (2, 0, i)),
            ],
            out_specs=(
                pl.BlockSpec((192, 768), lambda i: (i, 0)),
                pl.BlockSpec((64, 768), lambda i: (i, 0)),
                pl.BlockSpec((256, 2, 768), lambda i: (i, 0, 0)),
                pl.BlockSpec((256, 768), lambda i: (i, 0)),
            ),
            compiler_params=params(32),
            cost_estimate=pl.CostEstimate(flops=0, bytes_accessed=16_000_000, transcendentals=0),
        )(g_attn, g_attn, g_ff, g_ff)
        return (
            output, g_tok[None], g_qkv.reshape(3, 192, 768).transpose(2, 0, 1), g_out, g_gate_up, g_down,
            sums[0:2], sums[2:4],
        )

    placed = (
        P("dp", "tensor", None),
        P("dp", None),
        P(None, None, "tensor"),
        P("tensor", None),
        P(None, None, "tensor"),
        P("tensor", None),
        P(),
        P(),
        P("dp", "tensor", None),
    )
    return jax.shard_map(
        on_device,
        mesh=mesh,
        in_specs=placed,
        out_specs=(
            P("dp", "tensor", None),
            P("dp", "tensor", None),
            P(None, None, "tensor"),
            P("tensor", None),
            P(None, None, "tensor"),
            P("tensor", None),
            P(),
            P(),
        ),
        check_vma=False,
    )
```

```python
import functools
import math

import jax
import jax.numpy as jnp
import numpy as np
from jax import lax
from jax.experimental import pallas as pl
from jax.experimental.pallas import tpu as pltpu
from jax.sharding import PartitionSpec as P

HEAD_DIM = 64
SEGS = 8
BLK = 256
F32 = jnp.float32
BF16 = jnp.bfloat16
MESH = pl.DeviceIdType.MESH
CHUNKS = 4
CHUNK = 128

epsilon = 1e-05
far_below = -1e30
log_base = math.log(1000.0)


def nn(a, b):
    return lax.dot_general(a, b, (((1,), (0,)), ((), ())), preferred_element_type=F32)


def nt(a, b):
    return lax.dot_general(a, b, (((1,), (1,)), ((), ())), preferred_element_type=F32)


def tn(a, b):
    return lax.dot_general(a, b, (((0,), (0,)), ((), ())), preferred_element_type=F32)


class Place:
    def __init__(self):
        p, z = lax.axis_index("dp"), lax.axis_index("tensor")
        self.p, self.z = p, z
        c, x, y = p % 2, (p // 2) % 2, (p // 4) % 2
        self.c, self.x, self.y = c, x, y
        self.place = p % 8
        self.x_place = self.place + 2 - 4 * x
        self.y_place = self.place + 4 - 8 * y
        self.d_place = self.x_place + 4 - 8 * y
        self.z1_at, self.z2_at = z + 1 - 2 * (z % 2), (z + 2) % 4
        self.sib = {"dp": p + 1 - 2 * c}
        self.xn = {"dp": p + 2 - 4 * x}
        self.yn = {"dp": p + 4 - 8 * y}
        self.z1 = {"tensor": self.z1_at}
        self.z2 = {"tensor": self.z2_at}
        self.pair = {"dp": p + 1 - 2 * c, "tensor": self.z2_at}
        self.cross = c + z // 2 - 2 * c * (z // 2)
        self.slot = (z + 2 * self.cross) % 4
        self.slot1 = self.slot + 1 - 2 * (self.slot % 2)
        self.slot2 = (self.slot + 2) % 4
        self.slot3 = (self.slot1 + 2) % 4


def greet(partners):
    barrier = pltpu.get_barrier_semaphore()
    for partner in partners:
        pl.semaphore_signal(barrier, inc=1, device_id=partner, device_id_type=MESH)
    pl.semaphore_wait(barrier, len(partners))


class Links:
    def __init__(self, send, recv):
        self.send, self.recv, self.count, self.started = send, recv, 0, []

    def make(self, src, dst, to):
        i = self.count
        self.count += 1
        return pltpu.make_async_remote_copy(
            src_ref=src, dst_ref=dst, send_sem=self.send.at[i], recv_sem=self.recv.at[i], device_id=to, device_id_type=MESH
        )

    def start(self, src, dst, to):
        copy = self.make(src, dst, to)
        copy.start()
        self.started.append(copy)
        return copy

    def wait_sends(self):
        for copy in self.started:
            copy.wait_send()


class Spread:
    def __init__(self, me, links, view, src=None):
        self.me, self.links, self.view = me, links, view
        own = view(me.place, 0, 96)
        src = own if src is None else src
        self.from_x = links.start(src, own, me.xn)
        self.from_y = links.start(src, own, me.yn)
        self.from_sib = [links.start(src, own, me.sib)]

    def second(self):
        me, links, view = self.me, self.links, self.view
        self.from_x.wait_recv()
        part = view(me.x_place, 0, 48)
        self.low = links.start(part, part, me.yn)
        block = view(me.x_place, 0, 96)
        self.from_sib.append(links.start(block, block, me.sib))
        self.from_y.wait_recv()
        part = view(me.y_place, 48, 48)
        self.high = links.start(part, part, me.xn)
        block = view(me.y_place, 0, 96)
        self.from_sib.append(links.start(block, block, me.sib))

    def third(self):
        me, links, view = self.me, self.links, self.view
        self.low.wait_recv()
        self.high.wait_recv()
        block = view(me.d_place, 0, 96)
        self.from_sib.append(links.start(block, block, me.sib))

    def last(self):
        for copy in self.from_sib:
            copy.wait_recv()


class Corner(Spread):
    def __init__(self, me, links, view, own, from_x, from_y):
        self.me, self.links, self.view = me, links, view
        first, last = pl.ds(0, 48), pl.ds(48, 48)
        self.low = links.start(from_x.at[:, first], view(me.x_place, 0, 48), me.yn)
        self.high = links.start(from_y.at[:, last], view(me.y_place, 48, 48), me.xn)
        self.from_sib = [
            links.start(src, view(place, 0, 96), me.sib)
            for src, place in ((own, me.place), (from_x, me.x_place), (from_y, me.y_place))
        ]


def view_2d(ref):
    return lambda place, first, size: ref.at[pl.ds(pl.multiple_of(place * 96 + first, 16), size)]


def view_3d(ref):
    return lambda place, first, size: ref.at[:, pl.ds(pl.multiple_of(place * 96 + first, 16), size)]


class Moves:
    def __init__(self, sems):
        self.sems, self.count = sems, 0

    def start(self, src, dst):
        copy = pltpu.make_async_copy(src, dst, self.sems.at[self.count])
        self.count += 1
        copy.start()
        return copy


def start_kernel(
    x, wo, fb, near_row, inverse,
    tok, w, wf0, zb, zl, qa_out, ka_out, kt_out, vn_out, va_out, cos_out, sin_out, seg, first, end,
    tv, wx, wv, far_row, cos, sin, qa, ka, kt, vn, va, token_send, token_recv, send, recv, local,
):
    me = Place()
    moves = Moves(local)
    c, z = me.c, me.z
    away = z + c * (3 - 2 * z)

    barrier = pltpu.get_barrier_semaphore()
    partners = (me.sib, me.xn, me.yn, me.z1, me.z2)
    for partner in partners:
        pl.semaphore_signal(barrier, inc=1, device_id=partner, device_id_type=MESH)
    @pl.when(z % 3 != 0)
    def _():
        pl.semaphore_signal(barrier, inc=1, device_id={"tensor": 3 - z}, device_id_type=MESH)

    pl.semaphore_wait(barrier, len(partners) + z * (3 - z) // 2)

    def line(k):
        return k + c * (3 - 2 * k)

    def line_sib(k):
        return k + (1 - c) * (3 - 2 * k)

    far, near = {"tensor": line(0)}, {"tensor": line(1)}

    def part(ch):
        return pl.ds(ch * CHUNK, CHUNK)

    def copy(kind, k, ch, src, to):
        return pltpu.make_async_remote_copy(
            src_ref=src, dst_ref=tv.at[line(k), part(ch)],
            send_sem=token_send.at[kind, k, ch],
            recv_sem=token_recv.at[k, ch], device_id=to, device_id_type=MESH,
        )

    def own(ch):
        return x.at[part(ch)]

    def held(k, ch):
        return tv.at[line(k), part(ch)]

    links = Links(send, recv)
    rows_far = links.start(near_row, far_row, me.sib)
    attn_z = links.start(view_2d(wo)(me.place, 0, 96), view_2d(wx)(me.place, 0, 96), me.z2)
    ff_z1 = links.make(fb, zb.at[0], me.z1)
    ff_z2 = links.make(fb, zb.at[1], me.z2)
    for k, to in ((0, near), (1, far), (2, near), (3, near)):

        @pl.when(away == k)
        def _(k=k, to=to):
            for ch in range(CHUNKS):
                copy(0, k, ch, own(ch), to).start()
                if k < 2:
                    copy(1, k, ch, own(ch), me.sib).start()

    ff_z1.start()
    links.started.append(ff_z1)
    ff_z2.start()
    links.started.append(ff_z2)
    ff0 = Spread(me, links, view_3d(wf0), fb)
    here = moves.start(fb, view_3d(wf0)(me.place, 0, 96))

    @pl.when(away < 2)
    def _():
        mine = pltpu.make_async_copy(x, tv.at[z], local.at[30])
        mine.start()
        mine.wait()

    def forward(ch):
        @pl.when(away == 0)
        def _():
            for k in (1, 2, 3):
                copy(1, k, ch, held(k, ch), me.sib).wait_recv()
                copy(1, k, ch, held(k, ch), me.sib).start()

        @pl.when(away == 1)
        def _():
            for k in (2, 3, 0):
                copy(1, k, ch, held(k, ch), me.sib).wait_recv()
                if k:
                    copy(0, k, ch, held(k, ch), far).start()
                copy(1, k, ch, held(k, ch), me.sib).start()

    def documents():
        rows_far.wait_recv()
        row = jnp.where(me.cross == 1, far_row[...], near_row[...])
        seg[...] = row
        opened = jnp.zeros(row.shape, F32)
        closed = jnp.zeros(row.shape, F32)
        before = jnp.zeros((1, 1), F32)
        for d in range(SEGS):
            here = (row == d).astype(F32)
            opened += here * before
            before = before + jnp.sum(here, axis=1, keepdims=True)
            closed += here * before
        first[...] = opened.astype(jnp.int32)
        end[...] = closed.astype(jnp.int32)
        places = lax.broadcasted_iota(jnp.int32, row.shape, 1).astype(F32) - opened
        for e in range(4):
            at = slice(e * 512, (e + 1) * 512)
            angles = inverse[...] * places[:, at]
            cos[:, at] = jnp.cos(angles)
            sin[:, at] = jnp.sin(angles)

    attn_z.wait_recv()
    attn = Spread(me, links, view_2d(wx))
    documents()
    forward(0)
    attn.second()
    forward(1)
    attn.third()
    ff0.second()
    forward(2)
    forward(3)
    ff0.third()

    @pl.when(away >= 2)
    def _():
        for ch in range(CHUNKS):
            for k in range(4):
                pltpu.make_async_remote_copy(
                    src_ref=own(ch), dst_ref=tv.at[line_sib(k), part(ch)], send_sem=token_send.at[0, k, ch],
                    recv_sem=token_recv.at[k, ch], device_id=me.sib, device_id_type=MESH,
                ).wait_recv()

    attn.last()

    def chosen(src):
        return pltpu.make_async_copy(src, wv, local.at[31])

    @pl.when(me.cross == 0)
    def _():
        chosen(wo).start()

    @pl.when(me.cross == 1)
    def _():
        chosen(wx).start()

    chosen(wx).wait()
    moved = [here, moves.start(tv, tok), moves.start(wv, w), moves.start(cos, cos_out), moves.start(sin, sin_out)]

    heads = 3
    width = heads * HEAD_DIM

    def project(e, _):
        at = pl.ds(pl.multiple_of(e * 512, 512), 512)
        made = nt(wv[: 3 * width], tv[e])
        c_, s_ = cos[:, at], sin[:, at]
        hot = (seg[:, at] == lax.broadcasted_iota(jnp.int32, (SEGS, 512), 0)).astype(F32)
        rest = jnp.zeros((64 - SEGS, 512), F32)
        one_row = (lax.broadcasted_iota(jnp.int32, (16, 512), 0) == 0).astype(F32)
        for h in range(heads):
            r = h * HEAD_DIM
            a1, a2 = made[r : r + 32], made[r + 32 : r + 64]
            q = jnp.concatenate([a1 * c_ - a2 * s_, a2 * c_ + a1 * s_], axis=0).astype(BF16).astype(F32)
            qa[h, :, at] = jnp.concatenate([q * 0.125, hot, rest], axis=0).astype(BF16)
            r += width
            a1, a2 = made[r : r + 32], made[r + 32 : r + 64]
            k = jnp.concatenate([a1 * c_ - a2 * s_, a2 * c_ + a1 * s_], axis=0)
            kt[h * HEAD_DIM : (h + 1) * HEAD_DIM, at] = k.astype(BF16)
            ka[h, at, :] = jnp.concatenate([k, (1.0 - hot) * far_below, rest], axis=0).T.astype(BF16)
            r += width
            v = made[r : r + 64]
            va[h, :, at] = jnp.concatenate([v, one_row], axis=0).astype(BF16)
            vn[h, at, :] = jnp.concatenate([v, jnp.zeros_like(v)], axis=0).T[:, :HEAD_DIM].astype(BF16)
        return 0

    lax.fori_loop(0, 4, project, 0)
    for src, dst in ((qa, qa_out), (ka, ka_out), (kt, kt_out), (vn, vn_out), (va, va_out)):
        moved.append(moves.start(src, dst))
    ff0.last()
    ff_z2.wait_recv()
    moved.append(moves.start(zb.at[1], zl))
    ff_z1.wait_recv()
    for move in moved:
        move.wait()
    links.wait_sends()
    for k, to in ((0, near), (1, far), (2, near), (3, near)):

        @pl.when(away == k)
        def _(k=k, to=to):
            for ch in range(CHUNKS):
                copy(0, k, ch, own(ch), to).wait_send()
                if k == 1:
                    for j in (2, 3):
                        copy(0, j, ch, held(j, ch), to).wait_send()
                if k < 2:
                    for j in range(4):
                        copy(1, j, ch, own(ch) if j == k else held(j, ch), me.sib).wait_send()


FIRST, LAST = 256, 512


def list_pairs(first, end, pairs):
    idle = 8 * 16 + 8
    pairs[0] = idle

    def of_query(i, n):
        lo = first[0, i * BLK] // BLK
        hi = (end[0, i * BLK + BLK - 1] + (BLK - 1)) // BLK

        def of_key(j, n):
            pairs[n] = i * 16 + j + jnp.where(j == lo, FIRST, 0) + jnp.where(j == hi - 1, LAST, 0)
            return n + 1

        return lax.fori_loop(lo, hi, of_key, n)

    n = lax.fori_loop(0, 2048 // BLK, of_query, 1)
    for more in range(3):
        pairs[n + more] = idle
    return n - 1


def split_pair(code):
    return (code // 16) % 16, code % 16


def columns(block):
    return pl.ds(pl.multiple_of(block * BLK, BLK), BLK)


def real(block):
    return jnp.where(block == 8, 0, block)


def attend_forward_kernel(
    first, end, w_in, qa_in, ka_in, va_in, ot, logsum, part,
    w, qa, ka, va, mx, acc, s0, s1, p0, p1, al0, al1, pairs, sem,
):
    heads = 3
    width = heads * HEAD_DIM
    moves = Moves(sem)
    loads = [moves.start(src, dst) for src, dst in ((qa_in, qa), (ka_in, ka), (va_in, va), (w_in.at[pl.ds(3 * width, width)], w))]
    count = list_pairs(first, end, pairs)

    def score(t, s):
        i, j = split_pair(pairs[t])
        at, here = columns(real(i)), columns(real(j))
        for h in range(heads):
            s[h] = nn(ka[h, here, :], qa[h, :, at])

    def weigh(t, s, p, al):
        fresh = pairs[t] & FIRST
        for h in range(heads):
            scores = s[h]
            before = jnp.where(fresh > 0, -3e38, mx[h])
            largest = jnp.maximum(before, jnp.max(scores, axis=0, keepdims=True))
            p[h] = jnp.exp(scores - largest).astype(BF16)
            al[h] = jnp.exp(before - largest)
            mx[h] = largest

    def gather(t, p, al):
        code = pairs[t]
        i, j = split_pair(code)
        here = columns(real(j))
        for h in range(heads):
            acc[h] = acc[h] * al[h] + nn(va[h, :, here], p[h])

        @pl.when((code & LAST) > 0)
        def _():
            at = columns(i)
            for h in range(heads):
                total = acc[h, 64:65, :]
                ot[h * HEAD_DIM : (h + 1) * HEAD_DIM, at] = (acc[h, :64, :] / total).astype(BF16)
                logsum[pl.ds(h, 1), at] = mx[h] + jnp.log(total)

    def step(u, _):
        t = 2 * u + 1
        gather(t - 1, p1, al1)
        weigh(t, s0, p0, al0)
        score(t + 1, s1)
        gather(t, p0, al0)
        weigh(t + 1, s1, p1, al1)
        score(t + 2, s0)
        return 0

    acc[...] = jnp.zeros_like(acc)
    p1[...] = jnp.zeros_like(p1)
    al1[...] = jnp.zeros_like(al1)
    for load in loads:
        load.wait()
    score(1, s0)
    lax.fori_loop(0, (count + 2) // 2, step, 0)
    for e in range(4):
        part[e] = tn(ot[:, e * 512 : (e + 1) * 512], w[...]).astype(BF16)


def attend_backward_kernel(
    first, end, gb_in, tok_in, w_in, qa_in, ka_in, kt_in, vn_in, ot_in, logsum, cos_in, sin_in, grads, part,
    gb, tok, w, qa, ka, kt, vn, ot, cos, sin, dot_, inner, dq, dk, dv, gp, s0, s1, r0, r1, p0, p1, d0, d1, pairs, sem,
):
    heads = 3
    width = heads * HEAD_DIM
    moves = Moves(sem)
    loads = [
        moves.start(src, dst)
        for src, dst in (
            (w_in, w), (ot_in, ot), (gb_in, gb), (qa_in, qa), (ka_in, ka), (vn_in, vn), (kt_in, kt), (cos_in, cos),
            (sin_in, sin), (tok_in, tok),
        )
    ]
    for total in (dq, dk, dv, p1, d1):
        total[...] = jnp.zeros_like(total)
    count = list_pairs(first, end, pairs)
    for load in loads[:3]:
        load.wait()

    def begin(e, _):
        at = pl.ds(pl.multiple_of(e * 512, 512), 512)
        made = nt(w[3 * width :], gb[e]).astype(BF16)
        dot_[:, at] = made
        product = made.astype(F32) * ot[:, at].astype(F32)
        for h in range(heads):
            inner[pl.ds(h, 1), at] = jnp.sum(product[h * HEAD_DIM : (h + 1) * HEAD_DIM], axis=0, keepdims=True)
        return 0

    lax.fori_loop(0, 4, begin, 0)
    for load in loads[3:]:
        load.wait()

    def score(t, s, r):
        i, j = split_pair(pairs[t])
        at, here = columns(real(i)), columns(real(j))
        for h in range(heads):
            rows = slice(h * HEAD_DIM, (h + 1) * HEAD_DIM)
            s[h] = nn(ka[h, here, :], qa[h, :, at])
            r[h] = nn(vn[h, here, :], dot_[rows, at])

    def weigh(t, s, r, p, d):
        at = columns(real(split_pair(pairs[t])[0]))
        for h in range(heads):
            probability = jnp.exp(s[h] - logsum[pl.ds(h, 1), at])
            p[h] = probability.astype(BF16)
            d[h] = (probability * (r[h] - inner[pl.ds(h, 1), at])).astype(BF16)

    def gather(t, p, d):
        i, j = split_pair(pairs[t])
        at, here = columns(real(i)), columns(real(j))
        to_query, to_key = columns(i), columns(j)
        for h in range(heads):
            rows = slice(h * HEAD_DIM, (h + 1) * HEAD_DIM)
            dv[rows, to_key] += nt(dot_[rows, at], p[h])
            dk[rows, to_key] += nt(qa[h, :HEAD_DIM, at], d[h])
            dq[rows, to_query] += nn(kt[rows, here], d[h])

    def step(u, _):
        t = 2 * u + 1
        gather(t - 1, p1, d1)
        weigh(t, s0, r0, p0, d0)
        score(t + 1, s1, r1)
        gather(t, p0, d0)
        weigh(t + 1, s1, r1, p1, d1)
        score(t + 2, s0, r0)
        return 0

    score(1, s0, r0)
    lax.fori_loop(0, (count + 2) // 2, step, 0)

    def turn(e, _):
        at = pl.ds(pl.multiple_of(e * 512, 512), 512)
        c, s = cos[:, at], sin[:, at]
        for h in range(heads):
            r = h * HEAD_DIM
            for first, total, scale in ((0, dq, 0.125), (width, dk, 1.0)):
                d1_, d2_ = total[r : r + 32, at] * scale, total[r + 32 : r + 64, at] * scale
                gp[first + r : first + r + 64, at] = jnp.concatenate(
                    [d1_ * c + d2_ * s, d2_ * c - d1_ * s], axis=0
                ).astype(BF16)
        gp[2 * width :, at] = dv[:, at].astype(BF16)
        return 0

    lax.fori_loop(0, 4, turn, 0)
    for e in range(4):
        part[e] = tn(gp[:, e * 512 : (e + 1) * 512], w[: 3 * width]).astype(BF16)
    for block in range(4):
        if block < 3:
            rows = slice(block * width, (block + 1) * width)
            made = sum(nn(gp[rows, e * 512 : (e + 1) * 512], tok[e]) for e in range(4))
        else:
            made = sum(nn(ot[:, e * 512 : (e + 1) * 512], gb[e]) for e in range(4))
        grads[block * width : (block + 1) * width] = made.astype(BF16)


def row_mean(v):
    return jnp.mean(v, axis=-1, keepdims=True)


def norm_forward(summed):
    centred = summed - row_mean(summed)
    inverse = lax.rsqrt(row_mean(centred * centred) + epsilon)
    return centred * inverse, inverse


def norm_backward(scaled, normalized, inverse):
    return inverse * (scaled - row_mean(scaled) - normalized * row_mean(scaled * normalized))


def feed_forward_kernel(
    tok, part_in, cot_in, gain, bias, wf0, zb, zx, zy, zc,
    out, gz1, gb, sums, keep_a, keep_b, send_a, send_b, zs_out,
    part, own_g, w, slope_g, slope_u, hid, nb, nbt, gm, gmt, total, norm1, inv1, dw, lw, xs, cot, from_core, from_z, to_z,
    f1a, f1b, f2a, f2b, send, recv, local, out_sem, trade_sem,
):
    me = Place()
    greet((me.sib, me.xn, me.yn, me.z1, me.pair))
    links = Links(send, recv)
    moves = Moves(local)
    partial = moves.start(part_in, part)
    loads = [moves.start(tok.at[me.slot], xs), moves.start(wf0, w.at[0])]
    for ez in (2, 1):
        for place, src in ((me.place, zb), (me.x_place, zx), (me.y_place, zy)):
            loads.append(moves.start(src.at[ez - 1], view_3d(w.at[ez])(place, 0, 96)))
    loads.append(moves.start(zc, view_3d(w.at[3])(me.place, 0, 96)))

    def cot_here():
        return pltpu.make_async_copy(cot_in, cot, local.at[15])

    def cot_there():
        return pltpu.make_async_remote_copy(
            src_ref=cot_in, dst_ref=cot, send_sem=trade_sem.at[0], recv_sem=trade_sem.at[1], device_id=me.pair,
            device_id_type=MESH,
        )

    def rows(ch):
        return pl.ds(ch * CHUNK, CHUNK)

    partial.wait()
    cores = [
        [links.start(part.at[shard, rows(ch)], from_core.at[i, rows(ch)], me.sib) for ch in range(CHUNKS)]
        for i, shard in ((1, me.slot3), (0, me.slot2))
    ]
    ff2, ff1 = [Corner(me, links, view_3d(w.at[ez]), *(src.at[ez - 1] for src in (zb, zx, zy))) for ez in (2, 1)]
    ff3 = Spread(me, links, view_3d(w.at[3]), zc)
    zs = []
    for ch in range(CHUNKS):
        cores[0][ch].wait_recv()
        at = rows(ch)
        to_z[at] = (part[me.slot1, at].astype(F32) + from_core[1, at].astype(F32)).astype(BF16)
        zs.append(links.start(to_z.at[at], from_z.at[at], me.z1))

    @pl.when(me.cross == 0)
    def _():
        cot_here().start()

    @pl.when(me.cross == 1)
    def _():
        cot_there().start()

    ff2.third()
    ff1.third()
    loads[0].wait()
    for ch in range(CHUNKS):
        if ch == CHUNKS - 1:
            ff3.second()
        cores[1][ch].wait_recv()
        zs[ch].wait_recv()
        at = rows(ch)
        branch = part[me.slot, at].astype(F32) + from_core[0, at].astype(F32) + from_z[at].astype(F32)
        n1, i1 = norm_forward(xs[at].astype(F32) + branch)
        norm1[at] = n1
        inv1[at] = jnp.broadcast_to(i1, (CHUNK, 128))
        normed = n1 * gain[0:1, :] + bias[0:1, :]
        total[at] = normed
        nb[at] = normed.astype(BF16)
        nbt[:, ch * CHUNK : (ch + 1) * CHUNK] = normed.T.astype(BF16)

    def forward(ez):
        gate = nn(nb[...], w[ez, 0])
        up = nn(nb[...], w[ez, 1])
        sig = 1.0 / (1.0 + jnp.exp(-gate))
        active = gate * sig
        low = (active * up).astype(BF16)
        hid[ez] = low
        slope_u[ez] = active.astype(BF16)
        slope_g[ez] = (up * sig * (1.0 + gate * (1.0 - sig))).astype(BF16)
        total[...] += nn(low, w[ez, 2])

    loads[1].wait()
    forward(0)
    for load in loads[2:]:
        load.wait()
    ff2.last()
    forward(2)
    ff3.third()
    ff1.last()
    forward(1)
    ff3.last()
    forward(3)
    n2, i2 = norm_forward(total[...])
    out[...] = (n2 * gain[1:2, :] + bias[1:2, :]).astype(BF16)

    @pl.when(me.cross == 0)
    def _():
        cot_here().wait()

    @pl.when(me.cross == 1)
    def _():
        cot_there().wait()

    g = cot[...].astype(F32)
    sums[1:2, :] = jnp.sum(g * n2, axis=0, keepdims=True)
    sums[3:4, :] = jnp.sum(g, axis=0, keepdims=True)
    gz2 = norm_backward(g * gain[1:2, :], n2, i2)
    total[...] = gz2
    gm[...] = gz2.astype(BF16)
    gmt[...] = gz2.T.astype(BF16)

    def block(quad, core):
        return pl.ds(pl.multiple_of((quad * 2 + core) * 96, 32), 96)

    order = (3, 1, 0, 2)
    halves = []
    first, last = pl.ds(0, 48), pl.ds(48, 48)

    def slopes(ez):
        grad_hidden = nt(gm[...], w[ez, 2])
        gate = (grad_hidden * slope_g[ez].astype(F32)).astype(BF16)
        up = (grad_hidden * slope_u[ez].astype(F32)).astype(BF16)
        slope_g[ez] = gate
        slope_u[ez] = up
        total[...] += nt(gate, w[ez, 0]) + nt(up, w[ez, 1])

    def weights(n):
        i, ez = n % 2, order[n]
        if n >= 2:
            for copy in halves[n - 2]:
                copy.wait_send()
        dw[i, 2] = nn(gmt[...], hid[ez]).astype(BF16)
        dw[i, 0] = nn(nbt[...], slope_g[ez]).astype(BF16)
        dw[i, 1] = nn(nbt[...], slope_u[ez]).astype(BF16)
        halves.append([links.make(dw.at[i, :, block(quad, 1 - me.c)], lw.at[n, quad], me.sib) for quad in range(4)])
        for copy in halves[n]:
            copy.start()

    def settle(n):
        for quad in range(4):
            halves[n][quad].wait_recv()
            for m in range(3):
                lw[n, quad, m] = (lw[n, quad, m].astype(F32) + dw[n % 2, m, block(quad, me.c)].astype(F32)).astype(BF16)

    def plane_first():
        return [
            (
                links.start(lw.at[0, (1 - me.y) * 2 + o, :, first], f1a.at[o], me.yn),
                links.start(lw.at[0, o * 2 + 1 - me.x, :, last], f1b.at[o], me.xn),
            )
            for o in range(2)
        ]

    def plane_second(plane_1):
        for o in range(2):
            plane_1[o][0].wait_recv()
            f1a[o] = (f1a[o].astype(F32) + lw[0, me.y * 2 + o, :, first].astype(F32)).astype(BF16)
            plane_1[o][1].wait_recv()
            f1b[o] = (f1b[o].astype(F32) + lw[0, o * 2 + me.x, :, last].astype(F32)).astype(BF16)
        return links.start(f1a.at[1 - me.x], f2a, me.xn), links.start(f1b.at[1 - me.y], f2b, me.yn)

    def plane_last(plane_2):
        plane_2[0].wait_recv()
        zs_out[0] = (f1a[me.x].astype(F32) + f2a[...].astype(F32)).astype(BF16)
        plane_2[1].wait_recv()
        zs_out[1] = (f1b[me.y].astype(F32) + f2b[...].astype(F32)).astype(BF16)

    def stores(n):
        made = []
        for oy in range(2):
            for ox in range(2):
                src = lw.at[n, oy * 2 + ox]
                made.append((me.y == oy, src.at[:, first], keep_a.at[n - 1, ox], send_a.at[n - 1, ox]))
                made.append((me.x == ox, src.at[:, last], keep_b.at[n - 1, oy], send_b.at[n - 1, oy]))
        return made

    def store(n):
        for number, (here, src, kept, sent) in enumerate(stores(n)):

            @pl.when(here)
            def _(number=number, src=src, kept=kept):
                pltpu.make_async_copy(src, kept, out_sem.at[n - 1, number]).start()

            @pl.when(jnp.logical_not(here))
            def _(number=number, src=src, sent=sent):
                pltpu.make_async_copy(src, sent, out_sem.at[n - 1, number]).start()

    slopes(3)
    weights(0)
    slopes(1)
    slopes(0)
    settle(0)
    plane_1 = plane_first()
    slopes(2)
    g = total[...]
    sums[0:1, :] = jnp.sum(g * norm1[...], axis=0, keepdims=True)
    sums[2:3, :] = jnp.sum(g, axis=0, keepdims=True)
    sums[4:8, :] = jnp.zeros((4, 768), F32)
    to_pair, to_core, on_core = [], [], []
    for ch in range(CHUNKS):
        at = rows(ch)
        made = norm_backward(total[at] * gain[0:1, :], norm1[at], inv1[at, 0:1])
        gz1[at] = made
        own_g[at] = made.astype(BF16)
        mine = gb.at[me.slot, at]
        to_pair.append(links.start(own_g.at[at], mine, me.z1))
        to_core.append(links.start(own_g.at[at], mine, me.sib))
    kept_g = moves.start(own_g, gb.at[me.slot])
    weights(1)
    weights(2)
    settle(1)
    store(1)
    plane_2 = plane_second(plane_1)
    weights(3)
    settle(2)
    store(2)
    settle(3)
    store(3)
    for ch in range(CHUNKS):
        to_pair[ch].wait_recv()
        other = gb.at[me.slot1, rows(ch)]
        on_core.append(links.start(other, other, me.sib))
    plane_last(plane_2)
    kept_g.wait()
    for copy in to_core + on_core:
        copy.wait_recv()
    for n in (1, 2, 3):
        for number, (_, src, kept, _) in enumerate(stores(n)):
            pltpu.make_async_copy(src, kept, out_sem.at[n - 1, number]).wait()
    for n in (2, 3):
        for copy in halves[n]:
            copy.wait_send()
    links.wait_sends()


def finish_kernel(
    extra, keep_a, keep_b, recv_a, recv_b, zr, ga, part, gz1, sums_in,
    g_ff, g_attn, g_tok, sums,
    sa, sb, f2a, f2b, va, f3, f4, fe, a_in, a_mid, a_out, a_fin, a_two, ae, from_core, from_z, to_z, trade_out, trade_in, sum_in,
    send, recv, a_send, a_recv,
):
    me = Place()
    bits = [{"dp": me.p + bit - 2 * bit * ((me.p // bit) % 2)} for bit in extra]
    greet([me.sib, me.xn, me.yn, me.z1, me.z2, me.pair] + bits)
    links = Links(send, recv)

    def rows(ch):
        return pl.ds(ch * CHUNK, CHUNK)

    def add(*terms):
        return sum(t.astype(F32) for t in terms).astype(BF16)

    cores = [
        [links.start(part.at[shard, rows(ch)], from_core.at[i, rows(ch)], me.sib) for ch in range(CHUNKS)]
        for i, shard in ((1, me.slot3), (0, me.slot2))
    ]

    def half(oy, ox, h):
        return pl.ds(pl.multiple_of((oy * 2 + ox) * 192 + h * 96, 32), 96)

    attn_1 = []
    for o in range(2):
        attn_1.append(links.start(ga.at[half(1 - me.y, o, 0)], a_in.at[0, o], me.yn))
        attn_1.append(links.start(ga.at[half(o, 1 - me.x, 1)], a_in.at[1, o], me.xn))

    sums[...] = sums_in[...]
    around = [me.sib, me.xn, me.yn, me.z1, me.z2] + bits
    small = [links.start(sums, sum_in.at[0], around[0])]

    def small_step():
        n = len(small)
        small[-1].wait_recv()
        small[-1].wait_send()
        links.started = [copy for copy in links.started if copy is not small[n - 1]]
        sums[...] += sum_in[n - 1]
        if n < len(around):
            small.append(links.start(sums, sum_in.at[n], around[n]))

    ff_2 = {}

    def plane(ez):
        sa[ez] = add(keep_a[ez, 1 - me.x], recv_a[ez, 1 - me.x])
        sb[ez] = add(keep_b[ez, 1 - me.y], recv_b[ez, 1 - me.y])
        ff_2[ez] = (links.start(sa.at[ez], f2a.at[ez], me.xn), links.start(sb.at[ez], f2b.at[ez], me.yn))

    def planed(ez):
        ff_2[ez][0].wait_recv()
        va[ez, 0] = add(keep_a[ez, me.x], recv_a[ez, me.x], f2a[ez], *([zr[0]] if ez == 2 else []))
        ff_2[ez][1].wait_recv()
        va[ez, 1] = add(keep_b[ez, me.y], recv_b[ez, me.y], f2b[ez], *([zr[1]] if ez == 2 else []))

    plane(2)
    zs = []
    for ch in range(CHUNKS):
        cores[0][ch].wait_recv()
        at = rows(ch)
        to_z[at] = add(part[me.slot1, at], from_core[1, at])
        zs.append(links.start(to_z.at[at], from_z.at[at], me.z1))
    for copy in attn_1:
        copy.wait_recv()
    small_step()
    a_mid[0] = add(ga[half(me.y, 1 - me.x, 0)], a_in[0, 1 - me.x])
    a_mid[1] = add(ga[half(1 - me.y, me.x, 1)], a_in[1, 1 - me.y])
    attn_2 = [links.start(a_mid.at[0], a_out.at[0], me.xn), links.start(a_mid.at[1], a_out.at[1], me.yn)]
    planed(2)
    ff_4 = links.start(va.at[2], f4, me.z2)
    for copy in attn_2:
        copy.wait_recv()
    small_step()
    a_fin[:96] = add(ga[half(me.y, me.x, 0)], a_in[0, me.x], a_out[0])
    a_fin[96:] = add(ga[half(me.y, me.x, 1)], a_in[1, me.y], a_out[1])

    def attn_copy(n, src, dst, to):
        return pltpu.make_async_remote_copy(
            src_ref=src, dst_ref=dst, send_sem=a_send.at[n], recv_sem=a_recv.at[n], device_id=to, device_id_type=MESH
        )

    def quarter(oy, ox, first=0, size=192):
        return g_attn.at[pl.ds(pl.multiple_of((oy * 2 + ox) * 192 + first, 32), size)]

    def attn_over():
        return attn_copy(0, a_fin, a_two, me.z2)

    @pl.when(me.cross == 1)
    def _():
        attn_over().start()

    plane(0)
    plane(1)
    planed(0)
    ff_3 = links.start(va.at[0], f3, me.z1)
    planed(1)
    small_step()

    trades = [
        pltpu.make_async_remote_copy(
            src_ref=trade_out.at[rows(ch)], dst_ref=trade_in.at[rows(ch)], send_sem=a_send.at[8 + ch],
            recv_sem=a_recv.at[8 + ch], device_id=me.pair, device_id_type=MESH,
        )
        for ch in range(CHUNKS)
    ]
    mine = quarter(me.y, me.x)

    def attn_send(n, src, to):
        return attn_copy(n, src, src, to)

    block_x, block_y = quarter(me.y, 1 - me.x), quarter(1 - me.y, me.x)
    low_x, high_y = quarter(me.y, 1 - me.x, 0, 96), quarter(1 - me.y, me.x, 96, 96)
    corner = quarter(1 - me.y, 1 - me.x)

    @pl.when(me.cross == 0)
    def _():
        attn_over().wait_recv()
        total = add(a_fin[...], a_two[...])
        for n, bit in enumerate(bits):
            ae[n, 0] = total
            step = attn_copy(16 + n, ae.at[n, 0], ae.at[n, 1], bit)
            step.start()
            step.wait()
            total = add(total, ae[n, 1])
        g_attn[pl.ds(pl.multiple_of((me.y * 2 + me.x) * 192, 32), 192)] = total
        attn_send(1, mine, me.xn).start()
        attn_send(2, mine, me.yn).start()
        attn_send(3, mine, me.sib).start()

    for ch in range(CHUNKS):
        cores[1][ch].wait_recv()
        zs[ch].wait_recv()
        at = rows(ch)
        got = gz1[at] + (part[me.slot, at].astype(F32) + from_core[0, at].astype(F32) + from_z[at].astype(F32))

        @pl.when(me.cross == 0)
        def _(at=at, got=got):
            g_tok[at] = got

        @pl.when(me.cross == 1)
        def _(at=at, got=got, ch=ch):
            trade_out[at] = got.astype(BF16)

    small_step()


    @pl.when(me.cross == 0)
    def _():
        attn_send(1, block_x, me.xn).wait_recv()
        attn_send(4, low_x, me.yn).start()
        attn_send(5, block_x, me.sib).start()
        attn_send(2, block_y, me.yn).wait_recv()
        attn_send(6, high_y, me.xn).start()
        attn_send(7, block_y, me.sib).start()

    ff_3.wait_recv()
    ff_4.wait_recv()
    total = add(va[1], f3[...], f4[...])
    for n, bit in enumerate(bits):
        fe[n, 0] = total
        step = links.start(fe.at[n, 0], fe.at[n, 1], bit)
        step.wait_recv()
        total = add(total, fe[n, 1])
    for h in range(2):
        g_ff[:, pl.ds(pl.multiple_of(me.place * 96 + h * 48, 16), 48)] = total[h]
    spread = Spread(me, links, view_3d(g_ff))

    @pl.when(me.cross == 1)
    def _():
        for ch in range(CHUNKS):
            trades[ch].start()

    while len(small) < len(around):
        small_step()
    spread.second()
    small_step()

    @pl.when(me.cross == 0)
    def _():
        attn_send(4, low_x, me.yn).wait_recv()
        attn_send(6, high_y, me.xn).wait_recv()
        attn_send(12, corner, me.sib).start()
        for n, src, to in (
            (1, mine, me.xn), (2, mine, me.yn), (3, mine, me.sib), (4, low_x, me.yn), (5, block_x, me.sib),
            (6, high_y, me.xn), (7, block_y, me.sib), (12, corner, me.sib),
        ):
            attn_send(n, src, to).wait_send()

    @pl.when(me.cross == 1)
    def _():
        for ch in range(CHUNKS):
            trades[ch].wait_recv()
            g_tok[rows(ch)] = trade_in[rows(ch)].astype(F32)
        attn_over().wait_send()
        for n, src in ((3, mine), (5, block_x), (7, block_y), (12, corner)):
            attn_send(n, src, me.sib).wait_recv()
        for ch in range(CHUNKS):
            trades[ch].wait_send()

    spread.third()
    spread.last()
    links.wait_sends()


def widen_kernel(attn, out_rows, gate_up, down, g_qkv, g_out, g_gate_up, g_down):
    g_qkv[...] = attn[...].astype(F32)
    g_out[...] = out_rows[...].astype(F32)
    g_gate_up[:, 0, :] = gate_up[0].astype(F32)
    g_gate_up[:, 1, :] = gate_up[1].astype(F32)
    g_down[...] = down[0].astype(F32).T


def solution(mesh):
    dp, tensor = mesh.shape["dp"], mesh.shape["tensor"]
    assert tensor == 4 and dp >= 8 and dp & (dp - 1) == 0
    extra = [1 << b for b in range(3, dp.bit_length() - 1)]
    both = ("dp", "tensor")

    def cell(i, k):
        return i * tensor + k

    def over(x, bit):
        return lax.ppermute(x, "dp", [(i, i ^ bit) for i in range(dp)])

    away = [(i, k) for i in range(dp) for k in range(tensor) if (i & 1) != (k >> 1)]

    def trade(x):
        return lax.ppermute(x, both, [(cell(i, k), cell(i ^ 1, k ^ 2)) for i, k in away])

    smem = pl.BlockSpec(memory_space=pltpu.SMEM)
    vmem = pl.BlockSpec(memory_space=pltpu.VMEM)
    hbm = pl.BlockSpec(memory_space=pl.ANY)

    def shape(*dims, dtype=BF16):
        return jax.ShapeDtypeStruct(dims, dtype)

    far = pl.BlockSpec(memory_space=pltpu.HBM)

    def held(*dims, dtype=BF16):
        return pltpu.HBM(dims, dtype)

    def dma(*dims):
        return pltpu.SemaphoreType.DMA(dims)

    def params(mib, number=None):
        if number is None:
            return pltpu.CompilerParams(vmem_limit_bytes=mib << 20)
        return pltpu.CompilerParams(vmem_limit_bytes=mib << 20, collective_id=number, has_side_effects=True)

    def on_device(tokens, segments, w_qkv, w_out, w_gate_up, w_down, norm_gain, norm_bias, cotangent):
        p, z = lax.axis_index("dp"), lax.axis_index("tensor")
        swapped = (p & 1) != (z >> 1)
        place = p & 7

        own = jnp.concatenate([w_qkv.transpose(1, 2, 0).reshape(576, 768), w_out])
        rows = lax.dynamic_slice(w_gate_up, (place * 96, 0, 0), (96, 2, 768))
        block = jnp.stack([rows[:, 0], rows[:, 1], lax.dynamic_slice(w_down, (place * 96, 0), (96, 768))])

        length = segments.shape[1]
        inverse = jnp.asarray(np.exp(-2.0 * np.arange(HEAD_DIM // 2) / HEAD_DIM * log_base).astype(np.float32)[:, None])
        tok, w, wf0, zb, zl, qa, ka, kt, vn, va, cos, sin, seg, first, end = pl.pallas_call(
            start_kernel,
            name="start",
            out_shape=(
                held(4, 512, 768), held(768, 768), held(3, 768, 768), held(2, 3, 96, 768), held(3, 96, 768),
                held(3, 128, length), held(3, length, 128), held(192, length), held(3, length, 64), held(3, 80, length),
                held(32, length, dtype=F32), held(32, length, dtype=F32),
                *(shape(1, length, dtype=jnp.int32),) * 3,
            ),
            in_specs=[hbm] * 3 + [vmem] * 2,
            out_specs=(far,) * 12 + (vmem,) * 3,
            scratch_shapes=[
                pltpu.VMEM((4, 512, 768), BF16),
                pltpu.VMEM((768, 768), BF16),
                pltpu.VMEM((768, 768), BF16),
                pltpu.VMEM((1, length), jnp.int32),
                pltpu.VMEM((32, length), F32),
                pltpu.VMEM((32, length), F32),
                pltpu.VMEM((3, 128, length), BF16),
                pltpu.VMEM((3, length, 128), BF16),
                pltpu.VMEM((192, length), BF16),
                pltpu.VMEM((3, length, 64), BF16),
                pltpu.VMEM((3, 80, length), BF16),
                dma(2, 4, CHUNKS), dma(4, CHUNKS), dma(40), dma(40), dma(32),
            ],
            compiler_params=params(62, 0),
        )(tokens[0], own, block, segments, inverse)

        zc = lax.ppermute(zl, "tensor", [(i, i ^ 1) for i in range(tensor)])
        zx, zy = over(zb, 2), over(zb, 4)

        ot, logsum, part = pl.pallas_call(
            attend_forward_kernel,
            name="attend_forward",
            out_shape=(held(192, length), shape(8, length, dtype=F32), held(4, 512, 768)),
            in_specs=[smem] * 2 + [far] * 4,
            out_specs=(vmem,) * 3,
            scratch_shapes=[
                pltpu.VMEM((192, 768), BF16),
                pltpu.VMEM((3, 128, length), BF16),
                pltpu.VMEM((3, length, 128), BF16),
                pltpu.VMEM((3, 80, length), BF16),
                pltpu.VMEM((3, 1, BLK), F32),
                pltpu.VMEM((3, 80, BLK), F32),
                *[pltpu.VMEM((3, BLK, BLK), F32)] * 2,
                *[pltpu.VMEM((3, BLK, BLK), BF16)] * 2,
                *[pltpu.VMEM((3, 1, BLK), F32)] * 2,
                pltpu.SMEM((72,), jnp.int32),
                dma(4),
            ],
            compiler_params=params(62),
            cost_estimate=pl.CostEstimate(flops=20_000_000_000, bytes_accessed=24_000_000, transcendentals=6_000_000),
        )(first, end, w, qa, ka, va)

        plane = (3, 2, 3, 48, 768)
        out, gz1, gb, sums, keep_a, keep_b, send_a, send_b, zs = pl.pallas_call(
            feed_forward_kernel,
            name="feed_forward",
            out_shape=(
                shape(512, 768), shape(512, 768, dtype=F32), held(4, 512, 768), shape(8, 768, dtype=F32),
                *(held(*plane),) * 4, shape(2, 3, 48, 768),
            ),
            in_specs=[far, far, hbm, vmem, vmem] + [far] * 5,
            out_specs=(vmem, vmem, far, vmem) + (far,) * 4 + (vmem,),
            scratch_shapes=[
                pltpu.VMEM((4, 512, 768), BF16),
                pltpu.VMEM((512, 768), BF16),
                pltpu.VMEM((4, 3, 768, 768), BF16),
                pltpu.VMEM((4, 512, 768), BF16),
                pltpu.VMEM((4, 512, 768), BF16),
                pltpu.VMEM((4, 512, 768), BF16),
                pltpu.VMEM((512, 768), BF16),
                pltpu.VMEM((768, 512), BF16),
                pltpu.VMEM((512, 768), BF16),
                pltpu.VMEM((768, 512), BF16),
                pltpu.VMEM((512, 768), F32),
                pltpu.VMEM((512, 768), F32),
                pltpu.VMEM((512, 128), F32),
                pltpu.VMEM((2, 3, 768, 768), BF16),
                pltpu.VMEM((4, 4, 3, 96, 768), BF16),
                pltpu.VMEM((512, 768), BF16),
                pltpu.VMEM((512, 768), BF16),
                pltpu.VMEM((2, 512, 768), BF16),
                pltpu.VMEM((512, 768), BF16),
                pltpu.VMEM((512, 768), BF16),
                pltpu.VMEM((2, 3, 48, 768), BF16),
                pltpu.VMEM((2, 3, 48, 768), BF16),
                pltpu.VMEM((3, 48, 768), BF16),
                pltpu.VMEM((3, 48, 768), BF16),
                dma(80), dma(80), dma(16), dma(3, 8), dma(2),
            ],
            compiler_params=params(62, 1),
            cost_estimate=pl.CostEstimate(flops=22_000_000_000, bytes_accessed=36_000_000, transcendentals=3_000_000),
        )(tok, part, cotangent[0], norm_gain, norm_bias, wf0, zb, zx, zy, zc)

        recv_a, recv_b = over(send_a, 4), over(send_b, 2)
        zr = lax.ppermute(zs, "tensor", [(i, i ^ 1) for i in range(tensor)])
        output = jnp.where(swapped, trade(out), out)[None]

        grads, part = pl.pallas_call(
            attend_backward_kernel,
            name="attend_backward",
            out_shape=(shape(768, 768), shape(4, 512, 768)),
            in_specs=[smem] * 2 + [far] * 8 + [vmem] + [far] * 2,
            out_specs=(vmem,) * 2,
            scratch_shapes=[
                pltpu.VMEM((4, 512, 768), BF16),
                pltpu.VMEM((4, 512, 768), BF16),
                pltpu.VMEM((768, 768), BF16),
                pltpu.VMEM((3, 128, length), BF16),
                pltpu.VMEM((3, length, 128), BF16),
                pltpu.VMEM((192, length), BF16),
                pltpu.VMEM((3, length, 64), BF16),
                pltpu.VMEM((192, length), BF16),
                pltpu.VMEM((32, length), F32),
                pltpu.VMEM((32, length), F32),
                pltpu.VMEM((192, length), BF16),
                pltpu.VMEM((8, length), F32),
                *[pltpu.VMEM((192, length + BLK), F32)] * 3,
                pltpu.VMEM((576, length), BF16),
                *[pltpu.VMEM((3, BLK, BLK), F32)] * 4,
                *[pltpu.VMEM((3, BLK, BLK), BF16)] * 4,
                pltpu.SMEM((72,), jnp.int32),
                dma(10),
            ],
            compiler_params=params(62),
            cost_estimate=pl.CostEstimate(flops=40_000_000_000, bytes_accessed=24_000_000, transcendentals=6_000_000),
        )(first, end, gb, tok, w, qa, ka, kt, vn, ot, logsum, cos, sin)

        spare = max(len(extra), 1)
        half = (48, 768)
        g_ff, g_attn, g_tok, sums = pl.pallas_call(
            functools.partial(finish_kernel, extra),
            name="finish",
            out_shape=(shape(3, 768, 768), shape(768, 768), shape(512, 768, dtype=F32), shape(8, 768, dtype=F32)),
            in_specs=[vmem] * 9,
            out_specs=(vmem,) * 4,
            scratch_shapes=[
                *[pltpu.VMEM((3, 3, *half), BF16)] * 4,
                pltpu.VMEM((3, 2, 3, *half), BF16),
                pltpu.VMEM((2, 3, *half), BF16),
                pltpu.VMEM((2, 3, *half), BF16),
                pltpu.VMEM((spare, 2, 2, 3, *half), BF16),
                pltpu.VMEM((2, 2, 96, 768), BF16),
                pltpu.VMEM((2, 96, 768), BF16),
                pltpu.VMEM((2, 96, 768), BF16),
                pltpu.VMEM((192, 768), BF16),
                pltpu.VMEM((192, 768), BF16),
                pltpu.VMEM((spare, 2, 192, 768), BF16),
                pltpu.VMEM((2, 512, 768), BF16),
                pltpu.VMEM((512, 768), BF16),
                pltpu.VMEM((512, 768), BF16),
                pltpu.VMEM((512, 768), BF16),
                pltpu.VMEM((512, 768), BF16),
                pltpu.VMEM((5 + spare, 8, 768), F32),
                dma(64), dma(64), dma(16 + spare), dma(16 + spare),
            ],
            compiler_params=params(62, 2),
        )(keep_a, keep_b, recv_a, recv_b, zr, grads, part, gz1, sums)

        g_qkv, g_out, g_gate_up, g_down = pl.pallas_call(
            widen_kernel,
            name="widen",
            grid=(3,),
            out_shape=(
                shape(576, 768, dtype=F32), shape(192, 768, dtype=F32), shape(768, 2, 768, dtype=F32),
                shape(768, 768, dtype=F32),
            ),
            in_specs=[
                pl.BlockSpec((192, 768), lambda i: (i, 0)),
                pl.BlockSpec((64, 768), lambda i: (9 + i, 0)),
                pl.BlockSpec((2, 256, 768), lambda i: (0, i, 0)),
                pl.BlockSpec((1, 768, 256), lambda i: (2, 0, i)),
            ],
            out_specs=(
                pl.BlockSpec((192, 768), lambda i: (i, 0)),
                pl.BlockSpec((64, 768), lambda i: (i, 0)),
                pl.BlockSpec((256, 2, 768), lambda i: (i, 0, 0)),
                pl.BlockSpec((256, 768), lambda i: (i, 0)),
            ),
            compiler_params=params(62),
            cost_estimate=pl.CostEstimate(flops=0, bytes_accessed=16_000_000, transcendentals=0),
        )(g_attn, g_attn, g_ff, g_ff)
        return (
            output, g_tok[None], g_qkv.reshape(3, 192, 768).transpose(2, 0, 1), g_out, g_gate_up, g_down,
            sums[0:2], sums[2:4],
        )

    placed = (
        P("dp", "tensor", None),
        P("dp", None),
        P(None, None, "tensor"),
        P("tensor", None),
        P(None, None, "tensor"),
        P("tensor", None),
        P(),
        P(),
        P("dp", "tensor", None),
    )
    return jax.shard_map(
        on_device,
        mesh=mesh,
        in_specs=placed,
        out_specs=(
            P("dp", "tensor", None),
            P("dp", "tensor", None),
            P(None, None, "tensor"),
            P("tensor", None),
            P(None, None, "tensor"),
            P("tensor", None),
            P(),
            P(),
        ),
        check_vma=False,
    )
```

```python
import functools
import math

import jax
import jax.numpy as jnp
import numpy as np
from jax import lax
from jax.experimental import pallas as pl
from jax.experimental.pallas import tpu as pltpu
from jax.sharding import PartitionSpec as P

HEAD_DIM = 64
SEGS = 8
BLK = 256
F32 = jnp.float32
BF16 = jnp.bfloat16
MESH = pl.DeviceIdType.MESH
CHUNKS = 4
CHUNK = 128

epsilon = 1e-05
far_below = -1e30
log_base = math.log(1000.0)


def nn(a, b):
    return lax.dot_general(a, b, (((1,), (0,)), ((), ())), preferred_element_type=F32)


def nt(a, b):
    return lax.dot_general(a, b, (((1,), (1,)), ((), ())), preferred_element_type=F32)


def tn(a, b):
    return lax.dot_general(a, b, (((0,), (0,)), ((), ())), preferred_element_type=F32)


class Place:
    def __init__(self):
        p, z = lax.axis_index("dp"), lax.axis_index("tensor")
        self.p, self.z = p, z
        c, x, y = p % 2, (p // 2) % 2, (p // 4) % 2
        self.c, self.x, self.y = c, x, y
        self.place = p % 8
        self.x_place = self.place + 2 - 4 * x
        self.y_place = self.place + 4 - 8 * y
        self.d_place = self.x_place + 4 - 8 * y
        self.z1_at, self.z2_at = z + 1 - 2 * (z % 2), (z + 2) % 4
        self.sib = {"dp": p + 1 - 2 * c}
        self.xn = {"dp": p + 2 - 4 * x}
        self.yn = {"dp": p + 4 - 8 * y}
        self.z1 = {"tensor": self.z1_at}
        self.z2 = {"tensor": self.z2_at}
        self.pair = {"dp": p + 1 - 2 * c, "tensor": self.z2_at}
        self.cross = c + z // 2 - 2 * c * (z // 2)
        self.slot = (z + 2 * self.cross) % 4
        self.slot1 = self.slot + 1 - 2 * (self.slot % 2)
        self.slot2 = (self.slot + 2) % 4
        self.slot3 = (self.slot1 + 2) % 4


def greet(partners):
    barrier = pltpu.get_barrier_semaphore()
    for partner in partners:
        pl.semaphore_signal(barrier, inc=1, device_id=partner, device_id_type=MESH)
    pl.semaphore_wait(barrier, len(partners))


class Links:
    def __init__(self, send, recv):
        self.send, self.recv, self.count, self.started = send, recv, 0, []

    def make(self, src, dst, to):
        i = self.count
        self.count += 1
        return pltpu.make_async_remote_copy(
            src_ref=src, dst_ref=dst, send_sem=self.send.at[i], recv_sem=self.recv.at[i], device_id=to, device_id_type=MESH
        )

    def start(self, src, dst, to):
        copy = self.make(src, dst, to)
        copy.start()
        self.started.append(copy)
        return copy

    def wait_sends(self):
        for copy in self.started:
            copy.wait_send()


class Spread:
    def __init__(self, me, links, view, src=None):
        self.me, self.links, self.view = me, links, view
        own = view(me.place, 0, 96)
        src = own if src is None else src
        self.from_x = links.start(src, own, me.xn)
        self.from_y = links.start(src, own, me.yn)
        self.from_sib = [links.start(src, own, me.sib)]

    def second(self):
        me, links, view = self.me, self.links, self.view
        self.from_x.wait_recv()
        part = view(me.x_place, 0, 48)
        self.low = links.start(part, part, me.yn)
        block = view(me.x_place, 0, 96)
        self.from_sib.append(links.start(block, block, me.sib))
        self.from_y.wait_recv()
        part = view(me.y_place, 48, 48)
        self.high = links.start(part, part, me.xn)
        block = view(me.y_place, 0, 96)
        self.from_sib.append(links.start(block, block, me.sib))

    def third(self):
        me, links, view = self.me, self.links, self.view
        self.low.wait_recv()
        self.high.wait_recv()
        block = view(me.d_place, 0, 96)
        self.from_sib.append(links.start(block, block, me.sib))

    def last(self):
        for copy in self.from_sib:
            copy.wait_recv()


class Corner(Spread):
    def __init__(self, me, links, view, own, from_x, from_y):
        self.me, self.links, self.view = me, links, view
        first, last = pl.ds(0, 48), pl.ds(48, 48)
        self.low = links.start(from_x.at[:, first], view(me.x_place, 0, 48), me.yn)
        self.high = links.start(from_y.at[:, last], view(me.y_place, 48, 48), me.xn)
        self.from_sib = [
            links.start(src, view(place, 0, 96), me.sib)
            for src, place in ((own, me.place), (from_x, me.x_place), (from_y, me.y_place))
        ]


def view_2d(ref):
    return lambda place, first, size: ref.at[pl.ds(pl.multiple_of(place * 96 + first, 16), size)]


def view_3d(ref):
    return lambda place, first, size: ref.at[:, pl.ds(pl.multiple_of(place * 96 + first, 16), size)]


class Moves:
    def __init__(self, sems):
        self.sems, self.count = sems, 0

    def start(self, src, dst):
        copy = pltpu.make_async_copy(src, dst, self.sems.at[self.count])
        self.count += 1
        copy.start()
        return copy


def start_kernel(
    x, w_qkv, w_out, fb, near_row, inverse,
    tok, w, wf0, zb, zl, qa_out, ka_out, kt_out, vn_out, va_out, cos_out, sin_out, seg, first, end,
    wo, zv, tv, wx, wv, far_row, cos, sin, qa, ka, kt, vn, va, token_send, token_recv, send, recv, local,
):
    me = Place()
    moves = Moves(local)
    wo_here = [moves.start(w_qkv, wo.at[pl.ds(0, 576)]), moves.start(w_out, wo.at[pl.ds(576, 192)])]
    c, z = me.c, me.z
    away = z + c * (3 - 2 * z)

    barrier = pltpu.get_barrier_semaphore()
    partners = (me.sib, me.xn, me.yn, me.z1, me.z2)
    for partner in partners:
        pl.semaphore_signal(barrier, inc=1, device_id=partner, device_id_type=MESH)
    @pl.when(z % 3 != 0)
    def _():
        pl.semaphore_signal(barrier, inc=1, device_id={"tensor": 3 - z}, device_id_type=MESH)

    pl.semaphore_wait(barrier, len(partners) + z * (3 - z) // 2)

    def line(k):
        return k + c * (3 - 2 * k)

    def line_sib(k):
        return k + (1 - c) * (3 - 2 * k)

    far, near = {"tensor": line(0)}, {"tensor": line(1)}

    def part(ch):
        return pl.ds(ch * CHUNK, CHUNK)

    def copy(kind, k, ch, src, to):
        return pltpu.make_async_remote_copy(
            src_ref=src, dst_ref=tv.at[line(k), part(ch)],
            send_sem=token_send.at[kind, k, ch],
            recv_sem=token_recv.at[k, ch], device_id=to, device_id_type=MESH,
        )

    def own(ch):
        return x.at[part(ch)]

    def held(k, ch):
        return tv.at[line(k), part(ch)]

    links = Links(send, recv)
    rows_far = links.start(near_row, far_row, me.sib)
    for load in wo_here:
        load.wait()
    attn_z = links.start(view_2d(wo)(me.place, 0, 96), view_2d(wx)(me.place, 0, 96), me.z2)
    ff_z1 = links.make(fb, zb.at[0], me.z1)
    ff_z2 = links.make(fb, zv, me.z2)
    for k, to in ((0, near), (1, far), (2, near), (3, near)):

        @pl.when(away == k)
        def _(k=k, to=to):
            for ch in range(CHUNKS):
                copy(0, k, ch, own(ch), to).start()
                if k < 2:
                    copy(1, k, ch, own(ch), me.sib).start()

    ff_z1.start()
    links.started.append(ff_z1)
    ff_z2.start()
    links.started.append(ff_z2)
    ff0 = Spread(me, links, view_3d(wf0), fb)
    here = moves.start(fb, view_3d(wf0)(me.place, 0, 96))

    @pl.when(away < 2)
    def _():
        mine = pltpu.make_async_copy(x, tv.at[z], local.at[30])
        mine.start()
        mine.wait()

    def forward(ch):
        @pl.when(away == 0)
        def _():
            for k in (1, 2, 3):
                copy(1, k, ch, held(k, ch), me.sib).wait_recv()
                copy(1, k, ch, held(k, ch), me.sib).start()

        @pl.when(away == 1)
        def _():
            for k in (2, 3, 0):
                copy(1, k, ch, held(k, ch), me.sib).wait_recv()
                if k:
                    copy(0, k, ch, held(k, ch), far).start()
                copy(1, k, ch, held(k, ch), me.sib).start()

    def documents():
        rows_far.wait_recv()
        row = jnp.where(me.cross == 1, far_row[...], near_row[...])
        seg[...] = row
        opened = jnp.zeros(row.shape, F32)
        closed = jnp.zeros(row.shape, F32)
        before = jnp.zeros((1, 1), F32)
        for d in range(SEGS):
            here = (row == d).astype(F32)
            opened += here * before
            before = before + jnp.sum(here, axis=1, keepdims=True)
            closed += here * before
        first[...] = opened.astype(jnp.int32)
        end[...] = closed.astype(jnp.int32)
        places = lax.broadcasted_iota(jnp.int32, row.shape, 1).astype(F32) - opened
        for e in range(4):
            at = slice(e * 512, (e + 1) * 512)
            angles = inverse[...] * places[:, at]
            cos[:, at] = jnp.cos(angles)
            sin[:, at] = jnp.sin(angles)

    attn_z.wait_recv()
    attn = Spread(me, links, view_2d(wx))
    documents()
    forward(0)
    attn.second()
    forward(1)
    attn.third()
    ff0.second()
    forward(2)
    forward(3)
    ff0.third()

    @pl.when(away >= 2)
    def _():
        for ch in range(CHUNKS):
            for k in range(4):
                pltpu.make_async_remote_copy(
                    src_ref=own(ch), dst_ref=tv.at[line_sib(k), part(ch)], send_sem=token_send.at[0, k, ch],
                    recv_sem=token_recv.at[k, ch], device_id=me.sib, device_id_type=MESH,
                ).wait_recv()

    attn.last()

    def chosen(src):
        return pltpu.make_async_copy(src, wv, local.at[31])

    @pl.when(me.cross == 0)
    def _():
        chosen(wo).start()

    @pl.when(me.cross == 1)
    def _():
        chosen(wx).start()

    chosen(wx).wait()
    moved = [here, moves.start(tv, tok), moves.start(wv, w), moves.start(cos, cos_out), moves.start(sin, sin_out)]

    heads = 3
    width = heads * HEAD_DIM

    def project(e, _):
        at = pl.ds(pl.multiple_of(e * 512, 512), 512)
        made = nt(wv[: 3 * width], tv[e])
        c_, s_ = cos[:, at], sin[:, at]
        hot = (seg[:, at] == lax.broadcasted_iota(jnp.int32, (SEGS, 512), 0)).astype(F32)
        rest = jnp.zeros((64 - SEGS, 512), F32)
        one_row = (lax.broadcasted_iota(jnp.int32, (16, 512), 0) == 0).astype(F32)
        for h in range(heads):
            r = h * HEAD_DIM
            a1, a2 = made[r : r + 32], made[r + 32 : r + 64]
            q = jnp.concatenate([a1 * c_ - a2 * s_, a2 * c_ + a1 * s_], axis=0).astype(BF16).astype(F32)
            qa[h, :, at] = jnp.concatenate([q * 0.125, hot, rest], axis=0).astype(BF16)
            r += width
            a1, a2 = made[r : r + 32], made[r + 32 : r + 64]
            k = jnp.concatenate([a1 * c_ - a2 * s_, a2 * c_ + a1 * s_], axis=0)
            kt[h * HEAD_DIM : (h + 1) * HEAD_DIM, at] = k.astype(BF16)
            ka[h, at, :] = jnp.concatenate([k, (1.0 - hot) * far_below, rest], axis=0).T.astype(BF16)
            r += width
            v = made[r : r + 64]
            va[h, :, at] = jnp.concatenate([v, one_row], axis=0).astype(BF16)
            vn[h, at, :] = jnp.concatenate([v, jnp.zeros_like(v)], axis=0).T[:, :HEAD_DIM].astype(BF16)
        return 0

    lax.fori_loop(0, 4, project, 0)
    for src, dst in ((qa, qa_out), (ka, ka_out), (kt, kt_out), (vn, vn_out), (va, va_out)):
        moved.append(moves.start(src, dst))
    ff0.last()
    ff_z2.wait_recv()
    moved += [moves.start(zv, zb.at[1]), moves.start(zv, zl)]
    ff_z1.wait_recv()
    for move in moved:
        move.wait()
    links.wait_sends()
    for k, to in ((0, near), (1, far), (2, near), (3, near)):

        @pl.when(away == k)
        def _(k=k, to=to):
            for ch in range(CHUNKS):
                copy(0, k, ch, own(ch), to).wait_send()
                if k == 1:
                    for j in (2, 3):
                        copy(0, j, ch, held(j, ch), to).wait_send()
                if k < 2:
                    for j in range(4):
                        copy(1, j, ch, own(ch) if j == k else held(j, ch), me.sib).wait_send()


FIRST, LAST = 256, 512


def list_pairs(first, end, pairs):
    idle = 8 * 16 + 8
    pairs[0] = idle

    def of_query(i, n):
        lo = first[0, i * BLK] // BLK
        hi = (end[0, i * BLK + BLK - 1] + (BLK - 1)) // BLK

        def of_key(j, n):
            pairs[n] = i * 16 + j + jnp.where(j == lo, FIRST, 0) + jnp.where(j == hi - 1, LAST, 0)
            return n + 1

        return lax.fori_loop(lo, hi, of_key, n)

    n = lax.fori_loop(0, 2048 // BLK, of_query, 1)
    for more in range(3):
        pairs[n + more] = idle
    return n - 1


def split_pair(code):
    return (code // 16) % 16, code % 16


def columns(block):
    return pl.ds(pl.multiple_of(block * BLK, BLK), BLK)


def real(block):
    return jnp.where(block == 8, 0, block)


def attend_forward_kernel(
    first, end, w_in, qa_in, ka_in, va_in, ot, logsum, part,
    w, qa, ka, va, mx, acc, s0, s1, p0, p1, al0, al1, pairs, sem,
):
    heads = 3
    width = heads * HEAD_DIM
    moves = Moves(sem)
    loads = [moves.start(src, dst) for src, dst in ((qa_in, qa), (ka_in, ka), (va_in, va), (w_in.at[pl.ds(3 * width, width)], w))]
    count = list_pairs(first, end, pairs)

    def score(t, s):
        i, j = split_pair(pairs[t])
        at, here = columns(real(i)), columns(real(j))
        for h in range(heads):
            s[h] = nn(ka[h, here, :], qa[h, :, at])

    def weigh(t, s, p, al):
        fresh = pairs[t] & FIRST
        for h in range(heads):
            scores = s[h]
            before = jnp.where(fresh > 0, -3e38, mx[h])
            largest = jnp.maximum(before, jnp.max(scores, axis=0, keepdims=True))
            p[h] = jnp.exp(scores - largest).astype(BF16)
            al[h] = jnp.exp(before - largest)
            mx[h] = largest

    def gather(t, p, al):
        code = pairs[t]
        i, j = split_pair(code)
        here = columns(real(j))
        for h in range(heads):
            acc[h] = acc[h] * al[h] + nn(va[h, :, here], p[h])

        @pl.when((code & LAST) > 0)
        def _():
            at = columns(i)
            for h in range(heads):
                total = acc[h, 64:65, :]
                ot[h * HEAD_DIM : (h + 1) * HEAD_DIM, at] = (acc[h, :64, :] / total).astype(BF16)
                logsum[pl.ds(h, 1), at] = mx[h] + jnp.log(total)

    def step(u, _):
        t = 2 * u + 1
        gather(t - 1, p1, al1)
        weigh(t, s0, p0, al0)
        score(t + 1, s1)
        gather(t, p0, al0)
        weigh(t + 1, s1, p1, al1)
        score(t + 2, s0)
        return 0

    acc[...] = jnp.zeros_like(acc)
    p1[...] = jnp.zeros_like(p1)
    al1[...] = jnp.zeros_like(al1)
    for load in loads:
        load.wait()
    score(1, s0)
    lax.fori_loop(0, (count + 2) // 2, step, 0)
    for e in range(4):
        part[e] = tn(ot[:, e * 512 : (e + 1) * 512], w[...]).astype(BF16)


def attend_backward_kernel(
    first, end, gb_in, tok_in, w_in, qa_in, ka_in, kt_in, vn_in, ot_in, logsum, cos_in, sin_in, grads, part,
    gb, tok, w, qa, ka, kt, vn, ot, cos, sin, dot_, inner, dq, dk, dv, gp, s0, s1, r0, r1, p0, p1, d0, d1, pairs, sem,
):
    heads = 3
    width = heads * HEAD_DIM
    moves = Moves(sem)
    loads = [
        moves.start(src, dst)
        for src, dst in (
            (w_in, w), (ot_in, ot), (gb_in, gb), (qa_in, qa), (ka_in, ka), (vn_in, vn), (kt_in, kt), (cos_in, cos),
            (sin_in, sin), (tok_in, tok),
        )
    ]
    for total in (dq, dk, dv, p1, d1):
        total[...] = jnp.zeros_like(total)
    count = list_pairs(first, end, pairs)
    for load in loads[:3]:
        load.wait()

    def begin(e, _):
        at = pl.ds(pl.multiple_of(e * 512, 512), 512)
        made = nt(w[3 * width :], gb[e]).astype(BF16)
        dot_[:, at] = made
        product = made.astype(F32) * ot[:, at].astype(F32)
        for h in range(heads):
            inner[pl.ds(h, 1), at] = jnp.sum(product[h * HEAD_DIM : (h + 1) * HEAD_DIM], axis=0, keepdims=True)
        return 0

    lax.fori_loop(0, 4, begin, 0)
    for load in loads[3:]:
        load.wait()

    def score(t, s, r):
        i, j = split_pair(pairs[t])
        at, here = columns(real(i)), columns(real(j))
        for h in range(heads):
            rows = slice(h * HEAD_DIM, (h + 1) * HEAD_DIM)
            s[h] = nn(ka[h, here, :], qa[h, :, at])
            r[h] = nn(vn[h, here, :], dot_[rows, at])

    def weigh(t, s, r, p, d):
        at = columns(real(split_pair(pairs[t])[0]))
        for h in range(heads):
            probability = jnp.exp(s[h] - logsum[pl.ds(h, 1), at])
            p[h] = probability.astype(BF16)
            d[h] = (probability * (r[h] - inner[pl.ds(h, 1), at])).astype(BF16)

    def gather(t, p, d):
        i, j = split_pair(pairs[t])
        at, here = columns(real(i)), columns(real(j))
        to_query, to_key = columns(i), columns(j)
        for h in range(heads):
            rows = slice(h * HEAD_DIM, (h + 1) * HEAD_DIM)
            dv[rows, to_key] += nt(dot_[rows, at], p[h])
            dk[rows, to_key] += nt(qa[h, :HEAD_DIM, at], d[h])
            dq[rows, to_query] += nn(kt[rows, here], d[h])

    def step(u, _):
        t = 2 * u + 1
        gather(t - 1, p1, d1)
        weigh(t, s0, r0, p0, d0)
        score(t + 1, s1, r1)
        gather(t, p0, d0)
        weigh(t + 1, s1, r1, p1, d1)
        score(t + 2, s0, r0)
        return 0

    score(1, s0, r0)
    lax.fori_loop(0, (count + 2) // 2, step, 0)

    def turn(e, _):
        at = pl.ds(pl.multiple_of(e * 512, 512), 512)
        c, s = cos[:, at], sin[:, at]
        for h in range(heads):
            r = h * HEAD_DIM
            for first, total, scale in ((0, dq, 0.125), (width, dk, 1.0)):
                d1_, d2_ = total[r : r + 32, at] * scale, total[r + 32 : r + 64, at] * scale
                gp[first + r : first + r + 64, at] = jnp.concatenate(
                    [d1_ * c + d2_ * s, d2_ * c - d1_ * s], axis=0
                ).astype(BF16)
        gp[2 * width :, at] = dv[:, at].astype(BF16)
        return 0

    lax.fori_loop(0, 4, turn, 0)
    for e in range(4):
        part[e] = tn(gp[:, e * 512 : (e + 1) * 512], w[: 3 * width]).astype(BF16)
    for block in range(4):
        if block < 3:
            rows = slice(block * width, (block + 1) * width)
            made = sum(nn(gp[rows, e * 512 : (e + 1) * 512], tok[e]) for e in range(4))
        else:
            made = sum(nn(ot[:, e * 512 : (e + 1) * 512], gb[e]) for e in range(4))
        grads[block * width : (block + 1) * width] = made.astype(BF16)


def row_mean(v):
    return jnp.mean(v, axis=-1, keepdims=True)


def norm_forward(summed):
    centred = summed - row_mean(summed)
    inverse = lax.rsqrt(row_mean(centred * centred) + epsilon)
    return centred * inverse, inverse


def norm_backward(scaled, normalized, inverse):
    return inverse * (scaled - row_mean(scaled) - normalized * row_mean(scaled * normalized))


def feed_forward_kernel(
    tok, part_in, cot_in, gain, bias, wf0, zb, zx, zy, zc,
    out, gz1, gb, sums, keep_a, keep_b, send_a, send_b, zs_out,
    part, own_g, w, slope_g, slope_u, hid, nb, nbt, gm, gmt, total, norm1, inv1, dw, lw, xs, cot, from_core, from_z, to_z,
    f1a, f1b, f2a, f2b, send, recv, local, out_sem, trade_sem,
):
    me = Place()
    greet((me.sib, me.xn, me.yn, me.z1, me.pair))
    links = Links(send, recv)
    moves = Moves(local)
    partial = moves.start(part_in, part)
    loads = [moves.start(tok.at[me.slot], xs), moves.start(wf0, w.at[0])]
    for ez in (2, 1):
        for place, src in ((me.place, zb), (me.x_place, zx), (me.y_place, zy)):
            loads.append(moves.start(src.at[ez - 1], view_3d(w.at[ez])(place, 0, 96)))
    loads.append(moves.start(zc, view_3d(w.at[3])(me.place, 0, 96)))

    def cot_here():
        return pltpu.make_async_copy(cot_in, cot, local.at[15])

    def cot_there():
        return pltpu.make_async_remote_copy(
            src_ref=cot_in, dst_ref=cot, send_sem=trade_sem.at[0], recv_sem=trade_sem.at[1], device_id=me.pair,
            device_id_type=MESH,
        )

    def rows(ch):
        return pl.ds(ch * CHUNK, CHUNK)

    partial.wait()
    cores = [
        [links.start(part.at[shard, rows(ch)], from_core.at[i, rows(ch)], me.sib) for ch in range(CHUNKS)]
        for i, shard in ((1, me.slot3), (0, me.slot2))
    ]
    ff2, ff1 = [Corner(me, links, view_3d(w.at[ez]), *(src.at[ez - 1] for src in (zb, zx, zy))) for ez in (2, 1)]
    ff3 = Spread(me, links, view_3d(w.at[3]), zc)
    zs = []
    for ch in range(CHUNKS):
        cores[0][ch].wait_recv()
        at = rows(ch)
        to_z[at] = (part[me.slot1, at].astype(F32) + from_core[1, at].astype(F32)).astype(BF16)
        zs.append(links.start(to_z.at[at], from_z.at[at], me.z1))

    @pl.when(me.cross == 0)
    def _():
        cot_here().start()

    @pl.when(me.cross == 1)
    def _():
        cot_there().start()

    ff2.third()
    ff1.third()
    loads[0].wait()
    for ch in range(CHUNKS):
        if ch == CHUNKS - 1:
            ff3.second()
        cores[1][ch].wait_recv()
        zs[ch].wait_recv()
        at = rows(ch)
        branch = part[me.slot, at].astype(F32) + from_core[0, at].astype(F32) + from_z[at].astype(F32)
        n1, i1 = norm_forward(xs[at].astype(F32) + branch)
        norm1[at] = n1
        inv1[at] = jnp.broadcast_to(i1, (CHUNK, 128))
        normed = n1 * gain[0:1, :] + bias[0:1, :]
        total[at] = normed
        nb[at] = normed.astype(BF16)
        nbt[:, ch * CHUNK : (ch + 1) * CHUNK] = normed.T.astype(BF16)

    def forward(ez):
        gate = nn(nb[...], w[ez, 0])
        up = nn(nb[...], w[ez, 1])
        sig = 1.0 / (1.0 + jnp.exp(-gate))
        active = gate * sig
        low = (active * up).astype(BF16)
        hid[ez] = low
        slope_u[ez] = active.astype(BF16)
        slope_g[ez] = (up * sig * (1.0 + gate * (1.0 - sig))).astype(BF16)
        total[...] += nn(low, w[ez, 2])

    loads[1].wait()
    forward(0)
    for load in loads[2:]:
        load.wait()
    ff2.last()
    forward(2)
    ff3.third()
    ff1.last()
    forward(1)
    ff3.last()
    forward(3)
    n2, i2 = norm_forward(total[...])
    out[...] = (n2 * gain[1:2, :] + bias[1:2, :]).astype(BF16)

    @pl.when(me.cross == 0)
    def _():
        cot_here().wait()

    @pl.when(me.cross == 1)
    def _():
        cot_there().wait()

    g = cot[...].astype(F32)
    sums[1:2, :] = jnp.sum(g * n2, axis=0, keepdims=True)
    sums[3:4, :] = jnp.sum(g, axis=0, keepdims=True)
    gz2 = norm_backward(g * gain[1:2, :], n2, i2)
    total[...] = gz2
    gm[...] = gz2.astype(BF16)
    gmt[...] = gz2.T.astype(BF16)

    def block(quad, core):
        return pl.ds(pl.multiple_of((quad * 2 + core) * 96, 32), 96)

    order = (3, 1, 0, 2)
    halves = []
    first, last = pl.ds(0, 48), pl.ds(48, 48)

    def slopes(ez):
        grad_hidden = nt(gm[...], w[ez, 2])
        gate = (grad_hidden * slope_g[ez].astype(F32)).astype(BF16)
        up = (grad_hidden * slope_u[ez].astype(F32)).astype(BF16)
        slope_g[ez] = gate
        slope_u[ez] = up
        total[...] += nt(gate, w[ez, 0]) + nt(up, w[ez, 1])

    def weights(n):
        i, ez = n % 2, order[n]
        if n >= 2:
            for copy in halves[n - 2]:
                copy.wait_send()
        dw[i, 2] = nn(gmt[...], hid[ez]).astype(BF16)
        dw[i, 0] = nn(nbt[...], slope_g[ez]).astype(BF16)
        dw[i, 1] = nn(nbt[...], slope_u[ez]).astype(BF16)
        halves.append([links.make(dw.at[i, :, block(quad, 1 - me.c)], lw.at[n, quad], me.sib) for quad in range(4)])
        for copy in halves[n]:
            copy.start()

    def settle(n):
        for quad in range(4):
            halves[n][quad].wait_recv()
            for m in range(3):
                lw[n, quad, m] = (lw[n, quad, m].astype(F32) + dw[n % 2, m, block(quad, me.c)].astype(F32)).astype(BF16)

    def plane_first():
        return [
            (
                links.start(lw.at[0, (1 - me.y) * 2 + o, :, first], f1a.at[o], me.yn),
                links.start(lw.at[0, o * 2 + 1 - me.x, :, last], f1b.at[o], me.xn),
            )
            for o in range(2)
        ]

    def plane_second(plane_1):
        for o in range(2):
            plane_1[o][0].wait_recv()
            f1a[o] = (f1a[o].astype(F32) + lw[0, me.y * 2 + o, :, first].astype(F32)).astype(BF16)
            plane_1[o][1].wait_recv()
            f1b[o] = (f1b[o].astype(F32) + lw[0, o * 2 + me.x, :, last].astype(F32)).astype(BF16)
        return links.start(f1a.at[1 - me.x], f2a, me.xn), links.start(f1b.at[1 - me.y], f2b, me.yn)

    def plane_last(plane_2):
        plane_2[0].wait_recv()
        zs_out[0] = (f1a[me.x].astype(F32) + f2a[...].astype(F32)).astype(BF16)
        plane_2[1].wait_recv()
        zs_out[1] = (f1b[me.y].astype(F32) + f2b[...].astype(F32)).astype(BF16)

    def stores(n):
        made = []
        for oy in range(2):
            for ox in range(2):
                src = lw.at[n, oy * 2 + ox]
                made.append((me.y == oy, src.at[:, first], keep_a.at[n - 1, ox], send_a.at[n - 1, ox]))
                made.append((me.x == ox, src.at[:, last], keep_b.at[n - 1, oy], send_b.at[n - 1, oy]))
        return made

    def store(n):
        for number, (here, src, kept, sent) in enumerate(stores(n)):

            @pl.when(here)
            def _(number=number, src=src, kept=kept):
                pltpu.make_async_copy(src, kept, out_sem.at[n - 1, number]).start()

            @pl.when(jnp.logical_not(here))
            def _(number=number, src=src, sent=sent):
                pltpu.make_async_copy(src, sent, out_sem.at[n - 1, number]).start()

    slopes(3)
    weights(0)
    slopes(1)
    slopes(0)
    settle(0)
    plane_1 = plane_first()
    slopes(2)
    g = total[...]
    sums[0:1, :] = jnp.sum(g * norm1[...], axis=0, keepdims=True)
    sums[2:3, :] = jnp.sum(g, axis=0, keepdims=True)
    sums[4:8, :] = jnp.zeros((4, 768), F32)
    to_pair, to_core, on_core = [], [], []
    for ch in range(CHUNKS):
        at = rows(ch)
        made = norm_backward(total[at] * gain[0:1, :], norm1[at], inv1[at, 0:1])
        gz1[at] = made
        own_g[at] = made.astype(BF16)
        mine = gb.at[me.slot, at]
        to_pair.append(links.start(own_g.at[at], mine, me.z1))
        to_core.append(links.start(own_g.at[at], mine, me.sib))
    kept_g = moves.start(own_g, gb.at[me.slot])
    weights(1)
    weights(2)
    settle(1)
    store(1)
    plane_2 = plane_second(plane_1)
    weights(3)
    settle(2)
    store(2)
    settle(3)
    store(3)
    for ch in range(CHUNKS):
        to_pair[ch].wait_recv()
        other = gb.at[me.slot1, rows(ch)]
        on_core.append(links.start(other, other, me.sib))
    plane_last(plane_2)
    kept_g.wait()
    for copy in to_core + on_core:
        copy.wait_recv()
    for n in (1, 2, 3):
        for number, (_, src, kept, _) in enumerate(stores(n)):
            pltpu.make_async_copy(src, kept, out_sem.at[n - 1, number]).wait()
    for n in (2, 3):
        for copy in halves[n]:
            copy.wait_send()
    links.wait_sends()


def finish_kernel(
    extra, keep_a_in, keep_b_in, recv_a_in, recv_b_in, zr_in, ga_in, part_in, gz1_in, sums_in,
    g_ff, g_attn, g_tok, sums,
    keep_a, keep_b, recv_a, recv_b, zr, ga, part, gz1, block,
    sa, sb, f2a, f2b, va, f3, f4, fe, a_in, a_mid, a_out, a_fin, a_two, ae, from_core, from_z, to_z, trade_out, trade_in, sum_in,
    send, recv, a_send, a_recv, local,
):
    me = Place()
    moves = Moves(local)
    part_here, ga_here = moves.start(part_in, part), moves.start(ga_in, ga)
    ff_here = [
        moves.start(src, dst)
        for src, dst in ((keep_a_in, keep_a), (recv_a_in, recv_a), (keep_b_in, keep_b), (recv_b_in, recv_b), (zr_in, zr))
    ]
    gz1_here = moves.start(gz1_in, gz1)
    bits = [{"dp": me.p + bit - 2 * bit * ((me.p // bit) % 2)} for bit in extra]
    greet([me.sib, me.xn, me.yn, me.z1, me.z2, me.pair] + bits)
    links = Links(send, recv)

    def rows(ch):
        return pl.ds(ch * CHUNK, CHUNK)

    def add(*terms):
        return sum(t.astype(F32) for t in terms).astype(BF16)

    part_here.wait()
    cores = [
        [links.start(part.at[shard, rows(ch)], from_core.at[i, rows(ch)], me.sib) for ch in range(CHUNKS)]
        for i, shard in ((1, me.slot3), (0, me.slot2))
    ]

    def half(oy, ox, h):
        return pl.ds(pl.multiple_of((oy * 2 + ox) * 192 + h * 96, 32), 96)

    attn_1 = []
    ga_here.wait()
    for o in range(2):
        attn_1.append(links.start(ga.at[half(1 - me.y, o, 0)], a_in.at[0, o], me.yn))
        attn_1.append(links.start(ga.at[half(o, 1 - me.x, 1)], a_in.at[1, o], me.xn))

    sums[...] = sums_in[...]
    around = [me.sib, me.xn, me.yn, me.z1, me.z2] + bits
    small = [links.start(sums, sum_in.at[0], around[0])]

    def small_step():
        n = len(small)
        small[-1].wait_recv()
        small[-1].wait_send()
        links.started = [copy for copy in links.started if copy is not small[n - 1]]
        sums[...] += sum_in[n - 1]
        if n < len(around):
            small.append(links.start(sums, sum_in.at[n], around[n]))

    ff_2 = {}

    def plane(ez):
        sa[ez] = add(keep_a[ez, 1 - me.x], recv_a[ez, 1 - me.x])
        sb[ez] = add(keep_b[ez, 1 - me.y], recv_b[ez, 1 - me.y])
        ff_2[ez] = (links.start(sa.at[ez], f2a.at[ez], me.xn), links.start(sb.at[ez], f2b.at[ez], me.yn))

    def planed(ez):
        ff_2[ez][0].wait_recv()
        va[ez, 0] = add(keep_a[ez, me.x], recv_a[ez, me.x], f2a[ez], *([zr[0]] if ez == 2 else []))
        ff_2[ez][1].wait_recv()
        va[ez, 1] = add(keep_b[ez, me.y], recv_b[ez, me.y], f2b[ez], *([zr[1]] if ez == 2 else []))

    for load in ff_here:
        load.wait()
    plane(2)
    zs = []
    for ch in range(CHUNKS):
        cores[0][ch].wait_recv()
        at = rows(ch)
        to_z[at] = add(part[me.slot1, at], from_core[1, at])
        zs.append(links.start(to_z.at[at], from_z.at[at], me.z1))
    for copy in attn_1:
        copy.wait_recv()
    small_step()
    a_mid[0] = add(ga[half(me.y, 1 - me.x, 0)], a_in[0, 1 - me.x])
    a_mid[1] = add(ga[half(1 - me.y, me.x, 1)], a_in[1, 1 - me.y])
    attn_2 = [links.start(a_mid.at[0], a_out.at[0], me.xn), links.start(a_mid.at[1], a_out.at[1], me.yn)]
    planed(2)
    ff_4 = links.start(va.at[2], f4, me.z2)
    for copy in attn_2:
        copy.wait_recv()
    small_step()
    a_fin[:96] = add(ga[half(me.y, me.x, 0)], a_in[0, me.x], a_out[0])
    a_fin[96:] = add(ga[half(me.y, me.x, 1)], a_in[1, me.y], a_out[1])

    def attn_copy(n, src, dst, to):
        return pltpu.make_async_remote_copy(
            src_ref=src, dst_ref=dst, send_sem=a_send.at[n], recv_sem=a_recv.at[n], device_id=to, device_id_type=MESH
        )

    def quarter(oy, ox, first=0, size=192):
        return g_attn.at[pl.ds(pl.multiple_of((oy * 2 + ox) * 192 + first, 32), size)]

    def attn_over():
        return attn_copy(0, a_fin, a_two, me.z2)

    @pl.when(me.cross == 1)
    def _():
        attn_over().start()

    plane(0)
    plane(1)
    planed(0)
    ff_3 = links.start(va.at[0], f3, me.z1)
    planed(1)
    small_step()

    trades = [
        pltpu.make_async_remote_copy(
            src_ref=trade_out.at[rows(ch)], dst_ref=trade_in.at[rows(ch)], send_sem=a_send.at[8 + ch],
            recv_sem=a_recv.at[8 + ch], device_id=me.pair, device_id_type=MESH,
        )
        for ch in range(CHUNKS)
    ]
    mine = quarter(me.y, me.x)

    def attn_send(n, src, to):
        return attn_copy(n, src, src, to)

    block_x, block_y = quarter(me.y, 1 - me.x), quarter(1 - me.y, me.x)
    low_x, high_y = quarter(me.y, 1 - me.x, 0, 96), quarter(1 - me.y, me.x, 96, 96)
    corner = quarter(1 - me.y, 1 - me.x)

    @pl.when(me.cross == 0)
    def _():
        attn_over().wait_recv()
        total = add(a_fin[...], a_two[...])
        for n, bit in enumerate(bits):
            ae[n, 0] = total
            step = attn_copy(16 + n, ae.at[n, 0], ae.at[n, 1], bit)
            step.start()
            step.wait()
            total = add(total, ae[n, 1])
        g_attn[pl.ds(pl.multiple_of((me.y * 2 + me.x) * 192, 32), 192)] = total
        attn_send(1, mine, me.xn).start()
        attn_send(2, mine, me.yn).start()
        attn_send(3, mine, me.sib).start()

    gz1_here.wait()
    for ch in range(CHUNKS):
        cores[1][ch].wait_recv()
        zs[ch].wait_recv()
        at = rows(ch)
        got = gz1[at] + (part[me.slot, at].astype(F32) + from_core[0, at].astype(F32) + from_z[at].astype(F32))

        @pl.when(me.cross == 0)
        def _(at=at, got=got):
            g_tok[at] = got

        @pl.when(me.cross == 1)
        def _(at=at, got=got, ch=ch):
            trade_out[at] = got.astype(BF16)

    small_step()


    @pl.when(me.cross == 0)
    def _():
        attn_send(1, block_x, me.xn).wait_recv()
        attn_send(4, low_x, me.yn).start()
        attn_send(5, block_x, me.sib).start()
        attn_send(2, block_y, me.yn).wait_recv()
        attn_send(6, high_y, me.xn).start()
        attn_send(7, block_y, me.sib).start()

    ff_3.wait_recv()
    ff_4.wait_recv()
    total = add(va[1], f3[...], f4[...])
    for n, bit in enumerate(bits):
        fe[n, 0] = total
        step = links.start(fe.at[n, 0], fe.at[n, 1], bit)
        step.wait_recv()
        total = add(total, fe[n, 1])
    for h in range(2):
        block[:, h * 48 : (h + 1) * 48] = total[h]
    spread = Spread(me, links, view_3d(g_ff), block)
    kept = moves.start(block, view_3d(g_ff)(me.place, 0, 96))

    @pl.when(me.cross == 1)
    def _():
        for ch in range(CHUNKS):
            trades[ch].start()

    while len(small) < len(around):
        small_step()
    spread.second()
    small_step()

    @pl.when(me.cross == 0)
    def _():
        attn_send(4, low_x, me.yn).wait_recv()
        attn_send(6, high_y, me.xn).wait_recv()
        attn_send(12, corner, me.sib).start()
        for n, src, to in (
            (1, mine, me.xn), (2, mine, me.yn), (3, mine, me.sib), (4, low_x, me.yn), (5, block_x, me.sib),
            (6, high_y, me.xn), (7, block_y, me.sib), (12, corner, me.sib),
        ):
            attn_send(n, src, to).wait_send()

    @pl.when(me.cross == 1)
    def _():
        for ch in range(CHUNKS):
            trades[ch].wait_recv()
            g_tok[rows(ch)] = trade_in[rows(ch)].astype(F32)
        attn_over().wait_send()
        for n, src in ((3, mine), (5, block_x), (7, block_y), (12, corner)):
            attn_send(n, src, me.sib).wait_recv()
        for ch in range(CHUNKS):
            trades[ch].wait_send()

    spread.third()
    spread.last()
    kept.wait()
    links.wait_sends()


def widen_kernel(attn, out_rows, gate_up, down, tok, sums, g_qkv, g_out, g_gate_up, g_down, g_tok, gains, biases):
    g_qkv[...] = attn[...].astype(F32)
    g_out[...] = out_rows[...].astype(F32)
    g_gate_up[:, 0, :] = gate_up[0].astype(F32)
    g_gate_up[:, 1, :] = gate_up[1].astype(F32)
    g_down[...] = down[0].astype(F32).T
    g_tok[0] = tok[...]
    gains[...] = sums[0:2, :]
    biases[...] = sums[2:4, :]


def solution(mesh):
    dp, tensor = mesh.shape["dp"], mesh.shape["tensor"]
    assert tensor == 4 and dp >= 8 and dp & (dp - 1) == 0
    extra = [1 << b for b in range(3, dp.bit_length() - 1)]
    both = ("dp", "tensor")

    def cell(i, k):
        return i * tensor + k

    def over(x, bit):
        return lax.ppermute(x, "dp", [(i, i ^ bit) for i in range(dp)])

    away = [(i, k) for i in range(dp) for k in range(tensor) if (i & 1) != (k >> 1)]

    def trade(x):
        return lax.ppermute(x, both, [(cell(i, k), cell(i ^ 1, k ^ 2)) for i, k in away])

    smem = pl.BlockSpec(memory_space=pltpu.SMEM)
    vmem = pl.BlockSpec(memory_space=pltpu.VMEM)
    hbm = pl.BlockSpec(memory_space=pl.ANY)

    def shape(*dims, dtype=BF16):
        return jax.ShapeDtypeStruct(dims, dtype)

    far = pl.BlockSpec(memory_space=pltpu.HBM)

    def held(*dims, dtype=BF16):
        return pltpu.HBM(dims, dtype)

    def dma(*dims):
        return pltpu.SemaphoreType.DMA(dims)

    def params(mib, number=None):
        if number is None:
            return pltpu.CompilerParams(vmem_limit_bytes=mib << 20)
        return pltpu.CompilerParams(vmem_limit_bytes=mib << 20, collective_id=number, has_side_effects=True)

    def on_device(tokens, segments, w_qkv, w_out, w_gate_up, w_down, norm_gain, norm_bias, cotangent):
        p, z = lax.axis_index("dp"), lax.axis_index("tensor")
        swapped = (p & 1) != (z >> 1)
        place = p & 7

        rows = lax.dynamic_slice(w_gate_up, (place * 96, 0, 0), (96, 2, 768))
        block = jnp.stack([rows[:, 0], rows[:, 1], lax.dynamic_slice(w_down, (place * 96, 0), (96, 768))])

        length = segments.shape[1]
        inverse = jnp.asarray(np.exp(-2.0 * np.arange(HEAD_DIM // 2) / HEAD_DIM * log_base).astype(np.float32)[:, None])
        tok, w, wf0, zb, zl, qa, ka, kt, vn, va, cos, sin, seg, first, end = pl.pallas_call(
            start_kernel,
            name="start",
            out_shape=(
                held(4, 512, 768), held(768, 768), held(3, 768, 768), held(2, 3, 96, 768), held(3, 96, 768),
                held(3, 128, length), held(3, length, 128), held(192, length), held(3, length, 64), held(3, 80, length),
                held(32, length, dtype=F32), held(32, length, dtype=F32),
                *(shape(1, length, dtype=jnp.int32),) * 3,
            ),
            in_specs=[hbm] * 3 + [vmem] * 3,
            out_specs=(far,) * 12 + (vmem,) * 3,
            scratch_shapes=[
                pltpu.VMEM((768, 768), BF16),
                pltpu.VMEM((3, 96, 768), BF16),
                pltpu.VMEM((4, 512, 768), BF16),
                pltpu.VMEM((768, 768), BF16),
                pltpu.VMEM((768, 768), BF16),
                pltpu.VMEM((1, length), jnp.int32),
                pltpu.VMEM((32, length), F32),
                pltpu.VMEM((32, length), F32),
                pltpu.VMEM((3, 128, length), BF16),
                pltpu.VMEM((3, length, 128), BF16),
                pltpu.VMEM((192, length), BF16),
                pltpu.VMEM((3, length, 64), BF16),
                pltpu.VMEM((3, 80, length), BF16),
                dma(2, 4, CHUNKS), dma(4, CHUNKS), dma(40), dma(40), dma(32),
            ],
            compiler_params=params(62, 0),
        )(tokens[0], w_qkv.transpose(1, 2, 0).reshape(576, 768), w_out, block, segments, inverse)

        zc = lax.ppermute(zl, "tensor", [(i, i ^ 1) for i in range(tensor)])
        zx, zy = over(zb, 2), over(zb, 4)

        ot, logsum, part = pl.pallas_call(
            attend_forward_kernel,
            name="attend_forward",
            out_shape=(held(192, length), shape(8, length, dtype=F32), held(4, 512, 768)),
            in_specs=[smem] * 2 + [far] * 4,
            out_specs=(vmem,) * 3,
            scratch_shapes=[
                pltpu.VMEM((192, 768), BF16),
                pltpu.VMEM((3, 128, length), BF16),
                pltpu.VMEM((3, length, 128), BF16),
                pltpu.VMEM((3, 80, length), BF16),
                pltpu.VMEM((3, 1, BLK), F32),
                pltpu.VMEM((3, 80, BLK), F32),
                *[pltpu.VMEM((3, BLK, BLK), F32)] * 2,
                *[pltpu.VMEM((3, BLK, BLK), BF16)] * 2,
                *[pltpu.VMEM((3, 1, BLK), F32)] * 2,
                pltpu.SMEM((72,), jnp.int32),
                dma(4),
            ],
            compiler_params=params(62),
            cost_estimate=pl.CostEstimate(flops=20_000_000_000, bytes_accessed=24_000_000, transcendentals=6_000_000),
        )(first, end, w, qa, ka, va)

        plane = (3, 2, 3, 48, 768)
        out, gz1, gb, sums, keep_a, keep_b, send_a, send_b, zs = pl.pallas_call(
            feed_forward_kernel,
            name="feed_forward",
            out_shape=(
                shape(512, 768), shape(512, 768, dtype=F32), held(4, 512, 768), shape(8, 768, dtype=F32),
                *(held(*plane),) * 4, shape(2, 3, 48, 768),
            ),
            in_specs=[far, far, hbm, vmem, vmem] + [far] * 5,
            out_specs=(vmem, vmem, far, vmem) + (far,) * 4 + (vmem,),
            scratch_shapes=[
                pltpu.VMEM((4, 512, 768), BF16),
                pltpu.VMEM((512, 768), BF16),
                pltpu.VMEM((4, 3, 768, 768), BF16),
                pltpu.VMEM((4, 512, 768), BF16),
                pltpu.VMEM((4, 512, 768), BF16),
                pltpu.VMEM((4, 512, 768), BF16),
                pltpu.VMEM((512, 768), BF16),
                pltpu.VMEM((768, 512), BF16),
                pltpu.VMEM((512, 768), BF16),
                pltpu.VMEM((768, 512), BF16),
                pltpu.VMEM((512, 768), F32),
                pltpu.VMEM((512, 768), F32),
                pltpu.VMEM((512, 128), F32),
                pltpu.VMEM((2, 3, 768, 768), BF16),
                pltpu.VMEM((4, 4, 3, 96, 768), BF16),
                pltpu.VMEM((512, 768), BF16),
                pltpu.VMEM((512, 768), BF16),
                pltpu.VMEM((2, 512, 768), BF16),
                pltpu.VMEM((512, 768), BF16),
                pltpu.VMEM((512, 768), BF16),
                pltpu.VMEM((2, 3, 48, 768), BF16),
                pltpu.VMEM((2, 3, 48, 768), BF16),
                pltpu.VMEM((3, 48, 768), BF16),
                pltpu.VMEM((3, 48, 768), BF16),
                dma(80), dma(80), dma(16), dma(3, 8), dma(2),
            ],
            compiler_params=params(62, 1),
            cost_estimate=pl.CostEstimate(flops=22_000_000_000, bytes_accessed=36_000_000, transcendentals=3_000_000),
        )(tok, part, cotangent[0], norm_gain, norm_bias, wf0, zb, zx, zy, zc)

        recv_a, recv_b = over(send_a, 4), over(send_b, 2)
        zr = lax.ppermute(zs, "tensor", [(i, i ^ 1) for i in range(tensor)])
        output = jnp.where(swapped, trade(out), out)[None]

        grads, part = pl.pallas_call(
            attend_backward_kernel,
            name="attend_backward",
            out_shape=(shape(768, 768), shape(4, 512, 768)),
            in_specs=[smem] * 2 + [far] * 8 + [vmem] + [far] * 2,
            out_specs=(vmem,) * 2,
            scratch_shapes=[
                pltpu.VMEM((4, 512, 768), BF16),
                pltpu.VMEM((4, 512, 768), BF16),
                pltpu.VMEM((768, 768), BF16),
                pltpu.VMEM((3, 128, length), BF16),
                pltpu.VMEM((3, length, 128), BF16),
                pltpu.VMEM((192, length), BF16),
                pltpu.VMEM((3, length, 64), BF16),
                pltpu.VMEM((192, length), BF16),
                pltpu.VMEM((32, length), F32),
                pltpu.VMEM((32, length), F32),
                pltpu.VMEM((192, length), BF16),
                pltpu.VMEM((8, length), F32),
                *[pltpu.VMEM((192, length + BLK), F32)] * 3,
                pltpu.VMEM((576, length), BF16),
                *[pltpu.VMEM((3, BLK, BLK), F32)] * 4,
                *[pltpu.VMEM((3, BLK, BLK), BF16)] * 4,
                pltpu.SMEM((72,), jnp.int32),
                dma(10),
            ],
            compiler_params=params(62),
            cost_estimate=pl.CostEstimate(flops=40_000_000_000, bytes_accessed=24_000_000, transcendentals=6_000_000),
        )(first, end, gb, tok, w, qa, ka, kt, vn, ot, logsum, cos, sin)

        spare = max(len(extra), 1)
        half = (48, 768)
        g_ff, g_attn, g_tok, sums = pl.pallas_call(
            functools.partial(finish_kernel, extra),
            name="finish",
            out_shape=(held(3, 768, 768), shape(768, 768), shape(512, 768, dtype=F32), shape(8, 768, dtype=F32)),
            in_specs=[far] * 8 + [vmem],
            out_specs=(far, vmem, vmem, vmem),
            scratch_shapes=[
                *[pltpu.VMEM((3, 2, 3, *half), BF16)] * 4,
                pltpu.VMEM((2, 3, *half), BF16),
                pltpu.VMEM((768, 768), BF16),
                pltpu.VMEM((4, 512, 768), BF16),
                pltpu.VMEM((512, 768), F32),
                pltpu.VMEM((3, 96, 768), BF16),
                *[pltpu.VMEM((3, 3, *half), BF16)] * 4,
                pltpu.VMEM((3, 2, 3, *half), BF16),
                pltpu.VMEM((2, 3, *half), BF16),
                pltpu.VMEM((2, 3, *half), BF16),
                pltpu.VMEM((spare, 2, 2, 3, *half), BF16),
                pltpu.VMEM((2, 2, 96, 768), BF16),
                pltpu.VMEM((2, 96, 768), BF16),
                pltpu.VMEM((2, 96, 768), BF16),
                pltpu.VMEM((192, 768), BF16),
                pltpu.VMEM((192, 768), BF16),
                pltpu.VMEM((spare, 2, 192, 768), BF16),
                pltpu.VMEM((2, 512, 768), BF16),
                pltpu.VMEM((512, 768), BF16),
                pltpu.VMEM((512, 768), BF16),
                pltpu.VMEM((512, 768), BF16),
                pltpu.VMEM((512, 768), BF16),
                pltpu.VMEM((5 + spare, 8, 768), F32),
                dma(64), dma(64), dma(16 + spare), dma(16 + spare), dma(9),
            ],
            compiler_params=params(62, 2),
        )(keep_a, keep_b, recv_a, recv_b, zr, grads, part, gz1, sums)

        g_qkv, g_out, g_gate_up, g_down, g_tok, gains, biases = pl.pallas_call(
            widen_kernel,
            name="widen",
            grid=(6,),
            out_shape=(
                shape(576, 768, dtype=F32), shape(192, 768, dtype=F32), shape(768, 2, 768, dtype=F32),
                shape(768, 768, dtype=F32), shape(1, 512, 768, dtype=F32), *(shape(2, 768, dtype=F32),) * 2,
            ),
            in_specs=[
                pl.BlockSpec((96, 768), lambda i: (i, 0)),
                pl.BlockSpec((32, 768), lambda i: (18 + i, 0)),
                pl.BlockSpec((2, 128, 768), lambda i: (0, i, 0)),
                pl.BlockSpec((1, 768, 128), lambda i: (2, 0, i)),
                pl.BlockSpec((128, 768), lambda i: (jnp.minimum(i, 3), 0)),
                pl.BlockSpec((8, 768), lambda i: (0, 0)),
            ],
            out_specs=(
                pl.BlockSpec((96, 768), lambda i: (i, 0)),
                pl.BlockSpec((32, 768), lambda i: (i, 0)),
                pl.BlockSpec((128, 2, 768), lambda i: (i, 0, 0)),
                pl.BlockSpec((128, 768), lambda i: (i, 0)),
                pl.BlockSpec((1, 128, 768), lambda i: (0, jnp.minimum(i, 3), 0)),
                pl.BlockSpec((2, 768), lambda i: (0, 0)),
                pl.BlockSpec((2, 768), lambda i: (0, 0)),
            ),
            compiler_params=params(62),
            cost_estimate=pl.CostEstimate(flops=0, bytes_accessed=18_000_000, transcendentals=0),
        )(g_attn, g_attn, g_ff, g_ff, g_tok, sums)
        return output, g_tok, g_qkv.reshape(3, 192, 768).transpose(2, 0, 1), g_out, g_gate_up, g_down, gains, biases

    placed = (
        P("dp", "tensor", None),
        P("dp", None),
        P(None, None, "tensor"),
        P("tensor", None),
        P(None, None, "tensor"),
        P("tensor", None),
        P(),
        P(),
        P("dp", "tensor", None),
    )
    return jax.shard_map(
        on_device,
        mesh=mesh,
        in_specs=placed,
        out_specs=(
            P("dp", "tensor", None),
            P("dp", "tensor", None),
            P(None, None, "tensor"),
            P("tensor", None),
            P(None, None, "tensor"),
            P("tensor", None),
            P(),
            P(),
        ),
        check_vma=False,
    )
```

```python
import functools
import math

import jax
import jax.numpy as jnp
import numpy as np
from jax import lax
from jax.experimental import pallas as pl
from jax.experimental.pallas import tpu as pltpu
from jax.sharding import PartitionSpec as P

HEAD_DIM = 64
SEGS = 8
BLK = 256
F32 = jnp.float32
BF16 = jnp.bfloat16
MESH = pl.DeviceIdType.MESH
CHUNKS = 4
CHUNK = 128

epsilon = 1e-05
far_below = -1e30
log_base = math.log(1000.0)


def nn(a, b):
    return lax.dot_general(a, b, (((1,), (0,)), ((), ())), preferred_element_type=F32)


def nt(a, b):
    return lax.dot_general(a, b, (((1,), (1,)), ((), ())), preferred_element_type=F32)


def tn(a, b):
    return lax.dot_general(a, b, (((0,), (0,)), ((), ())), preferred_element_type=F32)


class Place:
    def __init__(self):
        p, z = lax.axis_index("dp"), lax.axis_index("tensor")
        self.p, self.z = p, z
        c, x, y = p % 2, (p // 2) % 2, (p // 4) % 2
        self.c, self.x, self.y = c, x, y
        self.place = p % 8
        self.x_place = self.place + 2 - 4 * x
        self.y_place = self.place + 4 - 8 * y
        self.d_place = self.x_place + 4 - 8 * y
        self.z1_at, self.z2_at = z + 1 - 2 * (z % 2), (z + 2) % 4
        self.sib = {"dp": p + 1 - 2 * c}
        self.xn = {"dp": p + 2 - 4 * x}
        self.yn = {"dp": p + 4 - 8 * y}
        self.z1 = {"tensor": self.z1_at}
        self.z2 = {"tensor": self.z2_at}
        self.pair = {"dp": p + 1 - 2 * c, "tensor": self.z2_at}
        self.cross = c + z // 2 - 2 * c * (z // 2)
        self.slot = (z + 2 * self.cross) % 4
        self.slot1 = self.slot + 1 - 2 * (self.slot % 2)
        self.slot2 = (self.slot + 2) % 4
        self.slot3 = (self.slot1 + 2) % 4


def greet(partners):
    barrier = pltpu.get_barrier_semaphore()
    for partner in partners:
        pl.semaphore_signal(barrier, inc=1, device_id=partner, device_id_type=MESH)
    pl.semaphore_wait(barrier, len(partners))


class Links:
    def __init__(self, send, recv):
        self.send, self.recv, self.count, self.started = send, recv, 0, []

    def make(self, src, dst, to):
        i = self.count
        self.count += 1
        return pltpu.make_async_remote_copy(
            src_ref=src, dst_ref=dst, send_sem=self.send.at[i], recv_sem=self.recv.at[i], device_id=to, device_id_type=MESH
        )

    def start(self, src, dst, to):
        copy = self.make(src, dst, to)
        copy.start()
        self.started.append(copy)
        return copy

    def wait_sends(self):
        for copy in self.started:
            copy.wait_send()


class Spread:
    def __init__(self, me, links, view, src=None):
        self.me, self.links, self.view = me, links, view
        own = view(me.place, 0, 96)
        src = own if src is None else src
        self.from_x = links.start(src, own, me.xn)
        self.from_y = links.start(src, own, me.yn)
        self.from_sib = [links.start(src, own, me.sib)]

    def second(self):
        me, links, view = self.me, self.links, self.view
        self.from_x.wait_recv()
        part = view(me.x_place, 0, 48)
        self.low = links.start(part, part, me.yn)
        block = view(me.x_place, 0, 96)
        self.from_sib.append(links.start(block, block, me.sib))
        self.from_y.wait_recv()
        part = view(me.y_place, 48, 48)
        self.high = links.start(part, part, me.xn)
        block = view(me.y_place, 0, 96)
        self.from_sib.append(links.start(block, block, me.sib))

    def third(self):
        me, links, view = self.me, self.links, self.view
        self.low.wait_recv()
        self.high.wait_recv()
        block = view(me.d_place, 0, 96)
        self.from_sib.append(links.start(block, block, me.sib))

    def last(self):
        for copy in self.from_sib:
            copy.wait_recv()


class Corner(Spread):
    def __init__(self, me, links, view, own, from_x, from_y):
        self.me, self.links, self.view = me, links, view
        first, last = pl.ds(0, 48), pl.ds(48, 48)
        self.low = links.start(from_x.at[:, first], view(me.x_place, 0, 48), me.yn)
        self.high = links.start(from_y.at[:, last], view(me.y_place, 48, 48), me.xn)
        self.from_sib = [
            links.start(src, view(place, 0, 96), me.sib)
            for src, place in ((own, me.place), (from_x, me.x_place), (from_y, me.y_place))
        ]


def view_2d(ref):
    return lambda place, first, size: ref.at[pl.ds(pl.multiple_of(place * 96 + first, 16), size)]


def view_3d(ref):
    return lambda place, first, size: ref.at[:, pl.ds(pl.multiple_of(place * 96 + first, 16), size)]


class Moves:
    def __init__(self, sems):
        self.sems, self.count = sems, 0

    def start(self, src, dst):
        copy = pltpu.make_async_copy(src, dst, self.sems.at[self.count])
        self.count += 1
        copy.start()
        return copy


def start_kernel(
    x, w_qkv, w_out, fb, near_row, inverse,
    tok, w, wf0, zb, zl, qa_out, ka_out, kt_out, vn_out, va_out, cos_out, sin_out, seg, first, end,
    wo, zv, tv, wx, wv, far_row, cos, sin, qa, ka, kt, vn, va, token_send, token_recv, send, recv, local,
):
    me = Place()
    moves = Moves(local)
    wo_here = [moves.start(w_qkv, wo.at[pl.ds(0, 576)]), moves.start(w_out, wo.at[pl.ds(576, 192)])]
    c, z = me.c, me.z
    away = z + c * (3 - 2 * z)

    barrier = pltpu.get_barrier_semaphore()
    partners = (me.sib, me.xn, me.yn, me.z1, me.z2)
    for partner in partners:
        pl.semaphore_signal(barrier, inc=1, device_id=partner, device_id_type=MESH)
    @pl.when(z % 3 != 0)
    def _():
        pl.semaphore_signal(barrier, inc=1, device_id={"tensor": 3 - z}, device_id_type=MESH)

    pl.semaphore_wait(barrier, len(partners) + z * (3 - z) // 2)

    def line(k):
        return k + c * (3 - 2 * k)

    def line_sib(k):
        return k + (1 - c) * (3 - 2 * k)

    far, near = {"tensor": line(0)}, {"tensor": line(1)}

    def part(ch):
        return pl.ds(ch * CHUNK, CHUNK)

    def copy(kind, k, ch, src, to):
        return pltpu.make_async_remote_copy(
            src_ref=src, dst_ref=tv.at[line(k), part(ch)],
            send_sem=token_send.at[kind, k, ch],
            recv_sem=token_recv.at[k, ch], device_id=to, device_id_type=MESH,
        )

    def own(ch):
        return x.at[part(ch)]

    def held(k, ch):
        return tv.at[line(k), part(ch)]

    links = Links(send, recv)
    rows_far = links.start(near_row, far_row, me.sib)
    for load in wo_here:
        load.wait()
    attn_z = links.start(view_2d(wo)(me.place, 0, 96), view_2d(wx)(me.place, 0, 96), me.z2)
    ff_z1 = links.make(fb, zb.at[0], me.z1)
    ff_z2 = links.make(fb, zv, me.z2)
    for k, to in ((0, near), (1, far), (2, near), (3, near)):

        @pl.when(away == k)
        def _(k=k, to=to):
            for ch in range(CHUNKS):
                copy(0, k, ch, own(ch), to).start()
                if k < 2:
                    copy(1, k, ch, own(ch), me.sib).start()

    ff_z1.start()
    links.started.append(ff_z1)
    ff_z2.start()
    links.started.append(ff_z2)
    ff0 = Spread(me, links, view_3d(wf0), fb)
    here = moves.start(fb, view_3d(wf0)(me.place, 0, 96))

    @pl.when(away < 2)
    def _():
        mine = pltpu.make_async_copy(x, tv.at[z], local.at[30])
        mine.start()
        mine.wait()

    def forward(ch):
        @pl.when(away == 0)
        def _():
            for k in (1, 2, 3):
                copy(1, k, ch, held(k, ch), me.sib).wait_recv()
                copy(1, k, ch, held(k, ch), me.sib).start()

        @pl.when(away == 1)
        def _():
            for k in (2, 3, 0):
                copy(1, k, ch, held(k, ch), me.sib).wait_recv()
                if k:
                    copy(0, k, ch, held(k, ch), far).start()
                copy(1, k, ch, held(k, ch), me.sib).start()

    def documents():
        rows_far.wait_recv()
        row = jnp.where(me.cross == 1, far_row[...], near_row[...])
        seg[...] = row
        opened = jnp.zeros(row.shape, F32)
        closed = jnp.zeros(row.shape, F32)
        before = jnp.zeros((1, 1), F32)
        for d in range(SEGS):
            here = (row == d).astype(F32)
            opened += here * before
            before = before + jnp.sum(here, axis=1, keepdims=True)
            closed += here * before
        first[...] = opened.astype(jnp.int32)
        end[...] = closed.astype(jnp.int32)
        places = lax.broadcasted_iota(jnp.int32, row.shape, 1).astype(F32) - opened
        for e in range(4):
            at = slice(e * 512, (e + 1) * 512)
            angles = inverse[...] * places[:, at]
            cos[:, at] = jnp.cos(angles)
            sin[:, at] = jnp.sin(angles)

    attn_z.wait_recv()
    attn = Spread(me, links, view_2d(wx))
    documents()
    forward(0)
    attn.second()
    forward(1)
    attn.third()
    ff0.second()
    forward(2)
    forward(3)
    ff0.third()

    @pl.when(away >= 2)
    def _():
        for ch in range(CHUNKS):
            for k in range(4):
                pltpu.make_async_remote_copy(
                    src_ref=own(ch), dst_ref=tv.at[line_sib(k), part(ch)], send_sem=token_send.at[0, k, ch],
                    recv_sem=token_recv.at[k, ch], device_id=me.sib, device_id_type=MESH,
                ).wait_recv()

    attn.last()

    def chosen(src):
        return pltpu.make_async_copy(src, wv, local.at[31])

    @pl.when(me.cross == 0)
    def _():
        chosen(wo).start()

    @pl.when(me.cross == 1)
    def _():
        chosen(wx).start()

    chosen(wx).wait()
    moved = [here, moves.start(tv, tok), moves.start(wv, w), moves.start(cos, cos_out), moves.start(sin, sin_out)]

    heads = 3
    width = heads * HEAD_DIM

    def project(e, _):
        at = pl.ds(pl.multiple_of(e * 512, 512), 512)
        made = nt(wv[: 3 * width], tv[e])
        c_, s_ = cos[:, at], sin[:, at]
        hot = (seg[:, at] == lax.broadcasted_iota(jnp.int32, (SEGS, 512), 0)).astype(F32)
        rest = jnp.zeros((64 - SEGS, 512), F32)
        one_row = (lax.broadcasted_iota(jnp.int32, (16, 512), 0) == 0).astype(F32)
        for h in range(heads):
            r = h * HEAD_DIM
            a1, a2 = made[r : r + 32], made[r + 32 : r + 64]
            q = jnp.concatenate([a1 * c_ - a2 * s_, a2 * c_ + a1 * s_], axis=0).astype(BF16).astype(F32)
            qa[h, :, at] = jnp.concatenate([q * 0.125, hot, rest], axis=0).astype(BF16)
            r += width
            a1, a2 = made[r : r + 32], made[r + 32 : r + 64]
            k = jnp.concatenate([a1 * c_ - a2 * s_, a2 * c_ + a1 * s_], axis=0)
            kt[h * HEAD_DIM : (h + 1) * HEAD_DIM, at] = k.astype(BF16)
            ka[h, at, :] = jnp.concatenate([k, (1.0 - hot) * far_below, rest], axis=0).T.astype(BF16)
            r += width
            v = made[r : r + 64]
            va[h, :, at] = jnp.concatenate([v, one_row], axis=0).astype(BF16)
            vn[h, at, :] = jnp.concatenate([v, jnp.zeros_like(v)], axis=0).T[:, :HEAD_DIM].astype(BF16)
        return 0

    lax.fori_loop(0, 4, project, 0)
    for src, dst in ((qa, qa_out), (ka, ka_out), (kt, kt_out), (vn, vn_out), (va, va_out)):
        moved.append(moves.start(src, dst))
    ff0.last()
    ff_z2.wait_recv()
    moved += [moves.start(zv, zb.at[1]), moves.start(zv, zl)]
    ff_z1.wait_recv()
    for move in moved:
        move.wait()
    links.wait_sends()
    for k, to in ((0, near), (1, far), (2, near), (3, near)):

        @pl.when(away == k)
        def _(k=k, to=to):
            for ch in range(CHUNKS):
                copy(0, k, ch, own(ch), to).wait_send()
                if k == 1:
                    for j in (2, 3):
                        copy(0, j, ch, held(j, ch), to).wait_send()
                if k < 2:
                    for j in range(4):
                        copy(1, j, ch, own(ch) if j == k else held(j, ch), me.sib).wait_send()


FIRST, LAST = 256, 512


def list_pairs(first, end, pairs):
    idle = 8 * 16 + 8
    pairs[0] = idle

    def of_query(i, n):
        lo = first[0, i * BLK] // BLK
        hi = (end[0, i * BLK + BLK - 1] + (BLK - 1)) // BLK

        def of_key(j, n):
            pairs[n] = i * 16 + j + jnp.where(j == lo, FIRST, 0) + jnp.where(j == hi - 1, LAST, 0)
            return n + 1

        return lax.fori_loop(lo, hi, of_key, n)

    n = lax.fori_loop(0, 2048 // BLK, of_query, 1)
    for more in range(3):
        pairs[n + more] = idle
    return n - 1


def split_pair(code):
    return (code // 16) % 16, code % 16


def columns(block):
    return pl.ds(pl.multiple_of(block * BLK, BLK), BLK)


def real(block):
    return jnp.where(block == 8, 0, block)


def attend_forward_kernel(
    first, end, w_in, qa_in, ka_in, va_in, ot, logsum, part,
    w, qa, ka, va, mx, acc, s0, s1, p0, p1, al0, al1, pairs, sem,
):
    heads = 3
    width = heads * HEAD_DIM
    moves = Moves(sem)
    loads = [moves.start(src, dst) for src, dst in ((qa_in, qa), (ka_in, ka), (va_in, va), (w_in.at[pl.ds(3 * width, width)], w))]
    count = list_pairs(first, end, pairs)

    def score(t, s):
        i, j = split_pair(pairs[t])
        at, here = columns(real(i)), columns(real(j))
        for h in range(heads):
            s[h] = nn(ka[h, here, :], qa[h, :, at])

    def weigh(t, s, p, al):
        fresh = pairs[t] & FIRST
        for h in range(heads):
            scores = s[h]
            before = jnp.where(fresh > 0, -3e38, mx[h])
            largest = jnp.maximum(before, jnp.max(scores, axis=0, keepdims=True))
            p[h] = jnp.exp(scores - largest).astype(BF16)
            al[h] = jnp.exp(before - largest)
            mx[h] = largest

    def gather(t, p, al):
        code = pairs[t]
        i, j = split_pair(code)
        here = columns(real(j))
        for h in range(heads):
            acc[h] = acc[h] * al[h] + nn(va[h, :, here], p[h])

        @pl.when((code & LAST) > 0)
        def _():
            at = columns(i)
            for h in range(heads):
                total = acc[h, 64:65, :]
                ot[h * HEAD_DIM : (h + 1) * HEAD_DIM, at] = (acc[h, :64, :] / total).astype(BF16)
                logsum[pl.ds(h, 1), at] = mx[h] + jnp.log(total)

    def step(u, _):
        t = 2 * u + 1
        gather(t - 1, p1, al1)
        weigh(t, s0, p0, al0)
        score(t + 1, s1)
        gather(t, p0, al0)
        weigh(t + 1, s1, p1, al1)
        score(t + 2, s0)
        return 0

    acc[...] = jnp.zeros_like(acc)
    p1[...] = jnp.zeros_like(p1)
    al1[...] = jnp.zeros_like(al1)
    for load in loads:
        load.wait()
    score(1, s0)
    lax.fori_loop(0, (count + 2) // 2, step, 0)
    for e in range(4):
        part[e] = tn(ot[:, e * 512 : (e + 1) * 512], w[...]).astype(BF16)


def attend_backward_kernel(
    first, end, gb_in, tok_in, w_in, qa_in, ka_in, kt_in, vn_in, ot_in, logsum, cos_in, sin_in, grads, part,
    gb, tok, w, qa, ka, kt, vn, ot, cos, sin, dot_, inner, dq, dk, dv, gp, s0, s1, r0, r1, p0, p1, d0, d1, pairs, sem,
):
    heads = 3
    width = heads * HEAD_DIM
    moves = Moves(sem)
    loads = [
        moves.start(src, dst)
        for src, dst in (
            (w_in, w), (ot_in, ot), (gb_in, gb), (qa_in, qa), (ka_in, ka), (vn_in, vn), (kt_in, kt), (cos_in, cos),
            (sin_in, sin), (tok_in, tok),
        )
    ]
    for total in (dq, dk, dv, p1, d1):
        total[...] = jnp.zeros_like(total)
    count = list_pairs(first, end, pairs)
    for load in loads[:3]:
        load.wait()

    def begin(e, _):
        at = pl.ds(pl.multiple_of(e * 512, 512), 512)
        made = nt(w[3 * width :], gb[e]).astype(BF16)
        dot_[:, at] = made
        product = made.astype(F32) * ot[:, at].astype(F32)
        for h in range(heads):
            inner[pl.ds(h, 1), at] = jnp.sum(product[h * HEAD_DIM : (h + 1) * HEAD_DIM], axis=0, keepdims=True)
        return 0

    lax.fori_loop(0, 4, begin, 0)
    for load in loads[3:]:
        load.wait()

    def score(t, s, r):
        i, j = split_pair(pairs[t])
        at, here = columns(real(i)), columns(real(j))
        for h in range(heads):
            rows = slice(h * HEAD_DIM, (h + 1) * HEAD_DIM)
            s[h] = nn(ka[h, here, :], qa[h, :, at])
            r[h] = nn(vn[h, here, :], dot_[rows, at])

    def weigh(t, s, r, p, d):
        at = columns(real(split_pair(pairs[t])[0]))
        for h in range(heads):
            probability = jnp.exp(s[h] - logsum[pl.ds(h, 1), at])
            p[h] = probability.astype(BF16)
            d[h] = (probability * (r[h] - inner[pl.ds(h, 1), at])).astype(BF16)

    def gather(t, p, d):
        i, j = split_pair(pairs[t])
        at, here = columns(real(i)), columns(real(j))
        to_query, to_key = columns(i), columns(j)
        for h in range(heads):
            rows = slice(h * HEAD_DIM, (h + 1) * HEAD_DIM)
            dv[rows, to_key] += nt(dot_[rows, at], p[h])
            dk[rows, to_key] += nt(qa[h, :HEAD_DIM, at], d[h])
            dq[rows, to_query] += nn(kt[rows, here], d[h])

    def step(u, _):
        t = 2 * u + 1
        gather(t - 1, p1, d1)
        weigh(t, s0, r0, p0, d0)
        score(t + 1, s1, r1)
        gather(t, p0, d0)
        weigh(t + 1, s1, r1, p1, d1)
        score(t + 2, s0, r0)
        return 0

    score(1, s0, r0)
    lax.fori_loop(0, (count + 2) // 2, step, 0)

    def turn(e, _):
        at = pl.ds(pl.multiple_of(e * 512, 512), 512)
        c, s = cos[:, at], sin[:, at]
        for h in range(heads):
            r = h * HEAD_DIM
            for first, total, scale in ((0, dq, 0.125), (width, dk, 1.0)):
                d1_, d2_ = total[r : r + 32, at] * scale, total[r + 32 : r + 64, at] * scale
                gp[first + r : first + r + 64, at] = jnp.concatenate(
                    [d1_ * c + d2_ * s, d2_ * c - d1_ * s], axis=0
                ).astype(BF16)
        gp[2 * width :, at] = dv[:, at].astype(BF16)
        return 0

    lax.fori_loop(0, 4, turn, 0)
    for e in range(4):
        part[e] = tn(gp[:, e * 512 : (e + 1) * 512], w[: 3 * width]).astype(BF16)
    for block in range(4):
        if block < 3:
            rows = slice(block * width, (block + 1) * width)
            made = sum(nn(gp[rows, e * 512 : (e + 1) * 512], tok[e]) for e in range(4))
        else:
            made = sum(nn(ot[:, e * 512 : (e + 1) * 512], gb[e]) for e in range(4))
        grads[block * width : (block + 1) * width] = made.astype(BF16)


def row_mean(v):
    return jnp.mean(v, axis=-1, keepdims=True)


def norm_forward(summed):
    centred = summed - row_mean(summed)
    inverse = lax.rsqrt(row_mean(centred * centred) + epsilon)
    return centred * inverse, inverse


def norm_backward(scaled, normalized, inverse):
    return inverse * (scaled - row_mean(scaled) - normalized * row_mean(scaled * normalized))


def feed_forward_kernel(
    tok, part_in, cot_in, gain, bias, wf0, zb, zx, zy, zc,
    out, gz1, gb, sums, keep_a, keep_b, send_a, send_b, zs_out,
    part, own_g, w, slope_g, slope_u, hid, nb, nbt, gm, gmt, total, norm1, inv1, dw, lw, xs, cot, from_core, from_z, to_z,
    f1a, f1b, f2a, f2b, send, recv, local, out_sem, trade_sem,
):
    me = Place()
    greet((me.sib, me.xn, me.yn, me.z1, me.pair))
    links = Links(send, recv)
    moves = Moves(local)
    partial = moves.start(part_in, part)
    loads = [moves.start(tok.at[me.slot], xs), moves.start(wf0, w.at[0])]
    for ez in (2, 1):
        for place, src in ((me.place, zb), (me.x_place, zx), (me.y_place, zy)):
            loads.append(moves.start(src.at[ez - 1], view_3d(w.at[ez])(place, 0, 96)))
    loads.append(moves.start(zc, view_3d(w.at[3])(me.place, 0, 96)))

    def cot_here():
        return pltpu.make_async_copy(cot_in, cot, local.at[15])

    def cot_there():
        return pltpu.make_async_remote_copy(
            src_ref=cot_in, dst_ref=cot, send_sem=trade_sem.at[0], recv_sem=trade_sem.at[1], device_id=me.pair,
            device_id_type=MESH,
        )

    def rows(ch):
        return pl.ds(ch * CHUNK, CHUNK)

    cores = [
        [links.start(part_in.at[shard, rows(ch)], from_core.at[i, rows(ch)], me.sib) for ch in range(CHUNKS)]
        for i, shard in ((1, me.slot3), (0, me.slot2))
    ]
    ff2, ff1 = [Corner(me, links, view_3d(w.at[ez]), *(src.at[ez - 1] for src in (zb, zx, zy))) for ez in (2, 1)]
    ff3 = Spread(me, links, view_3d(w.at[3]), zc)
    zs = []
    partial.wait()
    for ch in range(CHUNKS):
        cores[0][ch].wait_recv()
        at = rows(ch)
        to_z[at] = (part[me.slot1, at].astype(F32) + from_core[1, at].astype(F32)).astype(BF16)
        zs.append(links.start(to_z.at[at], from_z.at[at], me.z1))

    @pl.when(me.cross == 0)
    def _():
        cot_here().start()

    @pl.when(me.cross == 1)
    def _():
        cot_there().start()

    ff2.third()
    ff1.third()
    loads[0].wait()
    loads[1].wait()
    def forward(ez, at=pl.ds(0, 512)):
        gate = nn(nb[at], w[ez, 0])
        up = nn(nb[at], w[ez, 1])
        sig = 1.0 / (1.0 + jnp.exp(-gate))
        active = gate * sig
        low = (active * up).astype(BF16)
        hid[ez, at] = low
        slope_u[ez, at] = active.astype(BF16)
        slope_g[ez, at] = (up * sig * (1.0 + gate * (1.0 - sig))).astype(BF16)
        total[at] += nn(low, w[ez, 2])

    for ch in range(CHUNKS):
        if ch == CHUNKS // 2:
            forward(0, pl.ds(0, 256))
            ff3.second()
            for load in loads[2:]:
                load.wait()
            ff2.last()
            forward(2, pl.ds(0, 256))
        cores[1][ch].wait_recv()
        zs[ch].wait_recv()
        at = rows(ch)
        branch = part[me.slot, at].astype(F32) + from_core[0, at].astype(F32) + from_z[at].astype(F32)
        n1, i1 = norm_forward(xs[at].astype(F32) + branch)
        norm1[at] = n1
        inv1[at] = jnp.broadcast_to(i1, (CHUNK, 128))
        normed = n1 * gain[0:1, :] + bias[0:1, :]
        total[at] = normed
        nb[at] = normed.astype(BF16)
        nbt[:, ch * CHUNK : (ch + 1) * CHUNK] = normed.T.astype(BF16)

    forward(0, pl.ds(256, 256))
    forward(2, pl.ds(256, 256))
    ff3.third()
    ff1.last()
    forward(1)
    ff3.last()
    forward(3)
    n2, i2 = norm_forward(total[...])
    out[...] = (n2 * gain[1:2, :] + bias[1:2, :]).astype(BF16)

    @pl.when(me.cross == 0)
    def _():
        cot_here().wait()

    @pl.when(me.cross == 1)
    def _():
        cot_there().wait()

    g = cot[...].astype(F32)
    sums[1:2, :] = jnp.sum(g * n2, axis=0, keepdims=True)
    sums[3:4, :] = jnp.sum(g, axis=0, keepdims=True)
    gz2 = norm_backward(g * gain[1:2, :], n2, i2)
    total[...] = gz2
    gm[...] = gz2.astype(BF16)
    gmt[...] = gz2.T.astype(BF16)

    def block(quad, core):
        return pl.ds(pl.multiple_of((quad * 2 + core) * 96, 32), 96)

    order = (3, 1, 0, 2)
    halves = []
    first, last = pl.ds(0, 48), pl.ds(48, 48)

    upper, lower = pl.ds(0, 256), pl.ds(256, 256)

    def slopes(ez, at=pl.ds(0, 512)):
        grad_hidden = nt(gm[at], w[ez, 2])
        gate = (grad_hidden * slope_g[ez, at].astype(F32)).astype(BF16)
        up = (grad_hidden * slope_u[ez, at].astype(F32)).astype(BF16)
        slope_g[ez, at] = gate
        slope_u[ez, at] = up
        total[at] += nt(gate, w[ez, 0]) + nt(up, w[ez, 1])

    def weights(n):
        i, ez = n % 2, order[n]
        if n >= 2:
            for copy in halves[n - 2]:
                copy.wait_send()
        dw[i, 2] = nn(gmt[...], hid[ez]).astype(BF16)
        dw[i, 0] = nn(nbt[...], slope_g[ez]).astype(BF16)
        dw[i, 1] = nn(nbt[...], slope_u[ez]).astype(BF16)
        halves.append([links.make(dw.at[i, :, block(quad, 1 - me.c)], lw.at[n, quad], me.sib) for quad in range(4)])
        for copy in halves[n]:
            copy.start()

    def settle(n):
        for quad in range(4):
            halves[n][quad].wait_recv()
            for m in range(3):
                lw[n, quad, m] = (lw[n, quad, m].astype(F32) + dw[n % 2, m, block(quad, me.c)].astype(F32)).astype(BF16)

    def plane_first():
        return [
            (
                links.start(lw.at[0, (1 - me.y) * 2 + o, :, first], f1a.at[o], me.yn),
                links.start(lw.at[0, o * 2 + 1 - me.x, :, last], f1b.at[o], me.xn),
            )
            for o in range(2)
        ]

    def plane_second(plane_1):
        for o in range(2):
            plane_1[o][0].wait_recv()
            f1a[o] = (f1a[o].astype(F32) + lw[0, me.y * 2 + o, :, first].astype(F32)).astype(BF16)
            plane_1[o][1].wait_recv()
            f1b[o] = (f1b[o].astype(F32) + lw[0, o * 2 + me.x, :, last].astype(F32)).astype(BF16)
        return links.start(f1a.at[1 - me.x], f2a, me.xn), links.start(f1b.at[1 - me.y], f2b, me.yn)

    def plane_last(plane_2):
        plane_2[0].wait_recv()
        zs_out[0] = (f1a[me.x].astype(F32) + f2a[...].astype(F32)).astype(BF16)
        plane_2[1].wait_recv()
        zs_out[1] = (f1b[me.y].astype(F32) + f2b[...].astype(F32)).astype(BF16)

    def stores(n):
        made = []
        for oy in range(2):
            for ox in range(2):
                src = lw.at[n, oy * 2 + ox]
                made.append((me.y == oy, src.at[:, first], keep_a.at[n - 1, ox], send_a.at[n - 1, ox]))
                made.append((me.x == ox, src.at[:, last], keep_b.at[n - 1, oy], send_b.at[n - 1, oy]))
        return made

    def store(n):
        for number, (here, src, kept, sent) in enumerate(stores(n)):

            @pl.when(here)
            def _(number=number, src=src, kept=kept):
                pltpu.make_async_copy(src, kept, out_sem.at[n - 1, number]).start()

            @pl.when(jnp.logical_not(here))
            def _(number=number, src=src, sent=sent):
                pltpu.make_async_copy(src, sent, out_sem.at[n - 1, number]).start()

    slopes(3)
    weights(0)
    slopes(1)
    settle(0)
    plane_1 = plane_first()
    to_pair, to_core, on_core = [], [], []
    for ch in range(CHUNKS):
        if ch % 2 == 0:
            slopes(0, lower if ch else upper)
            slopes(2, lower if ch else upper)
        at = rows(ch)
        made = norm_backward(total[at] * gain[0:1, :], norm1[at], inv1[at, 0:1])
        gz1[at] = made
        own_g[at] = made.astype(BF16)
        mine = gb.at[me.slot, at]
        to_pair.append(links.start(own_g.at[at], mine, me.z1))
        to_core.append(links.start(own_g.at[at], mine, me.sib))
    kept_g = moves.start(own_g, gb.at[me.slot])
    g = total[...]
    sums[0:1, :] = jnp.sum(g * norm1[...], axis=0, keepdims=True)
    sums[2:3, :] = jnp.sum(g, axis=0, keepdims=True)
    sums[4:8, :] = jnp.zeros((4, 768), F32)
    weights(1)
    weights(2)
    settle(1)
    store(1)
    plane_2 = plane_second(plane_1)
    weights(3)
    settle(2)
    store(2)
    settle(3)
    store(3)
    for ch in range(CHUNKS):
        to_pair[ch].wait_recv()
        other = gb.at[me.slot1, rows(ch)]
        on_core.append(links.start(other, other, me.sib))
    plane_last(plane_2)
    kept_g.wait()
    for copy in to_core + on_core:
        copy.wait_recv()
    for n in (1, 2, 3):
        for number, (_, src, kept, _) in enumerate(stores(n)):
            pltpu.make_async_copy(src, kept, out_sem.at[n - 1, number]).wait()
    for n in (2, 3):
        for copy in halves[n]:
            copy.wait_send()
    links.wait_sends()


def finish_kernel(
    extra, keep_a_in, keep_b_in, recv_a_in, recv_b_in, zr_in, ga_in, part_in, gz1_in, sums_in,
    g_ff, g_attn, g_tok, sums,
    keep_a, keep_b, recv_a, recv_b, zr, ga, part, gz1, block,
    sa, sb, f2a, f2b, va, f3, f4, fe, a_in, a_mid, a_out, a_fin, a_two, ae, from_core, from_z, to_z, trade_out, trade_in, sum_in,
    send, recv, a_send, a_recv, local,
):
    me = Place()
    moves = Moves(local)
    part_here, ga_here = moves.start(part_in, part), moves.start(ga_in, ga)
    ff_here = [
        moves.start(src, dst)
        for src, dst in ((keep_a_in, keep_a), (recv_a_in, recv_a), (keep_b_in, keep_b), (recv_b_in, recv_b), (zr_in, zr))
    ]
    gz1_here = moves.start(gz1_in, gz1)
    bits = [{"dp": me.p + bit - 2 * bit * ((me.p // bit) % 2)} for bit in extra]
    greet([me.sib, me.xn, me.yn, me.z1, me.z2, me.pair] + bits)
    links = Links(send, recv)

    def rows(ch):
        return pl.ds(ch * CHUNK, CHUNK)

    def add(*terms):
        return sum(t.astype(F32) for t in terms).astype(BF16)

    part_here.wait()
    cores = [
        [links.start(part.at[shard, rows(ch)], from_core.at[i, rows(ch)], me.sib) for ch in range(CHUNKS)]
        for i, shard in ((1, me.slot3), (0, me.slot2))
    ]

    def half(oy, ox, h):
        return pl.ds(pl.multiple_of((oy * 2 + ox) * 192 + h * 96, 32), 96)

    attn_1 = []
    ga_here.wait()
    for o in range(2):
        attn_1.append(links.start(ga.at[half(1 - me.y, o, 0)], a_in.at[0, o], me.yn))
        attn_1.append(links.start(ga.at[half(o, 1 - me.x, 1)], a_in.at[1, o], me.xn))

    sums[...] = sums_in[...]
    around = [me.sib, me.xn, me.yn, me.z1, me.z2] + bits
    small = [links.start(sums, sum_in.at[0], around[0])]

    def small_step():
        n = len(small)
        small[-1].wait_recv()
        small[-1].wait_send()
        links.started = [copy for copy in links.started if copy is not small[n - 1]]
        sums[...] += sum_in[n - 1]
        if n < len(around):
            small.append(links.start(sums, sum_in.at[n], around[n]))

    ff_2 = {}

    def plane(ez):
        sa[ez] = add(keep_a[ez, 1 - me.x], recv_a[ez, 1 - me.x])
        sb[ez] = add(keep_b[ez, 1 - me.y], recv_b[ez, 1 - me.y])
        ff_2[ez] = (links.start(sa.at[ez], f2a.at[ez], me.xn), links.start(sb.at[ez], f2b.at[ez], me.yn))

    def planed(ez):
        ff_2[ez][0].wait_recv()
        va[ez, 0] = add(keep_a[ez, me.x], recv_a[ez, me.x], f2a[ez], *([zr[0]] if ez == 2 else []))
        ff_2[ez][1].wait_recv()
        va[ez, 1] = add(keep_b[ez, me.y], recv_b[ez, me.y], f2b[ez], *([zr[1]] if ez == 2 else []))

    for load in ff_here:
        load.wait()
    plane(2)
    zs = []
    for ch in range(CHUNKS):
        cores[0][ch].wait_recv()
        at = rows(ch)
        to_z[at] = add(part[me.slot1, at], from_core[1, at])
        zs.append(links.start(to_z.at[at], from_z.at[at], me.z1))
    for copy in attn_1:
        copy.wait_recv()
    small_step()
    a_mid[0] = add(ga[half(me.y, 1 - me.x, 0)], a_in[0, 1 - me.x])
    a_mid[1] = add(ga[half(1 - me.y, me.x, 1)], a_in[1, 1 - me.y])
    attn_2 = [links.start(a_mid.at[0], a_out.at[0], me.xn), links.start(a_mid.at[1], a_out.at[1], me.yn)]
    planed(2)
    ff_4 = links.start(va.at[2], f4, me.z2)
    for copy in attn_2:
        copy.wait_recv()
    small_step()
    a_fin[:96] = add(ga[half(me.y, me.x, 0)], a_in[0, me.x], a_out[0])
    a_fin[96:] = add(ga[half(me.y, me.x, 1)], a_in[1, me.y], a_out[1])

    def attn_copy(n, src, dst, to):
        return pltpu.make_async_remote_copy(
            src_ref=src, dst_ref=dst, send_sem=a_send.at[n], recv_sem=a_recv.at[n], device_id=to, device_id_type=MESH
        )

    def quarter(oy, ox, first=0, size=192):
        return g_attn.at[pl.ds(pl.multiple_of((oy * 2 + ox) * 192 + first, 32), size)]

    def attn_over():
        return attn_copy(0, a_fin, a_two, me.z2)

    @pl.when(me.cross == 1)
    def _():
        attn_over().start()

    plane(0)
    plane(1)
    planed(0)
    ff_3 = links.start(va.at[0], f3, me.z1)
    planed(1)
    small_step()

    trades = [
        pltpu.make_async_remote_copy(
            src_ref=trade_out.at[rows(ch)], dst_ref=trade_in.at[rows(ch)], send_sem=a_send.at[8 + ch],
            recv_sem=a_recv.at[8 + ch], device_id=me.pair, device_id_type=MESH,
        )
        for ch in range(CHUNKS)
    ]
    mine = quarter(me.y, me.x)

    def attn_send(n, src, to):
        return attn_copy(n, src, src, to)

    block_x, block_y = quarter(me.y, 1 - me.x), quarter(1 - me.y, me.x)
    low_x, high_y = quarter(me.y, 1 - me.x, 0, 96), quarter(1 - me.y, me.x, 96, 96)
    corner = quarter(1 - me.y, 1 - me.x)

    @pl.when(me.cross == 0)
    def _():
        attn_over().wait_recv()
        total = add(a_fin[...], a_two[...])
        for n, bit in enumerate(bits):
            ae[n, 0] = total
            step = attn_copy(16 + n, ae.at[n, 0], ae.at[n, 1], bit)
            step.start()
            step.wait()
            total = add(total, ae[n, 1])
        g_attn[pl.ds(pl.multiple_of((me.y * 2 + me.x) * 192, 32), 192)] = total
        attn_send(1, mine, me.xn).start()
        attn_send(2, mine, me.yn).start()
        attn_send(3, mine, me.sib).start()

    gz1_here.wait()
    for ch in range(CHUNKS):
        cores[1][ch].wait_recv()
        zs[ch].wait_recv()
        at = rows(ch)
        got = gz1[at] + (part[me.slot, at].astype(F32) + from_core[0, at].astype(F32) + from_z[at].astype(F32))

        @pl.when(me.cross == 0)
        def _(at=at, got=got):
            g_tok[at] = got

        @pl.when(me.cross == 1)
        def _(at=at, got=got, ch=ch):
            trade_out[at] = got.astype(BF16)

    small_step()


    @pl.when(me.cross == 0)
    def _():
        attn_send(1, block_x, me.xn).wait_recv()
        attn_send(4, low_x, me.yn).start()
        attn_send(5, block_x, me.sib).start()
        attn_send(2, block_y, me.yn).wait_recv()
        attn_send(6, high_y, me.xn).start()
        attn_send(7, block_y, me.sib).start()

    ff_3.wait_recv()
    ff_4.wait_recv()
    total = add(va[1], f3[...], f4[...])
    for n, bit in enumerate(bits):
        fe[n, 0] = total
        step = links.start(fe.at[n, 0], fe.at[n, 1], bit)
        step.wait_recv()
        total = add(total, fe[n, 1])
    for h in range(2):
        block[:, h * 48 : (h + 1) * 48] = total[h]
    spread = Spread(me, links, view_3d(g_ff), block)
    kept = moves.start(block, view_3d(g_ff)(me.place, 0, 96))

    @pl.when(me.cross == 1)
    def _():
        for ch in range(CHUNKS):
            trades[ch].start()

    while len(small) < len(around):
        small_step()
    spread.second()
    small_step()

    @pl.when(me.cross == 0)
    def _():
        attn_send(4, low_x, me.yn).wait_recv()
        attn_send(6, high_y, me.xn).wait_recv()
        attn_send(12, corner, me.sib).start()
        for n, src, to in (
            (1, mine, me.xn), (2, mine, me.yn), (3, mine, me.sib), (4, low_x, me.yn), (5, block_x, me.sib),
            (6, high_y, me.xn), (7, block_y, me.sib), (12, corner, me.sib),
        ):
            attn_send(n, src, to).wait_send()

    @pl.when(me.cross == 1)
    def _():
        for ch in range(CHUNKS):
            trades[ch].wait_recv()
            g_tok[rows(ch)] = trade_in[rows(ch)].astype(F32)
        attn_over().wait_send()
        for n, src in ((3, mine), (5, block_x), (7, block_y), (12, corner)):
            attn_send(n, src, me.sib).wait_recv()
        for ch in range(CHUNKS):
            trades[ch].wait_send()

    spread.third()
    spread.last()
    kept.wait()
    links.wait_sends()


def widen_kernel(attn, out_rows, gate_up, down, tok, sums, g_qkv, g_out, g_gate_up, g_down, g_tok, gains, biases):
    g_qkv[...] = attn[...].astype(F32)
    g_out[...] = out_rows[...].astype(F32)
    g_gate_up[:, 0, :] = gate_up[0].astype(F32)
    g_gate_up[:, 1, :] = gate_up[1].astype(F32)
    g_down[...] = down[0].astype(F32).T
    g_tok[0] = tok[...]
    gains[...] = sums[0:2, :]
    biases[...] = sums[2:4, :]


def solution(mesh):
    dp, tensor = mesh.shape["dp"], mesh.shape["tensor"]
    assert tensor == 4 and dp >= 8 and dp & (dp - 1) == 0
    extra = [1 << b for b in range(3, dp.bit_length() - 1)]
    both = ("dp", "tensor")

    def cell(i, k):
        return i * tensor + k

    def over(x, bit):
        return lax.ppermute(x, "dp", [(i, i ^ bit) for i in range(dp)])

    away = [(i, k) for i in range(dp) for k in range(tensor) if (i & 1) != (k >> 1)]

    def trade(x):
        return lax.ppermute(x, both, [(cell(i, k), cell(i ^ 1, k ^ 2)) for i, k in away])

    smem = pl.BlockSpec(memory_space=pltpu.SMEM)
    vmem = pl.BlockSpec(memory_space=pltpu.VMEM)
    hbm = pl.BlockSpec(memory_space=pl.ANY)

    def shape(*dims, dtype=BF16):
        return jax.ShapeDtypeStruct(dims, dtype)

    far = pl.BlockSpec(memory_space=pltpu.HBM)

    def held(*dims, dtype=BF16):
        return pltpu.HBM(dims, dtype)

    def dma(*dims):
        return pltpu.SemaphoreType.DMA(dims)

    def params(mib, number=None):
        if number is None:
            return pltpu.CompilerParams(vmem_limit_bytes=mib << 20)
        return pltpu.CompilerParams(vmem_limit_bytes=mib << 20, collective_id=number, has_side_effects=True)

    def on_device(tokens, segments, w_qkv, w_out, w_gate_up, w_down, norm_gain, norm_bias, cotangent):
        p, z = lax.axis_index("dp"), lax.axis_index("tensor")
        swapped = (p & 1) != (z >> 1)
        place = p & 7

        rows = lax.dynamic_slice(w_gate_up, (place * 96, 0, 0), (96, 2, 768))
        block = jnp.stack([rows[:, 0], rows[:, 1], lax.dynamic_slice(w_down, (place * 96, 0), (96, 768))])

        length = segments.shape[1]
        inverse = jnp.asarray(np.exp(-2.0 * np.arange(HEAD_DIM // 2) / HEAD_DIM * log_base).astype(np.float32)[:, None])
        tok, w, wf0, zb, zl, qa, ka, kt, vn, va, cos, sin, seg, first, end = pl.pallas_call(
            start_kernel,
            name="start",
            out_shape=(
                held(4, 512, 768), held(768, 768), held(3, 768, 768), held(2, 3, 96, 768), held(3, 96, 768),
                held(3, 128, length), held(3, length, 128), held(192, length), held(3, length, 64), held(3, 80, length),
                held(32, length, dtype=F32), held(32, length, dtype=F32),
                *(shape(1, length, dtype=jnp.int32),) * 3,
            ),
            in_specs=[hbm] * 3 + [vmem] * 3,
            out_specs=(far,) * 12 + (vmem,) * 3,
            scratch_shapes=[
                pltpu.VMEM((768, 768), BF16),
                pltpu.VMEM((3, 96, 768), BF16),
                pltpu.VMEM((4, 512, 768), BF16),
                pltpu.VMEM((768, 768), BF16),
                pltpu.VMEM((768, 768), BF16),
                pltpu.VMEM((1, length), jnp.int32),
                pltpu.VMEM((32, length), F32),
                pltpu.VMEM((32, length), F32),
                pltpu.VMEM((3, 128, length), BF16),
                pltpu.VMEM((3, length, 128), BF16),
                pltpu.VMEM((192, length), BF16),
                pltpu.VMEM((3, length, 64), BF16),
                pltpu.VMEM((3, 80, length), BF16),
                dma(2, 4, CHUNKS), dma(4, CHUNKS), dma(40), dma(40), dma(32),
            ],
            compiler_params=params(62, 0),
        )(tokens[0], w_qkv.transpose(1, 2, 0).reshape(576, 768), w_out, block, segments, inverse)

        zc = lax.ppermute(zl, "tensor", [(i, i ^ 1) for i in range(tensor)])
        zx, zy = over(zb, 2), over(zb, 4)

        ot, logsum, part = pl.pallas_call(
            attend_forward_kernel,
            name="attend_forward",
            out_shape=(held(192, length), shape(8, length, dtype=F32), held(4, 512, 768)),
            in_specs=[smem] * 2 + [far] * 4,
            out_specs=(vmem,) * 3,
            scratch_shapes=[
                pltpu.VMEM((192, 768), BF16),
                pltpu.VMEM((3, 128, length), BF16),
                pltpu.VMEM((3, length, 128), BF16),
                pltpu.VMEM((3, 80, length), BF16),
                pltpu.VMEM((3, 1, BLK), F32),
                pltpu.VMEM((3, 80, BLK), F32),
                *[pltpu.VMEM((3, BLK, BLK), F32)] * 2,
                *[pltpu.VMEM((3, BLK, BLK), BF16)] * 2,
                *[pltpu.VMEM((3, 1, BLK), F32)] * 2,
                pltpu.SMEM((72,), jnp.int32),
                dma(4),
            ],
            compiler_params=params(62),
            cost_estimate=pl.CostEstimate(flops=20_000_000_000, bytes_accessed=24_000_000, transcendentals=6_000_000),
        )(first, end, w, qa, ka, va)

        plane = (3, 2, 3, 48, 768)
        out, gz1, gb, sums, keep_a, keep_b, send_a, send_b, zs = pl.pallas_call(
            feed_forward_kernel,
            name="feed_forward",
            out_shape=(
                shape(512, 768), shape(512, 768, dtype=F32), held(4, 512, 768), shape(8, 768, dtype=F32),
                *(held(*plane),) * 4, shape(2, 3, 48, 768),
            ),
            in_specs=[far, far, hbm, vmem, vmem] + [far] * 5,
            out_specs=(vmem, vmem, far, vmem) + (far,) * 4 + (vmem,),
            scratch_shapes=[
                pltpu.VMEM((4, 512, 768), BF16),
                pltpu.VMEM((512, 768), BF16),
                pltpu.VMEM((4, 3, 768, 768), BF16),
                pltpu.VMEM((4, 512, 768), BF16),
                pltpu.VMEM((4, 512, 768), BF16),
                pltpu.VMEM((4, 512, 768), BF16),
                pltpu.VMEM((512, 768), BF16),
                pltpu.VMEM((768, 512), BF16),
                pltpu.VMEM((512, 768), BF16),
                pltpu.VMEM((768, 512), BF16),
                pltpu.VMEM((512, 768), F32),
                pltpu.VMEM((512, 768), F32),
                pltpu.VMEM((512, 128), F32),
                pltpu.VMEM((2, 3, 768, 768), BF16),
                pltpu.VMEM((4, 4, 3, 96, 768), BF16),
                pltpu.VMEM((512, 768), BF16),
                pltpu.VMEM((512, 768), BF16),
                pltpu.VMEM((2, 512, 768), BF16),
                pltpu.VMEM((512, 768), BF16),
                pltpu.VMEM((512, 768), BF16),
                pltpu.VMEM((2, 3, 48, 768), BF16),
                pltpu.VMEM((2, 3, 48, 768), BF16),
                pltpu.VMEM((3, 48, 768), BF16),
                pltpu.VMEM((3, 48, 768), BF16),
                dma(80), dma(80), dma(16), dma(3, 8), dma(2),
            ],
            compiler_params=params(62, 1),
            cost_estimate=pl.CostEstimate(flops=22_000_000_000, bytes_accessed=36_000_000, transcendentals=3_000_000),
        )(tok, part, cotangent[0], norm_gain, norm_bias, wf0, zb, zx, zy, zc)

        recv_a, recv_b = over(send_a, 4), over(send_b, 2)
        zr = lax.ppermute(zs, "tensor", [(i, i ^ 1) for i in range(tensor)])
        output = jnp.where(swapped, trade(out), out)[None]

        grads, part = pl.pallas_call(
            attend_backward_kernel,
            name="attend_backward",
            out_shape=(shape(768, 768), shape(4, 512, 768)),
            in_specs=[smem] * 2 + [far] * 8 + [vmem] + [far] * 2,
            out_specs=(vmem,) * 2,
            scratch_shapes=[
                pltpu.VMEM((4, 512, 768), BF16),
                pltpu.VMEM((4, 512, 768), BF16),
                pltpu.VMEM((768, 768), BF16),
                pltpu.VMEM((3, 128, length), BF16),
                pltpu.VMEM((3, length, 128), BF16),
                pltpu.VMEM((192, length), BF16),
                pltpu.VMEM((3, length, 64), BF16),
                pltpu.VMEM((192, length), BF16),
                pltpu.VMEM((32, length), F32),
                pltpu.VMEM((32, length), F32),
                pltpu.VMEM((192, length), BF16),
                pltpu.VMEM((8, length), F32),
                *[pltpu.VMEM((192, length + BLK), F32)] * 3,
                pltpu.VMEM((576, length), BF16),
                *[pltpu.VMEM((3, BLK, BLK), F32)] * 4,
                *[pltpu.VMEM((3, BLK, BLK), BF16)] * 4,
                pltpu.SMEM((72,), jnp.int32),
                dma(10),
            ],
            compiler_params=params(62),
            cost_estimate=pl.CostEstimate(flops=40_000_000_000, bytes_accessed=24_000_000, transcendentals=6_000_000),
        )(first, end, gb, tok, w, qa, ka, kt, vn, ot, logsum, cos, sin)

        spare = max(len(extra), 1)
        half = (48, 768)
        g_ff, g_attn, g_tok, sums = pl.pallas_call(
            functools.partial(finish_kernel, extra),
            name="finish",
            out_shape=(held(3, 768, 768), shape(768, 768), shape(512, 768, dtype=F32), shape(8, 768, dtype=F32)),
            in_specs=[far] * 8 + [vmem],
            out_specs=(far, vmem, vmem, vmem),
            scratch_shapes=[
                *[pltpu.VMEM((3, 2, 3, *half), BF16)] * 4,
                pltpu.VMEM((2, 3, *half), BF16),
                pltpu.VMEM((768, 768), BF16),
                pltpu.VMEM((4, 512, 768), BF16),
                pltpu.VMEM((512, 768), F32),
                pltpu.VMEM((3, 96, 768), BF16),
                *[pltpu.VMEM((3, 3, *half), BF16)] * 4,
                pltpu.VMEM((3, 2, 3, *half), BF16),
                pltpu.VMEM((2, 3, *half), BF16),
                pltpu.VMEM((2, 3, *half), BF16),
                pltpu.VMEM((spare, 2, 2, 3, *half), BF16),
                pltpu.VMEM((2, 2, 96, 768), BF16),
                pltpu.VMEM((2, 96, 768), BF16),
                pltpu.VMEM((2, 96, 768), BF16),
                pltpu.VMEM((192, 768), BF16),
                pltpu.VMEM((192, 768), BF16),
                pltpu.VMEM((spare, 2, 192, 768), BF16),
                pltpu.VMEM((2, 512, 768), BF16),
                pltpu.VMEM((512, 768), BF16),
                pltpu.VMEM((512, 768), BF16),
                pltpu.VMEM((512, 768), BF16),
                pltpu.VMEM((512, 768), BF16),
                pltpu.VMEM((5 + spare, 8, 768), F32),
                dma(64), dma(64), dma(16 + spare), dma(16 + spare), dma(9),
            ],
            compiler_params=params(62, 2),
        )(keep_a, keep_b, recv_a, recv_b, zr, grads, part, gz1, sums)

        g_qkv, g_out, g_gate_up, g_down, g_tok, gains, biases = pl.pallas_call(
            widen_kernel,
            name="widen",
            grid=(6,),
            out_shape=(
                shape(576, 768, dtype=F32), shape(192, 768, dtype=F32), shape(768, 2, 768, dtype=F32),
                shape(768, 768, dtype=F32), shape(1, 512, 768, dtype=F32), *(shape(2, 768, dtype=F32),) * 2,
            ),
            in_specs=[
                pl.BlockSpec((96, 768), lambda i: (i, 0)),
                pl.BlockSpec((32, 768), lambda i: (18 + i, 0)),
                pl.BlockSpec((2, 128, 768), lambda i: (0, i, 0)),
                pl.BlockSpec((1, 768, 128), lambda i: (2, 0, i)),
                pl.BlockSpec((128, 768), lambda i: (jnp.minimum(i, 3), 0)),
                pl.BlockSpec((8, 768), lambda i: (0, 0)),
            ],
            out_specs=(
                pl.BlockSpec((96, 768), lambda i: (i, 0)),
                pl.BlockSpec((32, 768), lambda i: (i, 0)),
                pl.BlockSpec((128, 2, 768), lambda i: (i, 0, 0)),
                pl.BlockSpec((128, 768), lambda i: (i, 0)),
                pl.BlockSpec((1, 128, 768), lambda i: (0, jnp.minimum(i, 3), 0)),
                pl.BlockSpec((2, 768), lambda i: (0, 0)),
                pl.BlockSpec((2, 768), lambda i: (0, 0)),
            ),
            compiler_params=params(62),
            cost_estimate=pl.CostEstimate(flops=0, bytes_accessed=18_000_000, transcendentals=0),
        )(g_attn, g_attn, g_ff, g_ff, g_tok, sums)
        return output, g_tok, g_qkv.reshape(3, 192, 768).transpose(2, 0, 1), g_out, g_gate_up, g_down, gains, biases

    placed = (
        P("dp", "tensor", None),
        P("dp", None),
        P(None, None, "tensor"),
        P("tensor", None),
        P(None, None, "tensor"),
        P("tensor", None),
        P(),
        P(),
        P("dp", "tensor", None),
    )
    return jax.shard_map(
        on_device,
        mesh=mesh,
        in_specs=placed,
        out_specs=(
            P("dp", "tensor", None),
            P("dp", "tensor", None),
            P(None, None, "tensor"),
            P("tensor", None),
            P(None, None, "tensor"),
            P("tensor", None),
            P(),
            P(),
        ),
        check_vma=False,
    )
```

```python
import functools
import math

import jax
import jax.numpy as jnp
import numpy as np
from jax import lax
from jax.experimental import pallas as pl
from jax.experimental.pallas import tpu as pltpu
from jax.sharding import PartitionSpec as P

HEAD_DIM = 64
SEGS = 8
BLK = 256
F32 = jnp.float32
BF16 = jnp.bfloat16
MESH = pl.DeviceIdType.MESH
CHUNKS = 4
CHUNK = 128

epsilon = 1e-05
far_below = -1e30
log_base = math.log(1000.0)


def nn(a, b):
    return lax.dot_general(a, b, (((1,), (0,)), ((), ())), preferred_element_type=F32)


def nt(a, b):
    return lax.dot_general(a, b, (((1,), (1,)), ((), ())), preferred_element_type=F32)


def tn(a, b):
    return lax.dot_general(a, b, (((0,), (0,)), ((), ())), preferred_element_type=F32)


class Place:
    def __init__(self):
        p, z = lax.axis_index("dp"), lax.axis_index("tensor")
        self.p, self.z = p, z
        c, x, y = p % 2, (p // 2) % 2, (p // 4) % 2
        self.c, self.x, self.y = c, x, y
        self.place = p % 8
        self.x_place = self.place + 2 - 4 * x
        self.y_place = self.place + 4 - 8 * y
        self.d_place = self.x_place + 4 - 8 * y
        self.z1_at, self.z2_at = z + 1 - 2 * (z % 2), (z + 2) % 4
        self.sib = {"dp": p + 1 - 2 * c}
        self.xn = {"dp": p + 2 - 4 * x}
        self.yn = {"dp": p + 4 - 8 * y}
        self.z1 = {"tensor": self.z1_at}
        self.z2 = {"tensor": self.z2_at}
        self.pair = {"dp": p + 1 - 2 * c, "tensor": self.z2_at}
        self.cross = c + z // 2 - 2 * c * (z // 2)
        self.slot = (z + 2 * self.cross) % 4
        self.slot1 = self.slot + 1 - 2 * (self.slot % 2)
        self.slot2 = (self.slot + 2) % 4
        self.slot3 = (self.slot1 + 2) % 4


def greet(partners):
    barrier = pltpu.get_barrier_semaphore()
    for partner in partners:
        pl.semaphore_signal(barrier, inc=1, device_id=partner, device_id_type=MESH)
    pl.semaphore_wait(barrier, len(partners))


class Links:
    def __init__(self, send, recv):
        self.send, self.recv, self.count, self.started = send, recv, 0, []

    def make(self, src, dst, to):
        i = self.count
        self.count += 1
        return pltpu.make_async_remote_copy(
            src_ref=src, dst_ref=dst, send_sem=self.send.at[i], recv_sem=self.recv.at[i], device_id=to, device_id_type=MESH
        )

    def start(self, src, dst, to):
        copy = self.make(src, dst, to)
        copy.start()
        self.started.append(copy)
        return copy

    def wait_sends(self):
        for copy in self.started:
            copy.wait_send()


class Spread:
    def __init__(self, me, links, view, src=None):
        self.me, self.links, self.view = me, links, view
        own = view(me.place, 0, 96)
        src = own if src is None else src
        self.from_x = links.start(src, own, me.xn)
        self.from_y = links.start(src, own, me.yn)
        self.from_sib = [links.start(src, own, me.sib)]

    def second(self):
        me, links, view = self.me, self.links, self.view
        self.from_x.wait_recv()
        part = view(me.x_place, 0, 48)
        self.low = links.start(part, part, me.yn)
        block = view(me.x_place, 0, 96)
        self.from_sib.append(links.start(block, block, me.sib))
        self.from_y.wait_recv()
        part = view(me.y_place, 48, 48)
        self.high = links.start(part, part, me.xn)
        block = view(me.y_place, 0, 96)
        self.from_sib.append(links.start(block, block, me.sib))

    def third(self):
        me, links, view = self.me, self.links, self.view
        self.low.wait_recv()
        self.high.wait_recv()
        block = view(me.d_place, 0, 96)
        self.from_sib.append(links.start(block, block, me.sib))

    def last(self):
        for copy in self.from_sib:
            copy.wait_recv()


class Corner(Spread):
    def __init__(self, me, links, view, own, from_x, from_y):
        self.me, self.links, self.view = me, links, view
        first, last = pl.ds(0, 48), pl.ds(48, 48)
        self.low = links.start(from_x.at[:, first], view(me.x_place, 0, 48), me.yn)
        self.high = links.start(from_y.at[:, last], view(me.y_place, 48, 48), me.xn)
        self.from_sib = [
            links.start(src, view(place, 0, 96), me.sib)
            for src, place in ((own, me.place), (from_x, me.x_place), (from_y, me.y_place))
        ]


def view_2d(ref):
    return lambda place, first, size: ref.at[pl.ds(pl.multiple_of(place * 96 + first, 16), size)]


def view_3d(ref):
    return lambda place, first, size: ref.at[:, pl.ds(pl.multiple_of(place * 96 + first, 16), size)]


class Moves:
    def __init__(self, sems):
        self.sems, self.count = sems, 0

    def start(self, src, dst):
        copy = pltpu.make_async_copy(src, dst, self.sems.at[self.count])
        self.count += 1
        copy.start()
        return copy


def start_kernel(
    x, w_qkv, w_out, fb, near_row, inverse,
    tok, w, wf0, zb, zl, qa_out, ka_out, kt_out, vn_out, va_out, cos_out, sin_out, seg, first, end,
    wo, zv, tv, wx, wv, far_row, cos, sin, qa, ka, kt, vn, va, token_send, token_recv, send, recv, local,
):
    me = Place()
    moves = Moves(local)
    wo_here = [moves.start(w_qkv, wo.at[pl.ds(0, 576)]), moves.start(w_out, wo.at[pl.ds(576, 192)])]
    c, z = me.c, me.z
    away = z + c * (3 - 2 * z)

    barrier = pltpu.get_barrier_semaphore()
    partners = (me.sib, me.xn, me.yn, me.z1, me.z2)
    for partner in partners:
        pl.semaphore_signal(barrier, inc=1, device_id=partner, device_id_type=MESH)
    @pl.when(z % 3 != 0)
    def _():
        pl.semaphore_signal(barrier, inc=1, device_id={"tensor": 3 - z}, device_id_type=MESH)

    pl.semaphore_wait(barrier, len(partners) + z * (3 - z) // 2)

    def line(k):
        return k + c * (3 - 2 * k)

    def line_sib(k):
        return k + (1 - c) * (3 - 2 * k)

    far, near = {"tensor": line(0)}, {"tensor": line(1)}

    def part(ch):
        return pl.ds(ch * CHUNK, CHUNK)

    def copy(kind, k, ch, src, to):
        return pltpu.make_async_remote_copy(
            src_ref=src, dst_ref=tv.at[line(k), part(ch)],
            send_sem=token_send.at[kind, k, ch],
            recv_sem=token_recv.at[k, ch], device_id=to, device_id_type=MESH,
        )

    def own(ch):
        return x.at[part(ch)]

    def held(k, ch):
        return tv.at[line(k), part(ch)]

    links = Links(send, recv)
    rows_far = links.start(near_row, far_row, me.sib)
    for load in wo_here:
        load.wait()
    attn_z = links.start(view_2d(wo)(me.place, 0, 96), view_2d(wx)(me.place, 0, 96), me.z2)
    ff_z1 = links.make(fb, zb.at[0], me.z1)
    ff_z2 = links.make(fb, zv, me.z2)
    for k, to in ((0, near), (1, far), (2, near), (3, near)):

        @pl.when(away == k)
        def _(k=k, to=to):
            for ch in range(CHUNKS):
                copy(0, k, ch, own(ch), to).start()
                if k < 2:
                    copy(1, k, ch, own(ch), me.sib).start()

    ff_z1.start()
    links.started.append(ff_z1)
    ff_z2.start()
    links.started.append(ff_z2)
    ff0 = Spread(me, links, view_3d(wf0), fb)
    here = moves.start(fb, view_3d(wf0)(me.place, 0, 96))

    @pl.when(away < 2)
    def _():
        mine = pltpu.make_async_copy(x, tv.at[z], local.at[30])
        mine.start()
        mine.wait()

    def forward(ch):
        @pl.when(away == 0)
        def _():
            for k in (1, 2, 3):
                copy(1, k, ch, held(k, ch), me.sib).wait_recv()
                copy(1, k, ch, held(k, ch), me.sib).start()

        @pl.when(away == 1)
        def _():
            for k in (2, 3, 0):
                copy(1, k, ch, held(k, ch), me.sib).wait_recv()
                if k:
                    copy(0, k, ch, held(k, ch), far).start()
                copy(1, k, ch, held(k, ch), me.sib).start()

    def documents():
        rows_far.wait_recv()
        row = jnp.where(me.cross == 1, far_row[...], near_row[...])
        seg[...] = row
        opened = jnp.zeros(row.shape, F32)
        closed = jnp.zeros(row.shape, F32)
        before = jnp.zeros((1, 1), F32)
        for d in range(SEGS):
            here = (row == d).astype(F32)
            opened += here * before
            before = before + jnp.sum(here, axis=1, keepdims=True)
            closed += here * before
        first[...] = opened.astype(jnp.int32)
        end[...] = closed.astype(jnp.int32)
        places = lax.broadcasted_iota(jnp.int32, row.shape, 1).astype(F32) - opened
        for e in range(4):
            at = slice(e * 512, (e + 1) * 512)
            angles = inverse[...] * places[:, at]
            cos[:, at] = jnp.cos(angles)
            sin[:, at] = jnp.sin(angles)

    attn_z.wait_recv()
    attn = Spread(me, links, view_2d(wx))
    documents()
    forward(0)
    attn.second()
    forward(1)
    attn.third()
    ff0.second()
    forward(2)
    forward(3)
    ff0.third()

    @pl.when(away >= 2)
    def _():
        for ch in range(CHUNKS):
            for k in range(4):
                pltpu.make_async_remote_copy(
                    src_ref=own(ch), dst_ref=tv.at[line_sib(k), part(ch)], send_sem=token_send.at[0, k, ch],
                    recv_sem=token_recv.at[k, ch], device_id=me.sib, device_id_type=MESH,
                ).wait_recv()

    attn.last()

    def chosen(src):
        return pltpu.make_async_copy(src, wv, local.at[31])

    @pl.when(me.cross == 0)
    def _():
        chosen(wo).start()

    @pl.when(me.cross == 1)
    def _():
        chosen(wx).start()

    chosen(wx).wait()
    moved = [here, moves.start(tv, tok), moves.start(wv, w), moves.start(cos, cos_out), moves.start(sin, sin_out)]

    heads = 3
    width = heads * HEAD_DIM

    def project(e, _):
        at = pl.ds(pl.multiple_of(e * 512, 512), 512)
        made = nt(wv[: 3 * width], tv[e])
        c_, s_ = cos[:, at], sin[:, at]
        hot = (seg[:, at] == lax.broadcasted_iota(jnp.int32, (SEGS, 512), 0)).astype(F32)
        rest = jnp.zeros((64 - SEGS, 512), F32)
        one_row = (lax.broadcasted_iota(jnp.int32, (16, 512), 0) == 0).astype(F32)
        for h in range(heads):
            r = h * HEAD_DIM
            a1, a2 = made[r : r + 32], made[r + 32 : r + 64]
            q = jnp.concatenate([a1 * c_ - a2 * s_, a2 * c_ + a1 * s_], axis=0).astype(BF16).astype(F32)
            qa[h, :, at] = jnp.concatenate([q * 0.125, hot, rest], axis=0).astype(BF16)
            r += width
            a1, a2 = made[r : r + 32], made[r + 32 : r + 64]
            k = jnp.concatenate([a1 * c_ - a2 * s_, a2 * c_ + a1 * s_], axis=0)
            kt[h * HEAD_DIM : (h + 1) * HEAD_DIM, at] = k.astype(BF16)
            ka[h, at, :] = jnp.concatenate([k, (1.0 - hot) * far_below, rest], axis=0).T.astype(BF16)
            r += width
            v = made[r : r + 64]
            va[h, :, at] = jnp.concatenate([v, one_row], axis=0).astype(BF16)
            vn[h, at, :] = jnp.concatenate([v, jnp.zeros_like(v)], axis=0).T[:, :HEAD_DIM].astype(BF16)
        return 0

    lax.fori_loop(0, 4, project, 0)
    for src, dst in ((qa, qa_out), (ka, ka_out), (kt, kt_out), (vn, vn_out), (va, va_out)):
        moved.append(moves.start(src, dst))
    ff0.last()
    ff_z2.wait_recv()
    moved += [moves.start(zv, zb.at[1]), moves.start(zv, zl)]
    ff_z1.wait_recv()
    for move in moved:
        move.wait()
    links.wait_sends()
    for k, to in ((0, near), (1, far), (2, near), (3, near)):

        @pl.when(away == k)
        def _(k=k, to=to):
            for ch in range(CHUNKS):
                copy(0, k, ch, own(ch), to).wait_send()
                if k == 1:
                    for j in (2, 3):
                        copy(0, j, ch, held(j, ch), to).wait_send()
                if k < 2:
                    for j in range(4):
                        copy(1, j, ch, own(ch) if j == k else held(j, ch), me.sib).wait_send()


FIRST, LAST = 256, 512


def list_pairs(first, end, pairs):
    idle = 8 * 16 + 8
    pairs[0] = idle

    def of_query(i, n):
        lo = first[0, i * BLK] // BLK
        hi = (end[0, i * BLK + BLK - 1] + (BLK - 1)) // BLK

        def of_key(j, n):
            pairs[n] = i * 16 + j + jnp.where(j == lo, FIRST, 0) + jnp.where(j == hi - 1, LAST, 0)
            return n + 1

        return lax.fori_loop(lo, hi, of_key, n)

    n = lax.fori_loop(0, 2048 // BLK, of_query, 1)
    for more in range(3):
        pairs[n + more] = idle
    return n - 1


def split_pair(code):
    return (code // 16) % 16, code % 16


def columns(block):
    return pl.ds(pl.multiple_of(block * BLK, BLK), BLK)


def real(block):
    return jnp.where(block == 8, 0, block)


def attend_forward_kernel(
    first, end, w_in, qa_in, ka_in, va_in, ot, logsum, part,
    w, qa, ka, va, mx, acc, s0, s1, p0, p1, al0, al1, pairs, sem,
):
    heads = 3
    width = heads * HEAD_DIM
    moves = Moves(sem)
    loads = [moves.start(src, dst) for src, dst in ((qa_in, qa), (ka_in, ka), (va_in, va), (w_in.at[pl.ds(3 * width, width)], w))]
    count = list_pairs(first, end, pairs)

    def score(t, s):
        i, j = split_pair(pairs[t])
        at, here = columns(real(i)), columns(real(j))
        for h in range(heads):
            s[h] = nn(ka[h, here, :], qa[h, :, at])

    def weigh(t, s, p, al):
        fresh = pairs[t] & FIRST
        for h in range(heads):
            scores = s[h]
            before = jnp.where(fresh > 0, -3e38, mx[h])
            largest = jnp.maximum(before, jnp.max(scores, axis=0, keepdims=True))
            p[h] = jnp.exp(scores - largest).astype(BF16)
            al[h] = jnp.exp(before - largest)
            mx[h] = largest

    def gather(t, p, al):
        code = pairs[t]
        i, j = split_pair(code)
        here = columns(real(j))
        for h in range(heads):
            acc[h] = acc[h] * al[h] + nn(va[h, :, here], p[h])

        @pl.when((code & LAST) > 0)
        def _():
            at = columns(i)
            for h in range(heads):
                total = acc[h, 64:65, :]
                ot[h * HEAD_DIM : (h + 1) * HEAD_DIM, at] = (acc[h, :64, :] / total).astype(BF16)
                logsum[pl.ds(h, 1), at] = mx[h] + jnp.log(total)

    def step(u, _):
        t = 2 * u + 1
        gather(t - 1, p1, al1)
        weigh(t, s0, p0, al0)
        score(t + 1, s1)
        gather(t, p0, al0)
        weigh(t + 1, s1, p1, al1)
        score(t + 2, s0)
        return 0

    acc[...] = jnp.zeros_like(acc)
    p1[...] = jnp.zeros_like(p1)
    al1[...] = jnp.zeros_like(al1)
    for load in loads:
        load.wait()
    score(1, s0)
    lax.fori_loop(0, (count + 2) // 2, step, 0)
    for e in range(4):
        part[e] = tn(ot[:, e * 512 : (e + 1) * 512], w[...]).astype(BF16)


def attend_backward_kernel(
    first, end, gb_in, tok_in, w_in, qa_in, ka_in, kt_in, vn_in, ot_in, logsum, cos_in, sin_in, grads, part,
    gb, tok, w, qa, ka, kt, vn, ot, cos, sin, dot_, inner, dq, dk, dv, gp, s0, s1, r0, r1, p0, p1, d0, d1, pairs, sem,
):
    heads = 3
    width = heads * HEAD_DIM
    moves = Moves(sem)
    loads = [
        moves.start(src, dst)
        for src, dst in (
            (w_in, w), (ot_in, ot), (gb_in, gb), (qa_in, qa), (ka_in, ka), (vn_in, vn), (kt_in, kt), (cos_in, cos),
            (sin_in, sin), (tok_in, tok),
        )
    ]
    for total in (dq, dk, dv, p1, d1):
        total[...] = jnp.zeros_like(total)
    count = list_pairs(first, end, pairs)
    for load in loads[:3]:
        load.wait()

    def begin(e, _):
        at = pl.ds(pl.multiple_of(e * 512, 512), 512)
        made = nt(w[3 * width :], gb[e]).astype(BF16)
        dot_[:, at] = made
        product = made.astype(F32) * ot[:, at].astype(F32)
        for h in range(heads):
            inner[pl.ds(h, 1), at] = jnp.sum(product[h * HEAD_DIM : (h + 1) * HEAD_DIM], axis=0, keepdims=True)
        return 0

    lax.fori_loop(0, 4, begin, 0)
    for load in loads[3:]:
        load.wait()

    def score(t, s, r):
        i, j = split_pair(pairs[t])
        at, here = columns(real(i)), columns(real(j))
        for h in range(heads):
            rows = slice(h * HEAD_DIM, (h + 1) * HEAD_DIM)
            s[h] = nn(ka[h, here, :], qa[h, :, at])
            r[h] = nn(vn[h, here, :], dot_[rows, at])

    def weigh(t, s, r, p, d):
        at = columns(real(split_pair(pairs[t])[0]))
        for h in range(heads):
            probability = jnp.exp(s[h] - logsum[pl.ds(h, 1), at])
            p[h] = probability.astype(BF16)
            d[h] = (probability * (r[h] - inner[pl.ds(h, 1), at])).astype(BF16)

    def gather(t, p, d):
        i, j = split_pair(pairs[t])
        at, here = columns(real(i)), columns(real(j))
        to_query, to_key = columns(i), columns(j)
        for h in range(heads):
            rows = slice(h * HEAD_DIM, (h + 1) * HEAD_DIM)
            dv[rows, to_key] += nt(dot_[rows, at], p[h])
            dk[rows, to_key] += nt(qa[h, :HEAD_DIM, at], d[h])
            dq[rows, to_query] += nn(kt[rows, here], d[h])

    def step(u, _):
        t = 2 * u + 1
        gather(t - 1, p1, d1)
        weigh(t, s0, r0, p0, d0)
        score(t + 1, s1, r1)
        gather(t, p0, d0)
        weigh(t + 1, s1, r1, p1, d1)
        score(t + 2, s0, r0)
        return 0

    score(1, s0, r0)
    lax.fori_loop(0, (count + 2) // 2, step, 0)

    def turn(e, _):
        at = pl.ds(pl.multiple_of(e * 512, 512), 512)
        c, s = cos[:, at], sin[:, at]
        for h in range(heads):
            r = h * HEAD_DIM
            for first, total, scale in ((0, dq, 0.125), (width, dk, 1.0)):
                d1_, d2_ = total[r : r + 32, at] * scale, total[r + 32 : r + 64, at] * scale
                gp[first + r : first + r + 64, at] = jnp.concatenate(
                    [d1_ * c + d2_ * s, d2_ * c - d1_ * s], axis=0
                ).astype(BF16)
        gp[2 * width :, at] = dv[:, at].astype(BF16)
        return 0

    lax.fori_loop(0, 4, turn, 0)
    for e in range(4):
        part[e] = tn(gp[:, e * 512 : (e + 1) * 512], w[: 3 * width]).astype(BF16)
    for block in range(4):
        if block < 3:
            rows = slice(block * width, (block + 1) * width)
            made = sum(nn(gp[rows, e * 512 : (e + 1) * 512], tok[e]) for e in range(4))
        else:
            made = sum(nn(ot[:, e * 512 : (e + 1) * 512], gb[e]) for e in range(4))
        grads[block * width : (block + 1) * width] = made.astype(BF16)


def row_mean(v):
    return jnp.mean(v, axis=-1, keepdims=True)


def norm_forward(summed):
    centred = summed - row_mean(summed)
    inverse = lax.rsqrt(row_mean(centred * centred) + epsilon)
    return centred * inverse, inverse


def norm_backward(scaled, normalized, inverse):
    return inverse * (scaled - row_mean(scaled) - normalized * row_mean(scaled * normalized))


def feed_forward_kernel(
    tok, part_in, cot_in, gain, bias, wf0, zb, zx, zy, zc,
    out, gz1, gb, sums, keep_a, keep_b, send_a, send_b, zs_out,
    part, own_g, w, slope_g, slope_u, hid, nb, nbt, gm, gmt, total, norm1, inv1, dw, lw, xs, cot, out_v, from_core, from_z, to_z,
    f1a, f1b, f2a, f2b, send, recv, local, out_sem, trade_sem,
):
    me = Place()
    greet((me.sib, me.xn, me.yn, me.z1, me.pair))
    links = Links(send, recv)
    moves = Moves(local)
    partial = moves.start(part_in, part)
    loads = [moves.start(tok.at[me.slot], xs), moves.start(wf0, w.at[0])]
    for ez in (2, 1):
        for place, src in ((me.place, zb), (me.x_place, zx), (me.y_place, zy)):
            loads.append(moves.start(src.at[ez - 1], view_3d(w.at[ez])(place, 0, 96)))
    loads.append(moves.start(zc, view_3d(w.at[3])(me.place, 0, 96)))

    def cot_here():
        return pltpu.make_async_copy(cot_in, cot, local.at[15])

    def cot_there():
        return pltpu.make_async_remote_copy(
            src_ref=cot_in, dst_ref=cot, send_sem=trade_sem.at[0], recv_sem=trade_sem.at[1], device_id=me.pair,
            device_id_type=MESH,
        )

    def rows(ch):
        return pl.ds(ch * CHUNK, CHUNK)

    cores = [
        [links.start(part_in.at[shard, rows(ch)], from_core.at[i, rows(ch)], me.sib) for ch in range(CHUNKS)]
        for i, shard in ((1, me.slot3), (0, me.slot2))
    ]
    ff2, ff1 = [Corner(me, links, view_3d(w.at[ez]), *(src.at[ez - 1] for src in (zb, zx, zy))) for ez in (2, 1)]
    ff3 = Spread(me, links, view_3d(w.at[3]), zc)
    zs = []
    partial.wait()
    for ch in range(CHUNKS):
        cores[0][ch].wait_recv()
        at = rows(ch)
        to_z[at] = (part[me.slot1, at].astype(F32) + from_core[1, at].astype(F32)).astype(BF16)
        zs.append(links.start(to_z.at[at], from_z.at[at], me.z1))

    @pl.when(me.cross == 0)
    def _():
        cot_here().start()

    @pl.when(me.cross == 1)
    def _():
        cot_there().start()

    ff2.third()
    ff1.third()
    loads[0].wait()
    loads[1].wait()
    def forward(ez, at=pl.ds(0, 512)):
        gate = nn(nb[at], w[ez, 0])
        up = nn(nb[at], w[ez, 1])
        sig = 1.0 / (1.0 + jnp.exp(-gate))
        active = gate * sig
        low = (active * up).astype(BF16)
        hid[ez, at] = low
        slope_u[ez, at] = active.astype(BF16)
        slope_g[ez, at] = (up * sig * (1.0 + gate * (1.0 - sig))).astype(BF16)
        total[at] += nn(low, w[ez, 2])

    for ch in range(CHUNKS):
        if ch == CHUNKS // 2:
            forward(0, pl.ds(0, 256))
            ff3.second()
            for load in loads[2:]:
                load.wait()
            ff2.last()
            forward(2, pl.ds(0, 256))
        cores[1][ch].wait_recv()
        zs[ch].wait_recv()
        at = rows(ch)
        branch = part[me.slot, at].astype(F32) + from_core[0, at].astype(F32) + from_z[at].astype(F32)
        n1, i1 = norm_forward(xs[at].astype(F32) + branch)
        norm1[at] = n1
        inv1[at] = jnp.broadcast_to(i1, (CHUNK, 128))
        normed = n1 * gain[0:1, :] + bias[0:1, :]
        total[at] = normed
        nb[at] = normed.astype(BF16)
        nbt[:, ch * CHUNK : (ch + 1) * CHUNK] = normed.T.astype(BF16)

    forward(0, pl.ds(256, 256))
    forward(2, pl.ds(256, 256))
    ff3.third()
    ff1.last()
    forward(1)
    ff3.last()
    forward(3)
    n2, i2 = norm_forward(total[...])
    out_v[...] = (n2 * gain[1:2, :] + bias[1:2, :]).astype(BF16)

    def out_here():
        return pltpu.make_async_copy(out_v, out, local.at[14])

    def out_there():
        return pltpu.make_async_remote_copy(
            src_ref=out_v, dst_ref=out, send_sem=trade_sem.at[2], recv_sem=trade_sem.at[3], device_id=me.pair,
            device_id_type=MESH,
        )

    @pl.when(me.cross == 0)
    def _():
        out_here().start()

    @pl.when(me.cross == 1)
    def _():
        out_there().start()


    @pl.when(me.cross == 0)
    def _():
        cot_here().wait()

    @pl.when(me.cross == 1)
    def _():
        cot_there().wait()

    g = cot[...].astype(F32)
    sums[1:2, :] = jnp.sum(g * n2, axis=0, keepdims=True)
    sums[3:4, :] = jnp.sum(g, axis=0, keepdims=True)
    gz2 = norm_backward(g * gain[1:2, :], n2, i2)
    total[...] = gz2
    gm[...] = gz2.astype(BF16)
    gmt[...] = gz2.T.astype(BF16)

    def block(quad, core):
        return pl.ds(pl.multiple_of((quad * 2 + core) * 96, 32), 96)

    order = (3, 1, 0, 2)
    halves = []
    first, last = pl.ds(0, 48), pl.ds(48, 48)

    upper, lower = pl.ds(0, 256), pl.ds(256, 256)

    def slopes(ez, at=pl.ds(0, 512)):
        grad_hidden = nt(gm[at], w[ez, 2])
        gate = (grad_hidden * slope_g[ez, at].astype(F32)).astype(BF16)
        up = (grad_hidden * slope_u[ez, at].astype(F32)).astype(BF16)
        slope_g[ez, at] = gate
        slope_u[ez, at] = up
        total[at] += nt(gate, w[ez, 0]) + nt(up, w[ez, 1])

    def weights(n):
        i, ez = n % 2, order[n]
        if n >= 2:
            for copy in halves[n - 2]:
                copy.wait_send()
        dw[i, 2] = nn(gmt[...], hid[ez]).astype(BF16)
        dw[i, 0] = nn(nbt[...], slope_g[ez]).astype(BF16)
        dw[i, 1] = nn(nbt[...], slope_u[ez]).astype(BF16)
        halves.append([links.make(dw.at[i, :, block(quad, 1 - me.c)], lw.at[n, quad], me.sib) for quad in range(4)])
        for copy in halves[n]:
            copy.start()

    def settle(n):
        for quad in range(4):
            halves[n][quad].wait_recv()
            for m in range(3):
                lw[n, quad, m] = (lw[n, quad, m].astype(F32) + dw[n % 2, m, block(quad, me.c)].astype(F32)).astype(BF16)

    def plane_first():
        return [
            (
                links.start(lw.at[0, (1 - me.y) * 2 + o, :, first], f1a.at[o], me.yn),
                links.start(lw.at[0, o * 2 + 1 - me.x, :, last], f1b.at[o], me.xn),
            )
            for o in range(2)
        ]

    def plane_second(plane_1):
        for o in range(2):
            plane_1[o][0].wait_recv()
            f1a[o] = (f1a[o].astype(F32) + lw[0, me.y * 2 + o, :, first].astype(F32)).astype(BF16)
            plane_1[o][1].wait_recv()
            f1b[o] = (f1b[o].astype(F32) + lw[0, o * 2 + me.x, :, last].astype(F32)).astype(BF16)
        return links.start(f1a.at[1 - me.x], f2a, me.xn), links.start(f1b.at[1 - me.y], f2b, me.yn)

    def plane_last(plane_2):
        plane_2[0].wait_recv()
        zs_out[0] = (f1a[me.x].astype(F32) + f2a[...].astype(F32)).astype(BF16)
        plane_2[1].wait_recv()
        zs_out[1] = (f1b[me.y].astype(F32) + f2b[...].astype(F32)).astype(BF16)

    def stores(n):
        made = []
        for oy in range(2):
            for ox in range(2):
                src = lw.at[n, oy * 2 + ox]
                made.append((me.y == oy, src.at[:, first], keep_a.at[n - 1, ox], send_a.at[n - 1, ox]))
                made.append((me.x == ox, src.at[:, last], keep_b.at[n - 1, oy], send_b.at[n - 1, oy]))
        return made

    def store(n):
        for number, (here, src, kept, sent) in enumerate(stores(n)):

            @pl.when(here)
            def _(number=number, src=src, kept=kept):
                pltpu.make_async_copy(src, kept, out_sem.at[n - 1, number]).start()

            @pl.when(jnp.logical_not(here))
            def _(number=number, src=src, sent=sent):
                pltpu.make_async_copy(src, sent, out_sem.at[n - 1, number]).start()

    slopes(3)
    weights(0)
    slopes(1)
    settle(0)
    plane_1 = plane_first()
    to_pair, to_core, on_core = [], [], []
    for ch in range(CHUNKS):
        if ch % 2 == 0:
            slopes(0, lower if ch else upper)
            slopes(2, lower if ch else upper)
        at = rows(ch)
        made = norm_backward(total[at] * gain[0:1, :], norm1[at], inv1[at, 0:1])
        gz1[at] = made
        own_g[at] = made.astype(BF16)
        mine = gb.at[me.slot, at]
        to_pair.append(links.start(own_g.at[at], mine, me.z1))
        to_core.append(links.start(own_g.at[at], mine, me.sib))
    kept_g = moves.start(own_g, gb.at[me.slot])
    g = total[...]
    sums[0:1, :] = jnp.sum(g * norm1[...], axis=0, keepdims=True)
    sums[2:3, :] = jnp.sum(g, axis=0, keepdims=True)
    sums[4:8, :] = jnp.zeros((4, 768), F32)
    weights(1)
    weights(2)
    settle(1)
    store(1)
    plane_2 = plane_second(plane_1)
    weights(3)
    settle(2)
    store(2)
    settle(3)
    store(3)
    for ch in range(CHUNKS):
        to_pair[ch].wait_recv()
        other = gb.at[me.slot1, rows(ch)]
        on_core.append(links.start(other, other, me.sib))
    plane_last(plane_2)
    kept_g.wait()
    for copy in to_core + on_core:
        copy.wait_recv()
    for n in (1, 2, 3):
        for number, (_, src, kept, _) in enumerate(stores(n)):
            pltpu.make_async_copy(src, kept, out_sem.at[n - 1, number]).wait()
    for n in (2, 3):
        for copy in halves[n]:
            copy.wait_send()
    links.wait_sends()

    @pl.when(me.cross == 0)
    def _():
        out_here().wait()

    @pl.when(me.cross == 1)
    def _():
        out_there().wait()


def finish_kernel(
    extra, keep_a_in, keep_b_in, recv_a_in, recv_b_in, zr_in, ga_in, part_in, gz1_in, sums_in,
    g_ff, g_attn, g_tok, sums,
    keep_a, keep_b, recv_a, recv_b, zr, ga, part, gz1, block,
    sa, sb, f2a, f2b, va, f3, f4, fe, a_in, a_mid, a_out, a_fin, a_two, ae, from_core, from_z, to_z, trade_out, trade_in, sum_in,
    send, recv, a_send, a_recv, local,
):
    me = Place()
    moves = Moves(local)
    part_here, ga_here = moves.start(part_in, part), moves.start(ga_in, ga)
    ff_here = [
        moves.start(src, dst)
        for src, dst in ((keep_a_in, keep_a), (recv_a_in, recv_a), (keep_b_in, keep_b), (recv_b_in, recv_b), (zr_in, zr))
    ]
    gz1_here = moves.start(gz1_in, gz1)
    bits = [{"dp": me.p + bit - 2 * bit * ((me.p // bit) % 2)} for bit in extra]
    greet([me.sib, me.xn, me.yn, me.z1, me.z2, me.pair] + bits)
    links = Links(send, recv)

    def rows(ch):
        return pl.ds(ch * CHUNK, CHUNK)

    def add(*terms):
        return sum(t.astype(F32) for t in terms).astype(BF16)

    part_here.wait()
    cores = [
        [links.start(part.at[shard, rows(ch)], from_core.at[i, rows(ch)], me.sib) for ch in range(CHUNKS)]
        for i, shard in ((1, me.slot3), (0, me.slot2))
    ]

    def half(oy, ox, h):
        return pl.ds(pl.multiple_of((oy * 2 + ox) * 192 + h * 96, 32), 96)

    attn_1 = []
    ga_here.wait()
    for o in range(2):
        attn_1.append(links.start(ga.at[half(1 - me.y, o, 0)], a_in.at[0, o], me.yn))
        attn_1.append(links.start(ga.at[half(o, 1 - me.x, 1)], a_in.at[1, o], me.xn))

    sums[...] = sums_in[...]
    around = [me.sib, me.xn, me.yn, me.z1, me.z2] + bits
    small = [links.start(sums, sum_in.at[0], around[0])]

    def small_step():
        n = len(small)
        small[-1].wait_recv()
        small[-1].wait_send()
        links.started = [copy for copy in links.started if copy is not small[n - 1]]
        sums[...] += sum_in[n - 1]
        if n < len(around):
            small.append(links.start(sums, sum_in.at[n], around[n]))

    ff_2 = {}

    def plane(ez):
        sa[ez] = add(keep_a[ez, 1 - me.x], recv_a[ez, 1 - me.x])
        sb[ez] = add(keep_b[ez, 1 - me.y], recv_b[ez, 1 - me.y])
        ff_2[ez] = (links.start(sa.at[ez], f2a.at[ez], me.xn), links.start(sb.at[ez], f2b.at[ez], me.yn))

    def planed(ez):
        ff_2[ez][0].wait_recv()
        va[ez, 0] = add(keep_a[ez, me.x], recv_a[ez, me.x], f2a[ez], *([zr[0]] if ez == 2 else []))
        ff_2[ez][1].wait_recv()
        va[ez, 1] = add(keep_b[ez, me.y], recv_b[ez, me.y], f2b[ez], *([zr[1]] if ez == 2 else []))

    for load in ff_here:
        load.wait()
    plane(2)
    zs = []
    for ch in range(CHUNKS):
        cores[0][ch].wait_recv()
        at = rows(ch)
        to_z[at] = add(part[me.slot1, at], from_core[1, at])
        zs.append(links.start(to_z.at[at], from_z.at[at], me.z1))
    for copy in attn_1:
        copy.wait_recv()
    small_step()
    a_mid[0] = add(ga[half(me.y, 1 - me.x, 0)], a_in[0, 1 - me.x])
    a_mid[1] = add(ga[half(1 - me.y, me.x, 1)], a_in[1, 1 - me.y])
    attn_2 = [links.start(a_mid.at[0], a_out.at[0], me.xn), links.start(a_mid.at[1], a_out.at[1], me.yn)]
    planed(2)
    ff_4 = links.start(va.at[2], f4, me.z2)
    for copy in attn_2:
        copy.wait_recv()
    small_step()
    a_fin[:96] = add(ga[half(me.y, me.x, 0)], a_in[0, me.x], a_out[0])
    a_fin[96:] = add(ga[half(me.y, me.x, 1)], a_in[1, me.y], a_out[1])

    def attn_copy(n, src, dst, to):
        return pltpu.make_async_remote_copy(
            src_ref=src, dst_ref=dst, send_sem=a_send.at[n], recv_sem=a_recv.at[n], device_id=to, device_id_type=MESH
        )

    def quarter(oy, ox, first=0, size=192):
        return g_attn.at[pl.ds(pl.multiple_of((oy * 2 + ox) * 192 + first, 32), size)]

    def attn_over():
        return attn_copy(0, a_fin, a_two, me.z2)

    @pl.when(me.cross == 1)
    def _():
        attn_over().start()

    plane(0)
    plane(1)
    planed(0)
    ff_3 = links.start(va.at[0], f3, me.z1)
    planed(1)
    small_step()

    trades = [
        pltpu.make_async_remote_copy(
            src_ref=trade_out.at[rows(ch)], dst_ref=trade_in.at[rows(ch)], send_sem=a_send.at[8 + ch],
            recv_sem=a_recv.at[8 + ch], device_id=me.pair, device_id_type=MESH,
        )
        for ch in range(CHUNKS)
    ]
    mine = quarter(me.y, me.x)

    def attn_send(n, src, to):
        return attn_copy(n, src, src, to)

    block_x, block_y = quarter(me.y, 1 - me.x), quarter(1 - me.y, me.x)
    low_x, high_y = quarter(me.y, 1 - me.x, 0, 96), quarter(1 - me.y, me.x, 96, 96)
    corner = quarter(1 - me.y, 1 - me.x)

    @pl.when(me.cross == 0)
    def _():
        attn_over().wait_recv()
        total = add(a_fin[...], a_two[...])
        for n, bit in enumerate(bits):
            ae[n, 0] = total
            step = attn_copy(16 + n, ae.at[n, 0], ae.at[n, 1], bit)
            step.start()
            step.wait()
            total = add(total, ae[n, 1])
        g_attn[pl.ds(pl.multiple_of((me.y * 2 + me.x) * 192, 32), 192)] = total
        attn_send(1, mine, me.xn).start()
        attn_send(2, mine, me.yn).start()
        attn_send(3, mine, me.sib).start()

    gz1_here.wait()
    for ch in range(CHUNKS):
        cores[1][ch].wait_recv()
        zs[ch].wait_recv()
        at = rows(ch)
        got = gz1[at] + (part[me.slot, at].astype(F32) + from_core[0, at].astype(F32) + from_z[at].astype(F32))

        @pl.when(me.cross == 0)
        def _(at=at, got=got):
            g_tok[at] = got

        @pl.when(me.cross == 1)
        def _(at=at, got=got, ch=ch):
            trade_out[at] = got.astype(BF16)

    small_step()


    @pl.when(me.cross == 0)
    def _():
        attn_send(1, block_x, me.xn).wait_recv()
        attn_send(4, low_x, me.yn).start()
        attn_send(5, block_x, me.sib).start()
        attn_send(2, block_y, me.yn).wait_recv()
        attn_send(6, high_y, me.xn).start()
        attn_send(7, block_y, me.sib).start()

    ff_3.wait_recv()
    ff_4.wait_recv()
    total = add(va[1], f3[...], f4[...])
    for n, bit in enumerate(bits):
        fe[n, 0] = total
        step = links.start(fe.at[n, 0], fe.at[n, 1], bit)
        step.wait_recv()
        total = add(total, fe[n, 1])
    for h in range(2):
        block[:, h * 48 : (h + 1) * 48] = total[h]
    spread = Spread(me, links, view_3d(g_ff), block)
    kept = moves.start(block, view_3d(g_ff)(me.place, 0, 96))

    @pl.when(me.cross == 1)
    def _():
        for ch in range(CHUNKS):
            trades[ch].start()

    while len(small) < len(around):
        small_step()
    spread.second()
    small_step()

    @pl.when(me.cross == 0)
    def _():
        attn_send(4, low_x, me.yn).wait_recv()
        attn_send(6, high_y, me.xn).wait_recv()
        attn_send(12, corner, me.sib).start()
        for n, src, to in (
            (1, mine, me.xn), (2, mine, me.yn), (3, mine, me.sib), (4, low_x, me.yn), (5, block_x, me.sib),
            (6, high_y, me.xn), (7, block_y, me.sib), (12, corner, me.sib),
        ):
            attn_send(n, src, to).wait_send()

    @pl.when(me.cross == 1)
    def _():
        for ch in range(CHUNKS):
            trades[ch].wait_recv()
            g_tok[rows(ch)] = trade_in[rows(ch)].astype(F32)
        attn_over().wait_send()
        for n, src in ((3, mine), (5, block_x), (7, block_y), (12, corner)):
            attn_send(n, src, me.sib).wait_recv()
        for ch in range(CHUNKS):
            trades[ch].wait_send()

    spread.third()
    spread.last()
    kept.wait()
    links.wait_sends()


def widen_kernel(attn, out_rows, gate_up, down, tok, sums, g_qkv, g_out, g_gate_up, g_down, g_tok, gains, biases):
    g_qkv[...] = attn[...].astype(F32)
    g_out[...] = out_rows[...].astype(F32)
    g_gate_up[:, 0, :] = gate_up[0].astype(F32)
    g_gate_up[:, 1, :] = gate_up[1].astype(F32)
    g_down[...] = down[0].astype(F32).T
    g_tok[0] = tok[...]
    gains[...] = sums[0:2, :]
    biases[...] = sums[2:4, :]


def solution(mesh):
    dp, tensor = mesh.shape["dp"], mesh.shape["tensor"]
    assert tensor == 4 and dp >= 8 and dp & (dp - 1) == 0
    extra = [1 << b for b in range(3, dp.bit_length() - 1)]
    def over(x, bit):
        return lax.ppermute(x, "dp", [(i, i ^ bit) for i in range(dp)])

    smem = pl.BlockSpec(memory_space=pltpu.SMEM)
    vmem = pl.BlockSpec(memory_space=pltpu.VMEM)
    hbm = pl.BlockSpec(memory_space=pl.ANY)

    def shape(*dims, dtype=BF16):
        return jax.ShapeDtypeStruct(dims, dtype)

    far = pl.BlockSpec(memory_space=pltpu.HBM)

    def held(*dims, dtype=BF16):
        return pltpu.HBM(dims, dtype)

    def dma(*dims):
        return pltpu.SemaphoreType.DMA(dims)

    def params(mib, number=None):
        if number is None:
            return pltpu.CompilerParams(vmem_limit_bytes=mib << 20)
        return pltpu.CompilerParams(vmem_limit_bytes=mib << 20, collective_id=number, has_side_effects=True)

    def on_device(tokens, segments, w_qkv, w_out, w_gate_up, w_down, norm_gain, norm_bias, cotangent):
        place = lax.axis_index("dp") & 7

        rows = lax.dynamic_slice(w_gate_up, (place * 96, 0, 0), (96, 2, 768))
        block = jnp.stack([rows[:, 0], rows[:, 1], lax.dynamic_slice(w_down, (place * 96, 0), (96, 768))])

        length = segments.shape[1]
        inverse = jnp.asarray(np.exp(-2.0 * np.arange(HEAD_DIM // 2) / HEAD_DIM * log_base).astype(np.float32)[:, None])
        tok, w, wf0, zb, zl, qa, ka, kt, vn, va, cos, sin, seg, first, end = pl.pallas_call(
            start_kernel,
            name="start",
            out_shape=(
                held(4, 512, 768), held(768, 768), held(3, 768, 768), held(2, 3, 96, 768), held(3, 96, 768),
                held(3, 128, length), held(3, length, 128), held(192, length), held(3, length, 64), held(3, 80, length),
                held(32, length, dtype=F32), held(32, length, dtype=F32),
                *(shape(1, length, dtype=jnp.int32),) * 3,
            ),
            in_specs=[hbm] * 3 + [vmem] * 3,
            out_specs=(far,) * 12 + (vmem,) * 3,
            scratch_shapes=[
                pltpu.VMEM((768, 768), BF16),
                pltpu.VMEM((3, 96, 768), BF16),
                pltpu.VMEM((4, 512, 768), BF16),
                pltpu.VMEM((768, 768), BF16),
                pltpu.VMEM((768, 768), BF16),
                pltpu.VMEM((1, length), jnp.int32),
                pltpu.VMEM((32, length), F32),
                pltpu.VMEM((32, length), F32),
                pltpu.VMEM((3, 128, length), BF16),
                pltpu.VMEM((3, length, 128), BF16),
                pltpu.VMEM((192, length), BF16),
                pltpu.VMEM((3, length, 64), BF16),
                pltpu.VMEM((3, 80, length), BF16),
                dma(2, 4, CHUNKS), dma(4, CHUNKS), dma(40), dma(40), dma(32),
            ],
            compiler_params=params(62, 0),
        )(tokens[0], w_qkv.transpose(1, 2, 0).reshape(576, 768), w_out, block, segments, inverse)

        zc = lax.ppermute(zl, "tensor", [(i, i ^ 1) for i in range(tensor)])
        zx, zy = over(zb, 2), over(zb, 4)

        ot, logsum, part = pl.pallas_call(
            attend_forward_kernel,
            name="attend_forward",
            out_shape=(held(192, length), shape(8, length, dtype=F32), held(4, 512, 768)),
            in_specs=[smem] * 2 + [far] * 4,
            out_specs=(vmem,) * 3,
            scratch_shapes=[
                pltpu.VMEM((192, 768), BF16),
                pltpu.VMEM((3, 128, length), BF16),
                pltpu.VMEM((3, length, 128), BF16),
                pltpu.VMEM((3, 80, length), BF16),
                pltpu.VMEM((3, 1, BLK), F32),
                pltpu.VMEM((3, 80, BLK), F32),
                *[pltpu.VMEM((3, BLK, BLK), F32)] * 2,
                *[pltpu.VMEM((3, BLK, BLK), BF16)] * 2,
                *[pltpu.VMEM((3, 1, BLK), F32)] * 2,
                pltpu.SMEM((72,), jnp.int32),
                dma(4),
            ],
            compiler_params=params(62),
            cost_estimate=pl.CostEstimate(flops=20_000_000_000, bytes_accessed=24_000_000, transcendentals=6_000_000),
        )(first, end, w, qa, ka, va)

        plane = (3, 2, 3, 48, 768)
        out, gz1, gb, sums, keep_a, keep_b, send_a, send_b, zs = pl.pallas_call(
            feed_forward_kernel,
            name="feed_forward",
            out_shape=(
                held(512, 768), shape(512, 768, dtype=F32), held(4, 512, 768), shape(8, 768, dtype=F32),
                *(held(*plane),) * 4, shape(2, 3, 48, 768),
            ),
            in_specs=[far, far, hbm, vmem, vmem] + [far] * 5,
            out_specs=(far, vmem, far, vmem) + (far,) * 4 + (vmem,),
            scratch_shapes=[
                pltpu.VMEM((4, 512, 768), BF16),
                pltpu.VMEM((512, 768), BF16),
                pltpu.VMEM((4, 3, 768, 768), BF16),
                pltpu.VMEM((4, 512, 768), BF16),
                pltpu.VMEM((4, 512, 768), BF16),
                pltpu.VMEM((4, 512, 768), BF16),
                pltpu.VMEM((512, 768), BF16),
                pltpu.VMEM((768, 512), BF16),
                pltpu.VMEM((512, 768), BF16),
                pltpu.VMEM((768, 512), BF16),
                pltpu.VMEM((512, 768), F32),
                pltpu.VMEM((512, 768), F32),
                pltpu.VMEM((512, 128), F32),
                pltpu.VMEM((2, 3, 768, 768), BF16),
                pltpu.VMEM((4, 4, 3, 96, 768), BF16),
                pltpu.VMEM((512, 768), BF16),
                pltpu.VMEM((512, 768), BF16),
                pltpu.VMEM((512, 768), BF16),
                pltpu.VMEM((2, 512, 768), BF16),
                pltpu.VMEM((512, 768), BF16),
                pltpu.VMEM((512, 768), BF16),
                pltpu.VMEM((2, 3, 48, 768), BF16),
                pltpu.VMEM((2, 3, 48, 768), BF16),
                pltpu.VMEM((3, 48, 768), BF16),
                pltpu.VMEM((3, 48, 768), BF16),
                dma(80), dma(80), dma(16), dma(3, 8), dma(4),
            ],
            compiler_params=params(62, 1),
            cost_estimate=pl.CostEstimate(flops=22_000_000_000, bytes_accessed=36_000_000, transcendentals=3_000_000),
        )(tok, part, cotangent[0], norm_gain, norm_bias, wf0, zb, zx, zy, zc)

        recv_a, recv_b = over(send_a, 4), over(send_b, 2)
        zr = lax.ppermute(zs, "tensor", [(i, i ^ 1) for i in range(tensor)])

        grads, part = pl.pallas_call(
            attend_backward_kernel,
            name="attend_backward",
            out_shape=(shape(768, 768), shape(4, 512, 768)),
            in_specs=[smem] * 2 + [far] * 8 + [vmem] + [far] * 2,
            out_specs=(vmem,) * 2,
            scratch_shapes=[
                pltpu.VMEM((4, 512, 768), BF16),
                pltpu.VMEM((4, 512, 768), BF16),
                pltpu.VMEM((768, 768), BF16),
                pltpu.VMEM((3, 128, length), BF16),
                pltpu.VMEM((3, length, 128), BF16),
                pltpu.VMEM((192, length), BF16),
                pltpu.VMEM((3, length, 64), BF16),
                pltpu.VMEM((192, length), BF16),
                pltpu.VMEM((32, length), F32),
                pltpu.VMEM((32, length), F32),
                pltpu.VMEM((192, length), BF16),
                pltpu.VMEM((8, length), F32),
                *[pltpu.VMEM((192, length + BLK), F32)] * 3,
                pltpu.VMEM((576, length), BF16),
                *[pltpu.VMEM((3, BLK, BLK), F32)] * 4,
                *[pltpu.VMEM((3, BLK, BLK), BF16)] * 4,
                pltpu.SMEM((72,), jnp.int32),
                dma(10),
            ],
            compiler_params=params(62),
            cost_estimate=pl.CostEstimate(flops=40_000_000_000, bytes_accessed=24_000_000, transcendentals=6_000_000),
        )(first, end, gb, tok, w, qa, ka, kt, vn, ot, logsum, cos, sin)

        spare = max(len(extra), 1)
        half = (48, 768)
        g_ff, g_attn, g_tok, sums = pl.pallas_call(
            functools.partial(finish_kernel, extra),
            name="finish",
            out_shape=(held(3, 768, 768), shape(768, 768), shape(512, 768, dtype=F32), shape(8, 768, dtype=F32)),
            in_specs=[far] * 8 + [vmem],
            out_specs=(far, vmem, vmem, vmem),
            scratch_shapes=[
                *[pltpu.VMEM((3, 2, 3, *half), BF16)] * 4,
                pltpu.VMEM((2, 3, *half), BF16),
                pltpu.VMEM((768, 768), BF16),
                pltpu.VMEM((4, 512, 768), BF16),
                pltpu.VMEM((512, 768), F32),
                pltpu.VMEM((3, 96, 768), BF16),
                *[pltpu.VMEM((3, 3, *half), BF16)] * 4,
                pltpu.VMEM((3, 2, 3, *half), BF16),
                pltpu.VMEM((2, 3, *half), BF16),
                pltpu.VMEM((2, 3, *half), BF16),
                pltpu.VMEM((spare, 2, 2, 3, *half), BF16),
                pltpu.VMEM((2, 2, 96, 768), BF16),
                pltpu.VMEM((2, 96, 768), BF16),
                pltpu.VMEM((2, 96, 768), BF16),
                pltpu.VMEM((192, 768), BF16),
                pltpu.VMEM((192, 768), BF16),
                pltpu.VMEM((spare, 2, 192, 768), BF16),
                pltpu.VMEM((2, 512, 768), BF16),
                pltpu.VMEM((512, 768), BF16),
                pltpu.VMEM((512, 768), BF16),
                pltpu.VMEM((512, 768), BF16),
                pltpu.VMEM((512, 768), BF16),
                pltpu.VMEM((5 + spare, 8, 768), F32),
                dma(64), dma(64), dma(16 + spare), dma(16 + spare), dma(9),
            ],
            compiler_params=params(62, 2),
        )(keep_a, keep_b, recv_a, recv_b, zr, grads, part, gz1, sums)

        g_qkv, g_out, g_gate_up, g_down, g_tok, gains, biases = pl.pallas_call(
            widen_kernel,
            name="widen",
            grid=(3,),
            out_shape=(
                shape(576, 768, dtype=F32), shape(192, 768, dtype=F32), shape(768, 2, 768, dtype=F32),
                shape(768, 768, dtype=F32), shape(1, 512, 768, dtype=F32), *(shape(2, 768, dtype=F32),) * 2,
            ),
            in_specs=[
                pl.BlockSpec((192, 768), lambda i: (i, 0)),
                pl.BlockSpec((64, 768), lambda i: (9 + i, 0)),
                pl.BlockSpec((2, 256, 768), lambda i: (0, i, 0)),
                pl.BlockSpec((1, 768, 256), lambda i: (2, 0, i)),
                pl.BlockSpec((256, 768), lambda i: (jnp.minimum(i, 1), 0)),
                pl.BlockSpec((8, 768), lambda i: (0, 0)),
            ],
            out_specs=(
                pl.BlockSpec((192, 768), lambda i: (i, 0)),
                pl.BlockSpec((64, 768), lambda i: (i, 0)),
                pl.BlockSpec((256, 2, 768), lambda i: (i, 0, 0)),
                pl.BlockSpec((256, 768), lambda i: (i, 0)),
                pl.BlockSpec((1, 256, 768), lambda i: (0, jnp.minimum(i, 1), 0)),
                pl.BlockSpec((2, 768), lambda i: (0, 0)),
                pl.BlockSpec((2, 768), lambda i: (0, 0)),
            ),
            compiler_params=params(62),
            cost_estimate=pl.CostEstimate(flops=0, bytes_accessed=18_000_000, transcendentals=0),
        )(g_attn, g_attn, g_ff, g_ff, g_tok, sums)
        return out[None], g_tok, g_qkv.reshape(3, 192, 768).transpose(2, 0, 1), g_out, g_gate_up, g_down, gains, biases

    placed = (
        P("dp", "tensor", None),
        P("dp", None),
        P(None, None, "tensor"),
        P("tensor", None),
        P(None, None, "tensor"),
        P("tensor", None),
        P(),
        P(),
        P("dp", "tensor", None),
    )
    return jax.shard_map(
        on_device,
        mesh=mesh,
        in_specs=placed,
        out_specs=(
            P("dp", "tensor", None),
            P("dp", "tensor", None),
            P(None, None, "tensor"),
            P("tensor", None),
            P(None, None, "tensor"),
            P("tensor", None),
            P(),
            P(),
        ),
        check_vma=False,
    )
```
